128 devices in a mesh: dp: 4 (over z), fsdp: 32 (over y, x, core).
Axes of the slice: x: 4, y: 4, z: 4, core: 2. Of those that a mesh axis runs over, the one named last changes fastest.
Arguments:
- layer_input: bfloat16 [32768, 768], P(('dp', 'fsdp')), may hold values from -6 to 6
- segments: int32 [128, 256], P(('dp', 'fsdp')), may hold values from 0 to 1, never falling along the last dimension, each value on 1 to 192 neighbouring positions
- norm_gain: bfloat16 [2, 2, 768], P(None, None, ('dp', 'fsdp')), may hold values from 0.25 to 1.75
- norm_bias: bfloat16 [2, 2, 768], P(None, None, ('dp', 'fsdp')), may hold values from -1.75 to 1.75
- query_weight: bfloat16 [2, 768, 768], P(None, ('dp', 'fsdp')), may hold values from -0.21875 to 0.21875
- query_bias: bfloat16 [2, 768], P(None, ('dp', 'fsdp')), may hold values from -1.75 to 1.75
- keyval_weight: bfloat16 [768, 128], P(('dp', 'fsdp')), may hold values from -0.21875 to 0.21875
- output_weight: bfloat16 [2, 768, 768], P(None, None, ('dp', 'fsdp')), may hold values from -1.25 to 1.25
- output_bias: bfloat16 [2, 768], P(None, ('dp', 'fsdp')), may hold values from -1.75 to 1.75
- upward_weight: bfloat16 [2, 768, 3072], P(None, None, ('dp', 'fsdp')), may hold values from -0.21875 to 0.21875
- upward_bias: bfloat16 [2, 3072], P(None, ('dp', 'fsdp')), may hold values from -1.75 to 1.75
- downward_weight: bfloat16 [2, 3072, 768], P(None, None, ('dp', 'fsdp')), may hold values from -0.109375 to 0.109375
- downward_bias: bfloat16 [2, 768], P(None, ('dp', 'fsdp')), may hold values from -1.75 to 1.75
- cotangent: bfloat16 [32768, 768], P(('dp', 'fsdp')), may hold values from -24 to 24
Outputs:
- block_output: bfloat16 [32768, 768], P(('dp', 'fsdp'))
- input_grad: bfloat16 [32768, 768], P(('dp', 'fsdp'))
- grad_norm_gain: float32 [2, 2, 768], P(None, None, ('dp', 'fsdp'))
- grad_norm_bias: float32 [2, 2, 768], P(None, None, ('dp', 'fsdp'))
- grad_query_weight: float32 [2, 768, 768], P(None, ('dp', 'fsdp'))
- grad_query_bias: float32 [2, 768], P(None, ('dp', 'fsdp'))
- grad_keyval_weight: float32 [768, 128], P(('dp', 'fsdp'))
- grad_output_weight: float32 [2, 768, 768], P(None, None, ('dp', 'fsdp'))
- grad_output_bias: float32 [2, 768], P(None, ('dp', 'fsdp'))
- grad_upward_weight: float32 [2, 768, 3072], P(None, None, ('dp', 'fsdp'))
- grad_upward_bias: float32 [2, 3072], P(None, ('dp', 'fsdp'))
- grad_downward_weight: float32 [2, 3072, 768], P(None, None, ('dp', 'fsdp'))
- grad_downward_bias: float32 [2, 768], P(None, ('dp', 'fsdp'))
The draws below stay inside these ranges and needn't reach their ends.
Inputs may be any that keep to these rules, and one draw needn't show every extreme that they name: `segments`: within one device's row document numbers never fall; every number appears; each document holds 64 to 192 tokens.
All inputs are finite; a program needn't handle non-finite values.
Results may differ from the reference program's by a relative error of at most 0.014.
Values may be sent and summed in bfloat16 or wider, within the bound.
A program may use at most 192 MiB of HBM per device.

```python
import math
import jax
import jax.numpy as jnp
import numpy as np
from jax import lax

H = 12
HD = 64
D = 768
FF = 3072
TOK_DEV = 256
SEGS = 2
MOST = 192
TOKENS = 32768
DEVICES = 128


def strengthened(drawn, stream_key, source, target, shards_of, factor):
    def block_of(dim):
        return (jnp.arange(drawn.shape[dim]) // (drawn.shape[dim] // shards_of)).reshape((-1,) + (1,) * (drawn.ndim - 1 - dim))

    near = jax.random.permutation(stream_key, shards_of)[block_of(target)]
    other_side = (block_of(target) + shards_of // 2) % shards_of
    return jnp.where((block_of(source) == near) | (block_of(source) == other_side), factor * drawn, drawn)


def shard_levels(stream_key, shape, shards, low, top_value):
    def one(position, parts):
        heights = jax.random.uniform(jax.random.fold_in(jax.random.fold_in(stream_key, 6), position), (parts,), jnp.float32, low / len(shards), top_value / len(shards))
        return jnp.repeat(jnp.exp(heights), shape[position] // parts).reshape((-1,) + (1,) * (len(shape) - position - 1))

    gain = one(*shards[0])
    for cut in shards[1:]:
        gain = gain * one(*cut)
    return gain


def length_profile(count, total, bound, slope):
    weights = [(1 << 20) // math.isqrt(standing ** slope) + 1 for standing in range(2, count + 1)]
    surplus, counts = total - bound - (count - 1), [1] * (count - 1)
    while surplus > 0:
        candidates = [i for i in range(count - 1) if counts[i] < bound]
        pool, budget = sum([weights[i] for i in candidates]), surplus
        for i in candidates:
            addition = min(bound - counts[i], max(1, budget * weights[i] // pool), surplus)
            counts[i] = counts[i] + addition
            surplus = surplus - addition
    return np.array([bound] + counts)


def ragged_sizes(rng, number_of, total, bound, slope):
    if number_of == 2:
        one = jax.random.randint(rng, (), max(1, total - bound), min(bound, total - 1) + 1)
        return jnp.stack([one, total - one])
    sizes = jnp.asarray(length_profile(number_of, total, bound, slope), jnp.int32)
    couples = (number_of - 1) // 2
    source_of, receiver = sizes[1:1 + 2 * couples:2], sizes[2:2 + 2 * couples:2]
    slack = jnp.minimum(source_of - 1, bound - receiver)
    shifted = jax.random.randint(jax.random.fold_in(rng, 1), (couples,), 0, 1 << 20) % (slack + 1)
    sizes = sizes.at[1:1 + 2 * couples:2].set(source_of - shifted).at[2:2 + 2 * couples:2].set(receiver + shifted)
    return sizes[jax.random.permutation(jax.random.fold_in(rng, 2), number_of)]


def gaussian(own_key, extent, spread, reach, cuts=(), held_as=jnp.bfloat16):
    gain = shard_levels(own_key, extent, cuts, -0.22, 0.18) if cuts else 1.0
    drawn = jax.random.normal(own_key, extent, jnp.float32) * spread * gain
    return jnp.minimum(jnp.maximum(drawn, -reach), reach).astype(held_as)


def gaussian_with(own_key, dims, spread, limit, split, heavy, kind=jnp.bfloat16):
    array = spread * jax.random.normal(own_key, dims, jnp.float32)
    if split:
        array = array * shard_levels(own_key, dims, split, -0.22, 0.18)
    return jnp.clip(strengthened(array, jax.random.fold_in(own_key, 3), *heavy), -limit, limit).astype(kind)


def setup_inputs(seed: int = 0) -> dict:
    splits = jax.random.split(jax.random.key(seed), 15)
    layer_input = gaussian(splits[0], (TOKENS, D), 1.0, 6.0, ((0, 128),))
    segments = jax.vmap(lambda own: jnp.searchsorted(jnp.cumsum(ragged_sizes(own, SEGS, TOK_DEV, MOST, 2)), jnp.arange(TOK_DEV), side="right"))(jax.random.split(splits[1], DEVICES)).reshape((DEVICES, TOK_DEV)).astype(jnp.int32)
    norm_gain = jnp.clip(1.0 + 0.15 * jax.random.normal(splits[2], (2, 2, D), jnp.float32), 0.25, 1.75).astype(jnp.bfloat16)
    norm_bias = gaussian(splits[3], (2, 2, D), 0.3, 1.75, ((2, 128),))
    query_weight = gaussian(splits[4], (2, D, D), D ** -0.5, 0.21875, ((1, 128),))
    query_bias = gaussian(splits[5], (2, D), 0.3, 1.75, ((1, 128),))
    keyval_weight = gaussian(splits[6], (D, 2 * HD), D ** -0.5, 0.21875, ((0, 128),))
    output_weight = gaussian(splits[7], (2, D, D), (D // 32) ** -0.5, 1.25, ((2, 128),))
    output_bias = gaussian(splits[8], (2, D), 0.3, 1.75, ((1, 128),))
    upward_weight = gaussian(splits[9], (2, D, FF), D ** -0.5, 0.21875, ((2, 128),))
    upward_bias = gaussian(splits[10], (2, FF), 0.3, 1.75, ((1, 128),))
    downward_weight = gaussian(splits[11], (2, FF, D), FF ** -0.5, 0.109375, ((2, 128),))
    downward_bias = gaussian(splits[12], (2, D), 0.3, 1.75, ((1, 128),))
    cotangent = gaussian_with(splits[13], (TOKENS, D), 1.0, 24.0, ((0, 128),), (0, 1, 128, 5.5))
    return {"layer_input": layer_input, "segments": segments, "norm_gain": norm_gain, "norm_bias": norm_bias, "query_weight": query_weight, "query_bias": query_bias, "keyval_weight": keyval_weight, "output_weight": output_weight, "output_bias": output_bias, "upward_weight": upward_weight, "upward_bias": upward_bias, "downward_weight": downward_weight, "downward_bias": downward_bias, "cotangent": cotangent}


@jax.custom_vjp
def low(v):
    return lax.optimization_barrier(v.astype(jnp.bfloat16)).astype(jnp.float32)

@jax.custom_vjp
def low_back(v):
    return v

def low_keep(v):
    return (low(v), None)

def low_pass(kept, grad):
    return (grad,)

def back_keep(v):
    return (v, None)

def back_low(kept, grad):
    return (low(grad),)
low.defvjp(low_keep, low_pass)
low_back.defvjp(back_keep, back_low)
norm_epsilon = 1e-05
masked_score = -1e+30
rotary_base = 10000.0

def dense_high(left, right):
    return jnp.dot(left, right, precision=lax.Precision.HIGHEST)

def layer_norm(residual, gain_row, bias_row):
    centred = residual - lax.optimization_barrier(jnp.mean(residual, axis=-1, keepdims=True))
    variance = lax.optimization_barrier(jnp.mean(centred * centred, axis=-1, keepdims=True))
    return centred * lax.rsqrt(variance + norm_epsilon) * gain_row + bias_row

def doc_layout(doc_row):
    places = jnp.arange(doc_row.shape[0], dtype=jnp.int32)
    earlier = lax.optimization_barrier(jnp.sum((doc_row[None, :] < doc_row[:, None]).astype(jnp.int32), axis=1))
    same_doc = doc_row[None, :] == doc_row[:, None]
    return (places - earlier, same_doc & (places[None, :] <= places[:, None]))

def rotary_tables(positions):
    half_width = HD // 8
    frequency = rotary_base ** (-(jnp.arange(half_width, dtype=jnp.float32) * 2.0) / (2 * half_width))
    angles = positions.astype(jnp.float32)[:, None] * frequency[None, :]
    angles = jnp.concatenate([angles, angles], axis=1)
    return (jnp.cos(angles), jnp.sin(angles))

def rotate(values, cosine, sine):
    rot_width = cosine.shape[-1]
    half_width = rot_width // 2
    leading = values[..., :rot_width]
    turned = jnp.concatenate([-leading[..., half_width:], leading[..., :half_width]], axis=-1)
    return jnp.concatenate([leading * cosine + turned * sine, values[..., rot_width:]], axis=-1)

def attend(queries, key_rows, value_rows, allowed):
    raw_scores = jnp.einsum('qhd,kd->hqk', queries, key_rows, precision=lax.Precision.HIGHEST)
    scores = low_back(raw_scores * HD ** (-0.5))
    scores = jnp.where(allowed[None], scores, masked_score)
    weights = low(jax.nn.softmax(scores, axis=-1))
    mixed = jnp.einsum('hqk,kd->qhd', weights, value_rows, precision=lax.Precision.HIGHEST)
    return low(low_back(mixed.reshape(TOK_DEV, D)))

def block(params, rows_in, doc_row):
    norm_gains, norm_biases, query_w, query_b, keyval_w, output_w, output_b, upward_w, upward_b, downward_w, downward_b = params
    positions, allowed = doc_layout(doc_row)
    cosine, sine = rotary_tables(positions)
    residual = rows_in
    shared = None
    for layer_index in range(2):
        attn_in = low(layer_norm(residual, norm_gains[layer_index, 0], norm_biases[layer_index, 0]))
        mlp_in = low(layer_norm(residual, norm_gains[layer_index, 1], norm_biases[layer_index, 1]))
        if layer_index == 0:
            keyval = low_back(dense_high(attn_in, keyval_w))
            shared = (low(rotate(keyval[:, :HD], cosine, sine)), low(keyval[:, HD:]))
        queries = low_back(dense_high(attn_in, query_w[layer_index]) + query_b[layer_index])
        queries = low(rotate(queries.reshape(TOK_DEV, H, HD), cosine[:, None, :], sine[:, None, :]))
        mixed = attend(queries, shared[0], shared[1], allowed)
        attention = low_back(dense_high(mixed, output_w[layer_index]) + output_b[layer_index])
        hidden = low_back(dense_high(mlp_in, upward_w[layer_index]) + upward_b[layer_index])
        activated = low(jax.nn.gelu(hidden, approximate=False))
        feed_out = low_back(dense_high(activated, downward_w[layer_index]) + downward_b[layer_index])
        residual = residual + attention + feed_out
    return residual

def reference(layer_input, segments, norm_gain, norm_bias, query_weight, query_bias, keyval_weight, output_weight, output_bias, upward_weight, upward_bias, downward_weight, downward_bias, cotangent):
    params = tuple((item.astype(jnp.float32) for item in (norm_gain, norm_bias, query_weight, query_bias, keyval_weight, output_weight, output_bias, upward_weight, upward_bias, downward_weight, downward_bias)))
    rows_all = layer_input.astype(jnp.float32).reshape(DEVICES, TOK_DEV, D)

    def forward(rows_in, weights):
        per_block = jax.checkpoint(lambda inputs: block(weights, inputs[0], inputs[1]))
        return lax.map(per_block, (rows_in, segments))
    result, pull = jax.vjp(forward, rows_all, params)
    grad_rows, grad_params = pull(cotangent.astype(jnp.float32).reshape(DEVICES, TOK_DEV, D))
    block_output = result.reshape(TOKENS, D).astype(jnp.bfloat16)
    input_grad = grad_rows.reshape(TOKENS, D).astype(jnp.bfloat16)
    return (block_output, input_grad, grad_params[0], grad_params[1], grad_params[2], grad_params[3], grad_params[4], grad_params[5], grad_params[6], grad_params[7], grad_params[8], grad_params[9], grad_params[10])
```

```python
import functools

import jax
import jax.numpy as jnp
import numpy as np
from jax import lax
from jax.experimental import pallas as pl
from jax.experimental.pallas import tpu as pltpu
from jax.sharding import PartitionSpec as P

MESH = pl.DeviceIdType.MESH
F32 = jnp.float32
BF16 = jnp.bfloat16

H = 12
HD = 64
D = 768
FF = 3072
TOK = 256
HALF = 384
ROWS = 512
KV0, VEC0, Q0, O0, D0, U0 = 0, 16, 32, 80, 128, 320
CHUNK = 64

norm_epsilon = 1e-05
masked_score = -1e30
rotary_base = 10000.0
root_half = 0.7071067811865476
inverse_root_tau = 0.3989422804014327
scale = HD**-0.5


def place_constants():
    qod = np.zeros((288, 512), np.float32)
    kv = np.zeros((48, 512), np.float32)
    for s in range(8):
        for i in range(6):
            r = s * 6 + i
            qod[r, s * CHUNK + 22 + i] = 1
            qod[48 + r, s * CHUNK + 28 + i] = 1
            for g in range(4):
                qod[96 + 48 * g + r, s * CHUNK + 34 + 4 * i + g] = 1
            kv[r, s * CHUNK + 16 + i] = 1
    up = np.zeros((192, 192), np.float32)
    for h in range(2):
        for x in range(4):
            for j in range(24):
                up[h * 96 + x * 24 + j, x * 48 + h * 24 + j] = 1
    perm = np.zeros((768, 768), np.float32)
    for chip in range(16):
        for c in range(2):
            for j in range(24):
                perm[chip * 48 + c * 24 + j, c * 384 + chip * 24 + j] = 1
    spread48 = np.zeros((128, 768), np.float32)
    spread48[np.arange(768) % 48, np.arange(768)] = 1
    spread96 = np.zeros((128, 1536), np.float32)
    spread96[np.arange(1536) % 96, np.arange(1536)] = 1
    return qod, kv, up, perm, spread48, spread96, qod.T, kv.T, up.T


CONSTS = place_constants()


def nn(a, b):
    return jnp.dot(a, b, preferred_element_type=F32)


def nt(a, b):
    return lax.dot_general(a, b, (((1,), (1,)), ((), ())), preferred_element_type=F32)


def tn(a, b):
    return lax.dot_general(a, b, (((0,), (0,)), ((), ())), preferred_element_type=F32)


def ranges(lengths):
    at, out = 0, []
    for n in lengths:
        out.append((at, n))
        at += n
    return out


class Place:
    def __init__(self):
        self.z = lax.axis_index("dp")
        f = lax.axis_index("fsdp")
        self.y = f // 8
        self.x = (f // 2) % 4
        self.c = f % 2

    def dev(self, dz=0, dy=0, dx=0, dc=0):
        z = (self.z + dz) % 4
        y = (self.y + dy) % 4
        x = (self.x + dx) % 4
        c = (self.c + dc) % 2
        return (z, y * 8 + x * 2 + c)

    def along(self, axis, d):
        return self.dev(**{"d" + axis: d})

    def pos(self, axis):
        return getattr(self, axis)


class Ring:
    def __init__(self, me, axis, view, sems, many):
        self.me, self.axis, self.view, self.sems, self.many = me, axis, view, sems, many
        self.p = me.pos(axis)

    def _copy(self, to, src, dst, sem):
        return pltpu.make_async_remote_copy(
            src_ref=src,
            dst_ref=dst,
            send_sem=self.sems.at[0],
            recv_sem=self.sems.at[sem],
            device_id=self.me.along(self.axis, to),
            device_id_type=MESH,
        )

    def _await(self, ref, sem):
        pltpu.make_async_copy(ref, ref, self.sems.at[sem]).wait()

    def sent(self):
        self._await(self.many(3), 0)


class Gather(Ring):
    def _pass(self, to, k, h, sem):
        block = self.view(k % 4, h)
        self._copy(to, block, block, sem).start()

    def start(self):
        p = self.p
        self._pass(1, p, 0, 1)
        self._pass(-1, p, 1, 2)
        self._pass(1, p, 1, 3)
        self._pass(-1, p, 0, 3)

    def forward(self):
        p = self.p
        self._await(self.view((p + 3) % 4, 0), 1)
        self._pass(1, p + 3, 0, 4)
        self._await(self.view((p + 1) % 4, 1), 2)
        self._pass(-1, p + 1, 1, 4)

    def near(self):
        self._await(self.many(1), 3)

    def far(self):
        self._await(self.many(1), 4)

    def finish(self):
        self.near()
        self.far()
        self.sent()


class Scatter(Ring):
    def __init__(self, me, axis, view, sems, many, buf, leads, rows):
        super().__init__(me, axis, view, sems, many)
        self.buf, self.leads, self.rows = buf, leads, rows

    def _slot(self, j, h):
        ref = self.buf.at[j]
        n = self.rows[h]
        if n != ref.shape[-2]:
            ref = ref.at[tuple(slice(None) for _ in self.leads) + (pl.ds(0, n),)]
        return ref

    def _pass(self, to, k, h, slot, sem):
        self._copy(to, self.view(k % 4, h), self._slot(slot, h), sem).start()

    def _add(self, k, h, slots):
        target = self.view(k, h)
        srcs = [self._slot(s, h) for s in slots]

        def one(idx):
            total = target[idx].astype(F32)
            for s in srcs:
                total = total + s[idx].astype(F32)
            target[idx] = total.astype(BF16)

        if not self.leads:
            one((slice(None), slice(None)))
        else:

            @pl.loop(0, self.leads[0])
            def _(i):
                one((i,))

    def start_far(self):
        p = self.p
        self._pass(1, p + 2, 0, 0, 1)
        self._pass(-1, p + 2, 1, 1, 2)

    def start_near(self):
        p = self.p
        self._pass(1, p + 1, 1, 3, 3)
        self._pass(-1, p + 3, 0, 4, 3)

    def start(self):
        self.start_far()
        self.start_near()

    def forward(self):
        p = self.p
        self._await(self._slot(0, 0), 1)
        self._add((p + 1) % 4, 0, [0])
        self._pass(1, p + 1, 0, 2, 3)
        self._await(self._slot(1, 1), 2)
        self._add((p + 3) % 4, 1, [1])
        self._pass(-1, p + 3, 1, 5, 3)

    def finish(self):
        self._await(self.many(2), 3)
        self._add(self.p, 0, [2, 4])
        self._add(self.p, 1, [3, 5])
        self.sent()


def kernel(
    xin, seg, cot, w_gain, w_nbias, w_q, w_qb, w_kv, w_o, w_ob, w_up, w_ub, w_down, w_db, h_qod, h_kv, h_up, h_perm, h_s48, h_s96, h_qodT, h_kvT, h_upT,
    out_y, out_gx, out_v, out_u,
    W, chunk, rawu, got, gotu, vecs, ubv,
    X2, gl, seg2, cosT, sinT, mbias, n_, r_, h1, attn, mlp, kvT, k_, v_, qT, p_, mixT, mixed, act, slope,
    acc, glT, attnT, gm, gmT, dk, dv, gs, vg, ubg, g_, xs, xr,
    bA2, bB2, bO2, bU2, bV2, bD1, bD2, bA3, bB3, bO3, bU3, bV3, bD3, rgot, rgotu,
    c_qod, c_kv, c_up, c_perm, c_s48, c_s96, c_qodT, c_kvT, c_upT,
    const_sem, pair_send, pair_recv, line_sem, ag_sem, rs_sem,
):
    me = Place()
    z, y, x, c = me.z, me.y, me.x, me.c
    s_me = x * 2 + c

    consts = [(h_perm, c_perm), (h_qod, c_qod), (h_kv, c_kv), (h_up, c_up), (h_s48, c_s48), (h_s96, c_s96),
              (h_qodT, c_qodT), (h_kvT, c_kvT), (h_upT, c_upT)]
    const_copies = [pltpu.make_async_copy(h, v, const_sem.at[i]) for i, (h, v) in enumerate(consts)]
    for cp in const_copies:
        cp.start()

    bar = pltpu.get_barrier_semaphore()
    line = [(dx, dc) for dx in range(4) for dc in range(2) if (dx, dc) != (0, 0)]
    partners = [me.dev(dx=dx, dc=dc) for dx, dc in line]
    partners += [me.dev(dy=1), me.dev(dy=-1), me.dev(dz=1), me.dev(dz=-1)]
    for d in partners:
        pl.semaphore_signal(bar, inc=1, device_id=d, device_id_type=MESH)
    sibling = me.dev(dc=1)

    def to_sibling(i, src, dst):
        return pltpu.make_async_remote_copy(
            src_ref=src, dst_ref=dst, send_sem=pair_send.at[i], recv_sem=pair_recv.at[i],
            device_id=sibling, device_id_type=MESH)

    def lane_place():
        r = lax.broadcasted_iota(jnp.int32, (128, HALF), 0)
        m = lax.broadcasted_iota(jnp.int32, (128, HALF), 1)
        small = (r < 6) & (m == r + 6 * s_me)
        wide = (r >= 8) & (r < 32) & (m == r - 8 + 128 + 24 * x)
        return jnp.where(small | wide, 1.0, 0.0).astype(BF16)

    def line_copies(l, bufs, into, bufu, intou, sems):
        out = []
        for dx, dc in line:
            t = (c + dc) % 2
            s_to = ((x + dx) % 4) * 2 + t
            out.append(pltpu.make_async_remote_copy(
                src_ref=bufs(s_to, t), dst_ref=into.at[l, s_me], send_sem=sems.at[0], recv_sem=sems.at[1],
                device_id=me.dev(dx=dx, dc=dc), device_id_type=MESH))
        for dx in range(1, 4):
            out.append(pltpu.make_async_remote_copy(
                src_ref=bufu((x + dx) % 4), dst_ref=intou.at[l, x], send_sem=sems.at[2],
                recv_sem=sems.at[3], device_id=me.dev(dx=dx), device_id_type=MESH))
        for cp in out:
            cp.start()

    def line_wait(sems):
        seven, three = W.at[0, 0, 0, pl.ds(0, 7 * CHUNK)], W.at[0, 0, 0, pl.ds(0, 144)]
        for i, ref in enumerate((seven, seven, three, three)):
            pltpu.make_async_copy(ref, ref, sems.at[i]).wait()

    h1[0:2 * CHUNK, :] = jnp.zeros((2 * CHUNK, D), F32)
    for l in range(2):
        h1[7 * l:7 * l + 2, 0:6] = w_gain[l].astype(F32)
        h1[7 * l + 2:7 * l + 4, 0:6] = w_nbias[l].astype(F32)
        for k, ref in ((4, w_qb), (5, w_ob), (6, w_db)):
            h1[7 * l + k:7 * l + k + 1, 0:6] = ref[...].astype(F32)[l:l + 1]
    h1[0:2, 8:32] = w_ub[...].astype(F32)
    h1[16:22, 0:128] = w_kv[...].astype(F32)
    for i in range(6):
        q2, o2, d2 = w_q[i].astype(F32), w_o[i].astype(F32), w_down[i].astype(F32)
        for l in range(2):
            at = CHUNK * l
            h1[at + 22 + i:at + 23 + i, :] = q2[l:l + 1]
            h1[at + 28 + i:at + 29 + i, :] = o2[l:l + 1]
            for g in range(4):
                h1[at + 34 + 4 * i + g:at + 35 + 4 * i + g, :] = d2[l:l + 1, g * D:(g + 1) * D]
    for l in range(2):
        u = w_up[l].astype(F32)
        rawu[l] = jnp.concatenate([u[:, 0:HALF], u[:, HALF:]], axis=0).astype(BF16)

    const_copies[0].wait()
    place = lane_place()

    def prepare(l):
        vf = h1[CHUNK * l:CHUNK * l + CHUNK, :]
        v = vf.astype(BF16)
        vp = nn(v, c_perm[...]).astype(BF16).astype(F32)
        row = lax.broadcasted_iota(jnp.int32, (CHUNK, HALF), 0)
        lane = lax.broadcasted_iota(jnp.int32, (CHUNK, HALF), 1)
        if l == 0:
            head = jnp.where(row < 16, nn(v[:, 0:128], place), jnp.where(lane < 128, vf[:, 0:HALF], 0.0))
        for t in range(2):
            part = jnp.where(row < 34, vf[:, t * HALF:(t + 1) * HALF], vp[:, t * HALF:(t + 1) * HALF])
            if l == 0:
                ours = jnp.where((lane < 128) | (c == t), head, 0.0)
                part = jnp.where(row < 22, ours, part)
            chunk[l, t] = part.astype(BF16)

    def send_chunks(l):
        line_copies(l, lambda s, t: chunk.at[l, t], got, lambda xx: rawu.at[l], gotu, line_sem.at[l])
        got[l, s_me] = chunk[l, c]
        gotu[l, x] = rawu[l]

    prepare(0)
    seg2[c] = jnp.broadcast_to(seg[...], (8, TOK))
    own = pl.ds(pl.multiple_of(c * TOK, TOK), TOK)

    pl.semaphore_wait(bar, len(partners))

    def to_sibling(i, src, dst):
        return pltpu.make_async_remote_copy(
            src_ref=src, dst_ref=dst, send_sem=pair_send.at[i], recv_sem=pair_recv.at[i],
            device_id=sibling, device_id_type=MESH)

    send_chunks(0)
    seg_copy = to_sibling(0, seg2.at[c], seg2.at[c])
    seg_copy.start()
    x_copy = to_sibling(1, xin, X2.at[c])
    x_copy.start()
    c_copy = to_sibling(2, cot, gl.at[own])
    c_copy.start()
    X2[c] = xin[...]
    gl[own, :] = cot[...]
    prepare(1)
    send_chunks(1)

    half_width = HD // 8
    frequency = np.float32(rotary_base) ** (-(np.arange(half_width, dtype=np.float32) * 2.0) / (2 * half_width))
    row = lax.broadcasted_iota(jnp.int32, (half_width, TOK), 0)
    freq = jnp.zeros((half_width, TOK), F32)
    for f in range(half_width):
        freq = jnp.where(row == f, float(frequency[f]), freq)
    seg_copy.wait()
    for b in range(2):
        docs = seg2[b].astype(F32)
        over_lanes = jnp.broadcast_to(docs[0:1], (TOK, TOK))
        over_rows = over_lanes.T
        earlier = jnp.sum(jnp.where(over_rows < over_lanes, 1.0, 0.0), axis=0, keepdims=True)
        place = lax.broadcasted_iota(jnp.int32, (1, TOK), 1).astype(F32) - earlier
        angle = jnp.broadcast_to(place, (8, TOK)) * freq
        cosT[:, b * TOK:(b + 1) * TOK] = jnp.cos(angle)
        sinT[:, b * TOK:(b + 1) * TOK] = jnp.sin(angle)
        kk = lax.broadcasted_iota(jnp.int32, (TOK, TOK), 0)
        qq = lax.broadcasted_iota(jnp.int32, (TOK, TOK), 1)
        mbias[b] = jnp.where((over_rows == over_lanes) & (kk <= qq), 0.0, masked_score)
    x_copy.wait()
    c_copy.wait()

    CH = 64

    def norm_of(h):
        centred = h - jnp.mean(h, axis=-1, keepdims=True)
        inverse = lax.rsqrt(jnp.mean(centred * centred, axis=-1, keepdims=True) + norm_epsilon)
        return centred * inverse, inverse

    def normalise(i, h):
        rows = pl.ds(pl.multiple_of(i * CH, CH), CH)
        n, inverse = norm_of(h)
        n_[rows, :] = n
        r_[rows, :] = jnp.broadcast_to(inverse, (CH, 128))

    def input_rows(i):
        return X2[i // 4, pl.ds(pl.multiple_of((i % 4) * CH, CH), CH), :].astype(F32)

    @pl.loop(0, 8)
    def _(i):
        normalise(i, input_rows(i))

    for cp in const_copies[1:]:
        cp.wait()

    def quarter(k):
        return pl.multiple_of(D0 + 48 * k, 16)

    def assemble(l):
        line_wait(line_sem.at[l])
        stack = got[l].reshape(512, HALF)
        W[l, z, y, Q0:D0, :] = nn(c_qod[0:96, :], stack).astype(BF16)
        down = nn(c_qod[pl.ds(pl.multiple_of(96 + 48 * x, 16), 48), :], stack).astype(BF16)
        W[l, z, y, pl.ds(quarter(x), 48), :] = down
        if l == 0:
            kv = nn(c_kv[...], stack[:, 0:128]).astype(BF16)
            W[0, z, y, KV0:KV0 + 16, :] = jnp.concatenate([kv[0:16], kv[16:32], kv[32:48]], axis=1)
            vec = got[0, 0, 0:16, :].astype(F32)
            for s in range(1, 8):
                vec = vec + got[0, s, 0:16, :].astype(F32)
            W[0, z, y, VEC0:VEC0 + 16, :] = vec.astype(BF16)
        W[l, z, y, U0:ROWS, :] = nn(c_up[...], gotu[l].reshape(192, HALF)).astype(BF16)

    def many(n, wide):
        if wide:
            return lambda count: W.at[0, pl.ds(0, count), :, pl.ds(0, n), :]
        return lambda count: W.at[0, 0, pl.ds(0, count), pl.ds(0, n), :]

    def cut(row0, n, h):
        first = halves(n)[0]
        return pl.ds(row0 if h == 0 else pl.multiple_of(row0 + first, 16), first if h == 0 else n - first)

    def halves(n):
        first = (n + 31) // 32 * 16
        return (first, n - first)

    def gathers(l):
        g = {}

        def y_then_z(i, name, row0, n):
            g[name + "2"] = Gather(me, "y", lambda k, h: W.at[l, z, k, cut(row0, n, h), :], ag_sem.at[l, i], many(n, False))
            g[name + "3"] = Gather(me, "z", lambda k, h: W.at[l, k, pl.ds(2 * h, 2), pl.ds(row0, n), :], ag_sem.at[l, i + 1],
                                   many(n, True))

        def z_then_y(i, name, row0, n):
            g[name + "2"] = Gather(me, "z", lambda k, h: W.at[l, k, y, cut(row0, n, h), :], ag_sem.at[l, i], many(n, False))
            g[name + "3"] = Gather(me, "y", lambda k, h: W.at[l, pl.ds(2 * h, 2), k, pl.ds(row0, n), :], ag_sem.at[l, i + 1],
                                   many(n, True))

        e0 = 0 if l == 0 else Q0
        en = (D0 - e0) // 2
        y_then_z(0, "E", e0, en)
        z_then_y(2, "F", e0 + en, en)
        z_then_y(4, "D", quarter(x), 48)
        y_then_z(6, "U", U0, 112)
        z_then_y(8, "V", U0 + 112, 80)
        for i, dy in enumerate((0, 1, 3, 2)):
            g["D4", i] = Gather(me, "x", lambda k, h, dy=dy: W.at[l, pl.ds(2 * h, 2), (y + dy) % 4, pl.ds(quarter(k), 48), :],
                                ag_sem.at[l, 10 + i], many(48, True))
        return g

    g0, g1 = gathers(0), gathers(1)

    def second_stage(l, g):
        assemble(l)
        for n in "EFDUV":
            g[n + "2"].start()

    def third_stage(g):
        for n in "EFDUV":
            g[n + "2"].forward()
        for n in "EFD":
            g[n + "2"].finish()
            g[n + "3"].start()
        g["D4", 0].start()
        for n in "UV":
            g[n + "2"].finish()
        g["E3"].forward()
        g["F3"].forward()
        for n in "UV":
            g[n + "3"].start()

    def fourth_stage(g):
        g["D3"].forward()
        g["D4", 0].forward()
        g["D3"].near()
        g["D4", 1].start()
        g["D4", 2].start()
        g["U3"].forward()
        g["V3"].forward()

    def heads_ready(g):
        g["E3"].finish()
        g["F3"].finish()

    def last_quarter(g):
        g["D3"].far()
        g["D4", 3].start()
        g["D4", 1].forward()
        g["D4", 2].forward()

    def hidden_ready(g):
        g["U3"].finish()
        g["V3"].finish()

    def down_ready(g):
        g["D3"].sent()
        for i in range(4):
            g["D4", i].finish()

    second_stage(0, g0)
    third_stage(g0)
    second_stage(1, g1)
    heads_ready(g0)

    tile = W[0, :, :, VEC0:VEC0 + 16, :].reshape(256, HALF)
    wide = nn(tile[:, 0:128], c_s48[...])
    at = lax.broadcasted_iota(jnp.int32, (16, D), 1)
    total = jnp.zeros((16, D), F32)
    for m in range(16):
        total = total + jnp.where((at >= 48 * m) & (at < 48 * m + 48), wide[16 * m:16 * m + 16], 0.0)
    vecs[...] = total
    wide = nn(tile[:, 128:256], c_s96[...])
    at = lax.broadcasted_iota(jnp.int32, (16, 1536), 1)
    total = jnp.zeros((16, 1536), F32)
    for m in range(16):
        total = total + jnp.where((at >= 96 * m) & (at < 96 * m + 96), wide[16 * m:16 * m + 16], 0.0)
    for l in range(2):
        for k in range(4):
            ubv[l, k] = jnp.broadcast_to(total[l:l + 1, k * HALF:(k + 1) * HALF], (8, HALF))

    def vec(l, k):
        return vecs[7 * l + k:7 * l + k + 1, :]

    def norm_inputs(l, again=False):
        @pl.loop(0, 8)
        def _(i):
            rows = pl.ds(pl.multiple_of(i * CH, CH), CH)
            n = norm_of(input_rows(i))[0] if again else n_[rows, :]
            attn[rows, :] = (n * vec(l, 0) + vec(l, 2)).astype(BF16)
            mlp[rows, :] = (n * vec(l, 1) + vec(l, 3)).astype(BF16)

    def key_weight():
        kvw = W[0, :, :, KV0:KV0 + 16, :]
        return jnp.concatenate([kvw[..., 0:128], kvw[..., 128:256], kvw[..., 256:384]], axis=2).reshape(D, 128)

    def weight(l, row0, n=48):
        return W[l, :, :, pl.ds(row0, n), :].reshape(16 * n, HALF)

    def up_weight(l, k, h):
        return W[l, k, :, U0 + 96 * h:U0 + 96 * h + 96, :].reshape(HALF, HALF)

    def down_weight(l, k):
        return weight(l, pl.multiple_of(D0 + 48 * k, 16))

    def rotate_heads(v, heads):
        v = v.reshape(heads, HD, 512)
        cs, sn = cosT[...][None], sinT[...][None]
        u1, u2 = v[:, 0:8, :], v[:, 8:16, :]
        return jnp.concatenate([u1 * cs - u2 * sn, u2 * cs + u1 * sn, v[:, 16:, :]], axis=1).reshape(heads * HD, 512)

    def rotate_heads_back(v, heads):
        v = v.reshape(heads, HD, 512)
        cs, sn = cosT[...][None], sinT[...][None]
        u1, u2 = v[:, 0:8, :], v[:, 8:16, :]
        return jnp.concatenate([u1 * cs + u2 * sn, u2 * cs - u1 * sn, v[:, 16:, :]], axis=1).reshape(heads * HD, 512)

    def serve(i, points):
        for at, step in points.items():
            pl.when(i == at)(step)

    def steps(*todo):
        def run():
            for step, *args in todo:
                step(*args)

        return run

    def down_block(l, rows):
        acc[rows, :] = nt(mixed[l, rows, :], weight(l, O0))
        for k in range(4):
            acc[rows, :] += nt(act[l, k, rows, :], down_weight(l, k))

    def forward(l, in_heads, before_ffn, in_ffn):
        norm_inputs(l)
        if l == 0:
            kv = nn(attn[...], key_weight()).T
            keys = rotate_heads(kv[0:HD], 1)
            kvT[0:HD, :] = keys.astype(BF16)
            kvT[HD:, :] = kv[HD:].astype(BF16)
            k_[...] = keys.T.astype(BF16)
            v_[...] = kv[HD:].T.astype(BF16)
        qb = vec(l, 4)
        qb = jnp.where(c == 0, qb[:, 0:HALF], qb[:, HALF:])
        q = nn(attn[...], weight(l, Q0)) + qb
        qT[l] = rotate_heads(q.T, 6).astype(BF16)

        @pl.loop(0, 12)
        def _(i):
            serve(i, in_heads)
            h, b = i // 2, i % 2
            hs = pl.ds(pl.multiple_of(h * HD, HD), HD)
            bs = pl.ds(pl.multiple_of(b * TOK, TOK), TOK)
            s = nn(k_[bs, :], qT[l, hs, bs]) * scale + mbias[b]
            e = jnp.exp(s - jnp.max(s, axis=0, keepdims=True))
            low = (e * (1.0 / jnp.sum(e, axis=0, keepdims=True))).astype(BF16)
            p_[l, h, b] = low
            mixT[hs, bs] = nn(kvT[HD:, bs], low).astype(BF16)

        mixed[l] = mixT[...].T
        before_ffn()

        @pl.loop(0, 4)
        def _(k):
            serve(k, in_ffn)
            for b in range(2):
                rows = slice(b * TOK, (b + 1) * TOK)
                hid = nt(mlp[rows, 0:HALF], up_weight(l, k, 0)) + nt(mlp[rows, HALF:], up_weight(l, k, 1))
                hid = hid + ubv[l, k, 0:1, :]
                phi = 0.5 * (1.0 + lax.erf(hid * root_half))
                low = (hid * phi).astype(BF16)
                act[l, k, rows, :] = low
                slope[l, k, rows, :] = (phi + hid * jnp.exp(-0.5 * hid * hid) * inverse_root_tau).astype(BF16)

    forward(
        0,
        {0: steps((fourth_stage, g0)), 3: steps((third_stage, g1)), 5: steps((last_quarter, g0)), 9: steps((g0["D4", 3].forward,))},
        steps((hidden_ready, g0)),
        {},
    )
    down_ready(g0)
    swap = [to_sibling(3 + b, xs.at[b], xr.at[b]) for b in range(2)]
    for b in range(2):
        down_block(0, slice(b * TOK, (b + 1) * TOK))
        xs[b] = acc[b * TOK:(b + 1) * TOK, :].astype(BF16)
        swap[b].start()
        if b == 0:
            fourth_stage(g1)
    heads_ready(g1)
    for cp in swap:
        cp.wait()

    @pl.loop(0, 8)
    def _(i):
        b = i // 4
        rows = pl.ds(pl.multiple_of((i % 4) * CH, CH), CH)
        h = X2[b, rows, :].astype(F32) + (vec(0, 5) + vec(0, 6))
        h = h + (xs[b, rows, :].astype(F32) + xr[b, rows, :].astype(F32))
        normalise(i, h)

        @pl.when(b == c)
        def _():
            h1[rows, :] = h

    forward(
        1,
        {2: steps((last_quarter, g1)), 7: steps((g1["D4", 3].forward,))},
        steps((hidden_ready, g1)),
        {},
    )
    down_ready(g1)
    other = pl.ds(pl.multiple_of((1 - c) * TOK, TOK), TOK)
    down_block(1, other)
    xs[0] = acc[other, :].astype(BF16)
    y_copy = to_sibling(5, xs.at[0], xr.at[2])
    y_copy.start()
    down_block(1, own)
    y_copy.wait()
    out_y[...] = (h1[...] + (vec(1, 5) + vec(1, 6)) + acc[own, :] + xr[2].astype(F32)).astype(BF16)

    def scatters(l):
        gslot = 2 if l == 1 else 1
        g = {}

        def z_then_y(i, n2, n3, row0, n, b2, b3):
            g[n2] = Scatter(me, "z", lambda k, h: W.at[gslot, k, pl.ds(2 * h, 2), pl.ds(row0, n), :], rs_sem.at[l, i],
                            many(n, True), b2.at[l], (2,), (n, n))
            g[n3] = Scatter(me, "y", lambda k, h: W.at[gslot, z, k, cut(row0, n, h), :], rs_sem.at[l, i + 1],
                            many(n, False), b3.at[l], (), halves(n))

        def y_then_z(i, n2, n3, row0, n, b2, b3):
            g[n2] = Scatter(me, "y", lambda k, h: W.at[gslot, pl.ds(2 * h, 2), k, pl.ds(row0, n), :], rs_sem.at[l, i],
                            many(n, True), b2.at[l], (2,), (n, n))
            g[n3] = Scatter(me, "z", lambda k, h: W.at[gslot, k, y, cut(row0, n, h), :], rs_sem.at[l, i + 1],
                            many(n, False), b3.at[l], (), halves(n))

        for i, dz in enumerate((2, 1, 3, 0)):
            g["D1", i] = Scatter(me, "x", lambda k, h, dz=dz: W.at[gslot, (z + dz) % 4, pl.ds(2 * h, 2), pl.ds(quarter(k), 48), :],
                                 rs_sem.at[l, i], many(48, True), bD1.at[l, i], (2,), (48, 48))
        z_then_y(4, "D2", "D3", quarter(x), 48, bD2, bD3)
        y_then_z(6, "O2", "O3", O0, 48, bO2, bO3)
        z_then_y(8, "U2", "U3", U0, 96, bU2, bU3)
        y_then_z(14, "V2", "V3", U0 + 96, 96, bV2, bV3)
        a0 = 0 if l == 0 else VEC0
        z_then_y(10, "A2", "A3", a0, 48 - a0, bA2, bA3)
        y_then_z(12, "B2", "B3", 48, 32, bB2, bB3)
        return g

    def finish_line(l):
        gslot = 2 if l == 1 else 1
        B = W.at[gslot, z, y]
        rowd = lax.broadcasted_iota(jnp.int32, (288, HALF), 0)
        lo = 96 + 48 * x
        blk = B[Q0:U0, :].astype(F32)
        blk = jnp.where((rowd < 96) | ((rowd >= lo) & (rowd < lo + 48)), blk, 0.0).astype(BF16)
        stack = nn(c_qodT[...], blk)
        if l == 0:
            kv = B[KV0:KV0 + 16, :]
            kv = jnp.concatenate([kv[:, 0:128], kv[:, 128:256], kv[:, 256:384]], axis=0)
            stack = stack + jnp.concatenate([nn(c_kvT[...], kv), jnp.zeros((512, 256), F32)], axis=1)
        stack = stack.astype(BF16).reshape(8, CHUNK, HALF)
        got[l] = stack
        for s in range(8):
            got[l, s, 0:16, :] = B[VEC0:VEC0 + 16, :]
        gotu[l] = nn(c_upT[...], B[U0:ROWS, :]).astype(BF16).reshape(4, 48, HALF)
        line_copies(l, lambda s, t: got.at[l, s], rgot, lambda xx: gotu.at[l, xx], rgotu, line_sem.at[2 + l])
        rgot[l, s_me] = got[l, s_me]
        rgotu[l, x] = gotu[l, x]

    def last_sums(l):
        line_wait(line_sem.at[2 + l])
        halves = []
        for t in range(2):
            v = rgot[l, t].astype(F32)
            for xx in range(1, 4):
                v = v + rgot[l, 2 * xx + t].astype(F32)
            halves.append(v)
        v = jnp.concatenate(halves, axis=1)
        hi = v.astype(BF16)
        lo = (v - hi.astype(F32)).astype(BF16)
        unperm = nt(hi, c_perm[...]) + nt(lo, c_perm[...])
        row = lax.broadcasted_iota(jnp.int32, (CHUNK, HALF), 0)
        lane = lax.broadcasted_iota(jnp.int32, (CHUNK, HALF), 1)
        both = halves[0] + halves[1]
        mine = jnp.where(lane < 128, both, jnp.where(c == 0, halves[0], halves[1]))
        hi = mine.astype(BF16)
        lo = (mine - hi.astype(F32)).astype(BF16)
        lp = lane_place()
        small = nt(hi, lp) + nt(lo, lp)
        first = jnp.where(row < 34, halves[0], unperm[:, 0:HALF])
        first = jnp.where(row < 22, both, first)
        out_v[l, :, 0:HALF] = first
        out_v[l, :, HALF:] = jnp.where(row < 34, halves[1], unperm[:, HALF:])
        out_v[l, 0:16, 0:128] = small[0:16]
        u = rgotu[l, 0].astype(F32)
        for xx in range(1, 4):
            u = u + rgotu[l, xx].astype(F32)
        out_u[l] = u

    r1, r0 = scatters(1), scatters(0)

    def first_sums(r):
        for i in range(4):
            r["D1", i].start()
        r["O2"].start()

    def forward_on(r, *names):
        for n in names:
            r[n].forward()

    def next_ring(r, *names):
        for n in names:
            r[n + "2"].finish()
            r[n + "3"].start()

    def down_second(r):
        r["D1", 0].finish()
        r["D2"].start_far()
        r["D1", 1].finish()
        r["D1", 2].finish()
        r["D2"].start_near()
        r["D1", 3].finish()

    def finish_third(r, names):
        for n in names:
            r[n].finish()

    def backward(l, r, after_norm, after_down, in_ffn, before_heads, in_heads, before_query):
        gslot = 2 if l == 1 else 1
        G = W.at[gslot]
        after_norm()
        glT[...] = gl[...].T
        vg[5:6, :] = jnp.sum(gl[own, :].astype(F32), axis=0, keepdims=True)

        for b in range(2):
            rows = slice(b * HALF, (b + 1) * HALF)
            part = nn(glT[rows, :], mixed[l]).astype(BF16).reshape(2, 4, 48, HALF)
            G[2 * b:2 * b + 2, :, O0:O0 + 48, :] = part

        acc[...] = jnp.zeros_like(acc)

        @pl.loop(0, 4)
        def _(k):
            rows_d = pl.ds(pl.multiple_of(D0 + 48 * k, 16), 48)
            for b in range(2):
                rows = slice(b * HALF, (b + 1) * HALF)
                part = nn(glT[rows, :], act[l, k]).astype(BF16).reshape(2, 4, 48, HALF)
                G[2 * b:2 * b + 2, :, rows_d, :] = part

        first_sums(r)
        after_down()

        @pl.loop(0, 4)
        def _(k):
            serve(k, in_ffn)
            sums = jnp.zeros((1, HALF), F32)
            for b in range(2):
                rows = slice(b * TOK, (b + 1) * TOK)
                gh = nn(gl[rows, :], down_weight(l, k)) * slope[l, k, rows, :].astype(F32)
                gh = gh.astype(BF16)
                slope[l, k, rows, :] = gh
                sums = sums + jnp.sum(gh.astype(F32), axis=0, keepdims=True)
                for h in range(2):
                    acc[rows, h * HALF:(h + 1) * HALF] += nn(gh, up_weight(l, k, h))
            ubg[k] = jnp.broadcast_to(sums, (8, HALF))
            ghT = slope[l, k].T
            for h in range(2):
                part = nn(ghT, mlp[:, h * HALF:(h + 1) * HALF]).astype(BF16).reshape(4, 96, HALF)
                G[k, :, U0 + 96 * h:U0 + 96 * h + 96, :] = part

        r["U2"].start()
        r["V2"].start()
        before_heads()

        for b in range(2):
            rows = slice(b * TOK, (b + 1) * TOK)
            gm[rows, :] = nn(gl[rows, :], weight(l, O0)).astype(BF16)
        gmT[...] = gm[...].T

        if l == 1:
            dk[...] = jnp.zeros_like(dk)
            dv[...] = jnp.zeros_like(dv)

        @pl.loop(0, 12)
        def _(i):
            h, b = i // 2, i % 2
            hs = pl.ds(pl.multiple_of(h * HD, HD), HD)
            bs = pl.ds(pl.multiple_of(b * TOK, TOK), TOK)
            serve(i, in_heads)
            low = p_[l, h, b]
            probs = low.astype(F32)
            t = probs * nn(v_[bs, :], gmT[hs, bs])
            grad = (t - probs * jnp.sum(t, axis=0, keepdims=True)).astype(BF16)
            dq = nn(kvT[0:HD, bs], grad) * scale
            cs, sn = cosT[:, bs], sinT[:, bs]
            u1, u2 = dq[0:8], dq[8:16]
            dq = jnp.concatenate([u1 * cs + u2 * sn, u2 * cs - u1 * sn, dq[16:]], axis=0)
            mixT[hs, bs] = dq.astype(BF16)
            dk[bs, :] += nt(grad, qT[l, hs, bs])
            dv[bs, :] += nt(low, gmT[hs, bs])

        before_query()
        low = mixT[...].T
        gm[...] = low
        qsum = jnp.sum(low.astype(F32), axis=0, keepdims=True)
        zero = jnp.zeros_like(qsum)
        vg[4:5, :] = jnp.concatenate([jnp.where(c == 0, qsum, zero), jnp.where(c == 0, zero, qsum)], axis=1)
        if l == 0:
            keys = rotate_heads_back((dk[...] * scale).T, 1).T
            gs[...] = jnp.concatenate([keys, dv[...]], axis=1).astype(BF16)

    def query_grad(l, r):
        G = W.at[2 if l == 1 else 1]
        for b in range(2):
            rows = slice(b * HALF, (b + 1) * HALF)
            part = nn(attnT[rows, :], gm[...]).astype(BF16).reshape(2, 4, 48, HALF)
            G[2 * b:2 * b + 2, :, Q0:Q0 + 48, :] = part
        r["B2"].start()
        if l == 0:
            dkv = nn(attnT[...], gs[...]).astype(BF16).reshape(4, 4, 48, 128)
            G[:, :, KV0:KV0 + 16, :] = jnp.concatenate([dkv[:, :, 0:16], dkv[:, :, 16:32], dkv[:, :, 32:48]], axis=3)

    def fold_block(l, b, sums):
        rows = slice(b * TOK, (b + 1) * TOK)
        ea = nt(gm[rows, :], weight(l, Q0))
        if l == 0:
            ea = ea + nt(gs[rows, :], key_weight())
        h1[...] = ea

        def fold(i, sums):
            rows = pl.ds(pl.multiple_of(i * CH, CH), CH)
            all_rows = pl.ds(pl.multiple_of(b * TOK + i * CH, CH), CH)
            n = n_[all_rows, :] if l == 1 else norm_of(X2[b, rows, :].astype(F32))[0]
            ea, em = h1[rows, :], acc[all_rows, :]
            xs[b, rows, :] = (ea * vec(l, 0) + em * vec(l, 1)).astype(BF16)
            add = [ea * n, em * n, ea, em]
            return tuple(s + jnp.sum(a, axis=0, keepdims=True) for s, a in zip(sums, add))

        return lax.fori_loop(0, 4, fold, sums)

    def vector_grad(l, r, sums):
        G = W.at[2 if l == 1 else 1]
        for k in range(4):
            vg[k:k + 1, :] = sums[k]
        at = lax.broadcasted_iota(jnp.int32, (16, D), 1)
        rowk = lax.broadcasted_iota(jnp.int32, (16, D), 0)
        vv = jnp.where(rowk < 6, vg[...], 0.0)
        parts = [jnp.where((at >= 48 * m) & (at < 48 * m + 48), vv, 0.0).astype(BF16) for m in range(16)]
        small = nt(jnp.concatenate(parts, axis=0), c_s48[...]).astype(BF16)
        ub = jnp.concatenate([ubg[k][0:1, :] for k in range(4)], axis=1)
        at = lax.broadcasted_iota(jnp.int32, (16, 1536), 1)
        rowk = lax.broadcasted_iota(jnp.int32, (16, 1536), 0)
        ub = jnp.where(rowk == 6, jnp.broadcast_to(ub, (16, 1536)), 0.0)
        parts = [jnp.where((at >= 96 * m) & (at < 96 * m + 96), ub, 0.0).astype(BF16) for m in range(16)]
        wide = nt(jnp.concatenate(parts, axis=0), c_s96[...]).astype(BF16)
        both = jnp.concatenate([small, wide, jnp.zeros((256, 128), BF16)], axis=1)
        G[:, :, VEC0:VEC0 + 16, :] = both.reshape(4, 4, 16, HALF)
        r["A2"].start()

    def through_norm(n, inverse, g, s):
        m1 = jnp.mean(s, axis=-1, keepdims=True)
        m2 = jnp.mean(s * n, axis=-1, keepdims=True)
        return g + inverse * (s - m1 - n * m2)

    no_sums = (jnp.zeros((1, D), F32),) * 4

    attnT[...] = attn[...].T
    backward(
        1, r1, steps(), steps(),
        {3: steps((forward_on, r1, ("D1", 0), "O2"))},
        steps((forward_on, r1, ("D1", 1))),
        {4: steps((next_ring, r1, "O"), (forward_on, r1, ("D1", 2))), 9: steps((forward_on, r1, ("D1", 3)))},
        steps((forward_on, r1, "U2", "V2", "O3")),
    )
    swap = [to_sibling(6 + b, xs.at[b], xr.at[b]) for b in range(2)]
    sums = no_sums
    for b in range(2):
        sums = fold_block(1, b, sums)
        swap[b].start()
    query_grad(1, r1)
    vector_grad(1, r1, sums)
    r1["O3"].finish()
    norm_inputs(0, again=True)
    attnT[...] = attn[...].T
    down_second(r1)
    for cp in swap:
        cp.wait()

    @pl.loop(0, 8)
    def _(i):
        b = i // 4
        rows = pl.ds(pl.multiple_of((i % 4) * CH, CH), CH)
        s = xs[b, rows, :].astype(F32) + xr[b, rows, :].astype(F32)
        all_rows = pl.ds(pl.multiple_of(i * CH, CH), CH)
        g = through_norm(n_[all_rows, :], r_[all_rows, 0:1], gl[all_rows, :].astype(F32), s)
        gl[all_rows, :] = g.astype(BF16)

        @pl.when(b == c)
        def _():
            g_[rows, :] = g

    backward(
        0, r0,
        steps((forward_on, r1, "A2", "B2")),
        steps((forward_on, r1, "D2")),
        {
            1: steps((next_ring, r1, "U", "V")),
            2: steps((next_ring, r1, "A", "B", "D")),
            3: steps((forward_on, r1, "U3", "V3")),
        },
        steps((forward_on, r0, ("D1", 0), "O2"), (forward_on, r1, "A3", "B3", "D3")),
        {
            3: steps((forward_on, r0, ("D1", 1))),
            6: steps((forward_on, r0, ("D1", 2)), (next_ring, r0, "O")),
            10: steps((forward_on, r0, ("D1", 3))),
        },
        steps((forward_on, r0, "U2", "V2", "O3")),
    )
    query_grad(0, r0)
    sums = no_sums
    for b in range(2):
        sums = fold_block(0, b, sums)
    swap = to_sibling(8, xs.at[1 - c], xr.at[2])
    swap.start()
    vector_grad(0, r0, sums)
    finish_third(r1, ("U3", "V3", "A3", "B3", "D3"))
    finish_line(1)
    swap.wait()

    @pl.loop(0, 4)
    def _(i):
        rows = pl.ds(pl.multiple_of(i * CH, CH), CH)
        s = xs[c, rows, :].astype(F32) + xr[2, rows, :].astype(F32)
        n, inverse = norm_of(X2[c, rows, :].astype(F32))
        out_gx[rows, :] = through_norm(n, inverse, g_[rows, :], s).astype(BF16)

    forward_on(r0, "B2", "A2")
    down_second(r0)
    next_ring(r0, "U", "V", "B", "A")
    forward_on(r0, "D2", "U3", "V3")
    next_ring(r0, "D")
    forward_on(r0, "B3", "A3", "D3")
    last_sums(1)
    finish_third(r0, ("O3", "U3", "V3", "A3", "B3", "D3"))
    finish_line(0)
    last_sums(0)


def vmem(*shape, dtype=BF16):
    return pltpu.VMEM(shape, dtype)


def make_call():
    T2 = 2 * TOK
    scratch = [
        vmem(3, 4, 4, ROWS, HALF), vmem(2, 2, CHUNK, HALF), vmem(2, 48, HALF), vmem(2, 8, CHUNK, HALF), vmem(2, 4, 48, HALF),
        vmem(16, D, dtype=F32), vmem(2, 4, 8, HALF, dtype=F32),
        vmem(2, TOK, D), vmem(T2, D), vmem(2, 8, TOK, dtype=jnp.int32), vmem(8, T2, dtype=F32), vmem(8, T2, dtype=F32),
        vmem(2, TOK, TOK, dtype=F32), vmem(T2, D, dtype=F32), vmem(T2, 128, dtype=F32), vmem(TOK, D, dtype=F32),
        vmem(T2, D), vmem(T2, D), vmem(128, T2), vmem(T2, HD), vmem(T2, HD), vmem(2, HALF, T2), vmem(2, 6, 2, TOK, TOK),
        vmem(HALF, T2), vmem(2, T2, HALF), vmem(2, 4, T2, HALF), vmem(2, 4, T2, HALF),
        vmem(T2, D, dtype=F32), vmem(D, T2), vmem(D, T2), vmem(T2, HALF), vmem(HALF, T2),
        vmem(T2, HD, dtype=F32), vmem(T2, HD, dtype=F32), vmem(T2, 128), vmem(16, D, dtype=F32),
        vmem(4, 8, HALF, dtype=F32), vmem(TOK, D, dtype=F32), vmem(2, TOK, D), vmem(3, TOK, D),
        vmem(2, 6, 2, 48, HALF), vmem(2, 6, 2, 32, HALF), vmem(2, 6, 2, 48, HALF), vmem(2, 6, 2, 96, HALF), vmem(2, 6, 2, 96, HALF),
        vmem(2, 4, 6, 2, 48, HALF), vmem(2, 6, 2, 48, HALF),
        vmem(2, 6, 32, HALF), vmem(2, 6, 16, HALF), vmem(2, 6, 32, HALF), vmem(2, 6, 48, HALF), vmem(2, 6, 48, HALF), vmem(2, 6, 32, HALF),
        vmem(2, 8, CHUNK, HALF), vmem(2, 4, 48, HALF),
        *[vmem(*v.shape) for v in (CONSTS[i] for i in range(9))],
        pltpu.SemaphoreType.DMA((9,)), pltpu.SemaphoreType.DMA((9,)), pltpu.SemaphoreType.DMA((9,)),
        pltpu.SemaphoreType.DMA((4, 4)), pltpu.SemaphoreType.DMA((2, 14, 5)), pltpu.SemaphoreType.DMA((2, 16, 4)),
    ]
    whole = pl.BlockSpec(memory_space=pltpu.VMEM)
    return pl.pallas_call(
        kernel,
        out_shape=(
            jax.ShapeDtypeStruct((TOK, D), BF16),
            jax.ShapeDtypeStruct((TOK, D), BF16),
            jax.ShapeDtypeStruct((2, CHUNK, D), F32),
            jax.ShapeDtypeStruct((2, 48, HALF), F32),
        ),
        in_specs=[whole] * 14 + [pl.BlockSpec(memory_space=pl.ANY)] * 9,
        out_specs=(whole,) * 4,
        scratch_shapes=scratch,
        compiler_params=pltpu.CompilerParams(
            collective_id=0, has_side_effects=True, vmem_limit_bytes=64 * 2**20 - 65536
        ),
        name="two_layers",
    )


def pack_kernel(
    y, gx, v, u,
    o_y, o_gx, o_gain, o_nbias, o_q, o_qb, o_kv, o_o, o_ob, o_up, o_ub, o_down, o_db,
):
    o_y[...] = y[...]
    o_gx[...] = gx[...]
    for l in range(2):
        o_gain[l] = v[l, 0:2, 0:6]
        o_nbias[l] = v[l, 2:4, 0:6]
        o_qb[l:l + 1, :] = v[l, 4:5, 0:6]
        o_ob[l:l + 1, :] = v[l, 5:6, 0:6]
        o_db[l:l + 1, :] = v[l, 5:6, 0:6]
        o_ub[l:l + 1, :] = v[l, 6:7, 8:32]
        for h in range(2):
            o_up[l, :, h * HALF:(h + 1) * HALF] = u[l, 24 * h:24 * h + 24, :]
        for i in range(6):
            o_q[i, l:l + 1, :] = v[l, 22 + i:23 + i, :]
            o_o[i, l:l + 1, :] = v[l, 28 + i:29 + i, :]
            for g in range(4):
                o_down[i, l:l + 1, g * D:(g + 1) * D] = v[l, 34 + 4 * i + g:35 + 4 * i + g, :]
    o_kv[...] = v[0, 16:22, 0:128]


def pack(y, gx, v, u):
    whole = pl.BlockSpec(memory_space=pltpu.VMEM)
    shapes = [(2, 2, 6), (2, 2, 6), (6, 2, D), (2, 6), (6, 128), (6, 2, D), (2, 6), (2, 24, D), (2, 24), (6, 2, FF), (2, 6)]
    return pl.pallas_call(
        pack_kernel,
        out_shape=tuple(
            [jax.ShapeDtypeStruct((TOK, D), BF16)] * 2 + [jax.ShapeDtypeStruct(shape, F32) for shape in shapes]),
        in_specs=[whole] * 4,
        out_specs=(whole,) * 13,
        name="results",
    )(y, gx, v, u)


def on_device(
    layer_input, segments, norm_gain, norm_bias, query_weight, query_bias, keyval_weight, output_weight,
    output_bias, upward_weight, upward_bias, downward_weight, downward_bias, cotangent,
):
    consts = [jnp.asarray(v, BF16) for v in CONSTS]
    y, gx, gain, nbias, q, qb, kv, o, ob, up, ub, down, db = pack(*make_call()(
        layer_input, segments, cotangent, norm_gain, norm_bias, query_weight.transpose(1, 0, 2), query_bias,
        keyval_weight, output_weight.transpose(2, 0, 1), output_bias, upward_weight.transpose(0, 2, 1), upward_bias,
        downward_weight.transpose(2, 0, 1), downward_bias, *consts))
    return (
        y, gx, gain, nbias, q.transpose(1, 0, 2), qb, kv, o.transpose(1, 2, 0), ob, up.transpose(0, 2, 1), ub,
        down.transpose(1, 2, 0), db,
    )


def solution(mesh):
    in_specs = (
        P(("dp", "fsdp"), None),
        P(("dp", "fsdp"), None),
        P(None, None, ("dp", "fsdp")),
        P(None, None, ("dp", "fsdp")),
        P(None, ("dp", "fsdp"), None),
        P(None, ("dp", "fsdp")),
        P(("dp", "fsdp"), None),
        P(None, None, ("dp", "fsdp")),
        P(None, ("dp", "fsdp")),
        P(None, None, ("dp", "fsdp")),
        P(None, ("dp", "fsdp")),
        P(None, None, ("dp", "fsdp")),
        P(None, ("dp", "fsdp")),
        P(("dp", "fsdp"), None),
    )
    out_specs = (
        P(("dp", "fsdp"), None),
        P(("dp", "fsdp"), None),
        P(None, None, ("dp", "fsdp")),
        P(None, None, ("dp", "fsdp")),
        P(None, ("dp", "fsdp"), None),
        P(None, ("dp", "fsdp")),
        P(("dp", "fsdp"), None),
        P(None, None, ("dp", "fsdp")),
        P(None, ("dp", "fsdp")),
        P(None, None, ("dp", "fsdp")),
        P(None, ("dp", "fsdp")),
        P(None, None, ("dp", "fsdp")),
        P(None, ("dp", "fsdp")),
    )
    return jax.shard_map(on_device, mesh=mesh, in_specs=in_specs, out_specs=out_specs, check_vma=False)
```

```python
import functools

import jax
import jax.numpy as jnp
import numpy as np
from jax import lax
from jax.experimental import pallas as pl
from jax.experimental.pallas import tpu as pltpu
from jax.sharding import PartitionSpec as P

MESH = pl.DeviceIdType.MESH
F32 = jnp.float32
BF16 = jnp.bfloat16

H = 12
HD = 64
D = 768
FF = 3072
TOK = 256
HALF = 384
ROWS = 512
KV0, VEC0, Q0, O0, D0, U0 = 0, 16, 32, 80, 128, 320
CHUNK = 64

norm_epsilon = 1e-05
masked_score = -1e30
rotary_base = 10000.0
root_half = 0.7071067811865476
inverse_root_tau = 0.3989422804014327
scale = HD**-0.5


def place_constants():
    qod = np.zeros((288, 512), np.float32)
    kv = np.zeros((48, 512), np.float32)
    for s in range(8):
        for i in range(6):
            r = s * 6 + i
            qod[r, s * CHUNK + 22 + i] = 1
            qod[48 + r, s * CHUNK + 28 + i] = 1
            for g in range(4):
                qod[96 + 48 * g + r, s * CHUNK + 34 + 4 * i + g] = 1
            kv[r, s * CHUNK + 16 + i] = 1
    sums = np.zeros((256, 160), np.float32)
    sums_kv = np.zeros((256, 48), np.float32)
    for s in range(8):
        for i in range(6):
            for kind in range(3):
                sums[s * 32 + 6 * kind + i, 48 * kind + s * 6 + i] = 1
            sums_kv[s * 32 + 18 + i, s * 6 + i] = 1
        for k in range(8):
            sums[s * 32 + 24 + k, 144 + k] = 1
    up = np.zeros((192, 192), np.float32)
    for h in range(2):
        for x in range(4):
            for j in range(24):
                up[h * 96 + x * 24 + j, x * 48 + h * 24 + j] = 1
    perm = np.zeros((768, 768), np.float32)
    for chip in range(16):
        for c in range(2):
            for j in range(24):
                perm[chip * 48 + c * 24 + j, c * 384 + chip * 24 + j] = 1
    spread48 = np.zeros((128, 768), np.float32)
    spread48[np.arange(768) % 48, np.arange(768)] = 1
    spread96 = np.zeros((128, 1536), np.float32)
    spread96[np.arange(1536) % 96, np.arange(1536)] = 1
    return qod, kv, up, perm, spread48, spread96, sums, sums_kv, up.T


CONSTS = place_constants()


def nn(a, b):
    return jnp.dot(a, b, preferred_element_type=F32)


def nt(a, b):
    return lax.dot_general(a, b, (((1,), (1,)), ((), ())), preferred_element_type=F32)


def tn(a, b):
    return lax.dot_general(a, b, (((0,), (0,)), ((), ())), preferred_element_type=F32)


def ranges(lengths):
    at, out = 0, []
    for n in lengths:
        out.append((at, n))
        at += n
    return out


class Place:
    def __init__(self):
        self.z = lax.axis_index("dp")
        f = lax.axis_index("fsdp")
        self.y = f // 8
        self.x = (f // 2) % 4
        self.c = f % 2

    def dev(self, dz=0, dy=0, dx=0, dc=0):
        z = (self.z + dz) % 4
        y = (self.y + dy) % 4
        x = (self.x + dx) % 4
        c = (self.c + dc) % 2
        return (z, y * 8 + x * 2 + c)

    def along(self, axis, d):
        return self.dev(**{"d" + axis: d})

    def pos(self, axis):
        return getattr(self, axis)


class Ring:
    def __init__(self, me, axis, view, sems, many):
        self.me, self.axis, self.view, self.sems, self.many = me, axis, view, sems, many
        self.p = me.pos(axis)

    def _copy(self, to, src, dst, sem):
        return pltpu.make_async_remote_copy(
            src_ref=src,
            dst_ref=dst,
            send_sem=self.sems.at[0],
            recv_sem=self.sems.at[sem],
            device_id=self.me.along(self.axis, to),
            device_id_type=MESH,
        )

    def _await(self, ref, sem):
        pltpu.make_async_copy(ref, ref, self.sems.at[sem]).wait()

    def sent(self):
        self._await(self.many(3), 0)


class Gather(Ring):
    def _pass(self, to, k, h, sem):
        block = self.view(k % 4, h)
        self._copy(to, block, block, sem).start()

    def start(self):
        p = self.p
        self._pass(1, p, 0, 1)
        self._pass(-1, p, 1, 2)
        self._pass(1, p, 1, 3)
        self._pass(-1, p, 0, 3)

    def forward(self):
        p = self.p
        self._await(self.view((p + 3) % 4, 0), 1)
        self._pass(1, p + 3, 0, 4)
        self._await(self.view((p + 1) % 4, 1), 2)
        self._pass(-1, p + 1, 1, 4)

    def near(self):
        self._await(self.many(1), 3)

    def far(self):
        self._await(self.many(1), 4)

    def finish(self):
        self.near()
        self.far()
        self.sent()


class Scatter(Ring):
    def __init__(self, me, axis, view, sems, many, buf, leads, rows):
        super().__init__(me, axis, view, sems, many)
        self.buf, self.leads, self.rows = buf, leads, rows

    def _slot(self, j, h):
        ref = self.buf.at[j]
        n = self.rows[h]
        if n != ref.shape[-2]:
            ref = ref.at[tuple(slice(None) for _ in self.leads) + (pl.ds(0, n),)]
        return ref

    def _pass(self, to, k, h, slot, sem):
        self._copy(to, self.view(k % 4, h), self._slot(slot, h), sem).start()

    def _add(self, k, h, slots):
        target = self.view(k, h)
        srcs = [self._slot(s, h) for s in slots]

        def one(idx):
            total = target[idx].astype(F32)
            for s in srcs:
                total = total + s[idx].astype(F32)
            target[idx] = total.astype(BF16)

        if not self.leads:
            one((slice(None), slice(None)))
        else:

            @pl.loop(0, self.leads[0])
            def _(i):
                one((i,))

    def start_far(self):
        p = self.p
        self._pass(1, p + 2, 0, 0, 1)
        self._pass(-1, p + 2, 1, 1, 2)

    def start_near(self):
        p = self.p
        self._pass(1, p + 1, 1, 3, 3)
        self._pass(-1, p + 3, 0, 4, 3)

    def start(self):
        self.start_far()
        self.start_near()

    def forward(self):
        p = self.p
        self._await(self._slot(0, 0), 1)
        self._add((p + 1) % 4, 0, [0])
        self._pass(1, p + 1, 0, 2, 3)
        self._await(self._slot(1, 1), 2)
        self._add((p + 3) % 4, 1, [1])
        self._pass(-1, p + 3, 1, 5, 3)

    def finish(self):
        self._await(self.many(2), 3)
        self._add(self.p, 0, [2, 4])
        self._add(self.p, 1, [3, 5])
        self.sent()


class Direct(Ring):
    def __init__(self, me, axis, view, sems, many, buf):
        super().__init__(me, axis, view, sems, many)
        self.buf = buf

    def start(self):
        for j, to in enumerate((2, 1, -1)):
            self._copy(to, self.view((self.p + to) % 4), self.buf.at[j], 1).start()

    def finish(self):
        self._await(self.many(3), 1)
        target = self.view(self.p)
        total = target[...].astype(F32)
        for j in range(3):
            total = total + self.buf[j].astype(F32)
        target[...] = total.astype(BF16)
        self.sent()


def kernel(
    xin, seg, cot, w_gain, w_nbias, w_q, w_qb, w_kv, w_o, w_ob, w_up, w_ub, w_down, w_db, h_qod, h_kv, h_up, h_perm, h_s48, h_s96, h_sums, h_sums_kv, h_upT,
    out_y, out_gx, out_v, out_u,
    W, chunk, rawu, got, gotu, vecs, ubv,
    X2, gl, seg2, cosT, sinT, mbias, n_, r_, h1, attn, mlp, kvT, k_, v_, qT, p_, mixT, mixed, act, slope,
    acc, glT, attnT, gm, gmT, dk, dv, gs, vg, ubg, g_, xs, xr,
    bA2, bB2, bO2, bU2, bD1, bD2, bA3, bB3, bO3, bU3, bD3, back, rgot, rgotu,
    c_qod, c_kv, c_up, c_perm, c_s48, c_s96, c_sums, c_sums_kv, c_upT,
    const_sem, pair_send, pair_recv, line_sem, ag_sem, rs_sem,
):
    me = Place()
    z, y, x, c = me.z, me.y, me.x, me.c
    s_me = x * 2 + c

    consts = [(h_perm, c_perm), (h_qod, c_qod), (h_kv, c_kv), (h_up, c_up), (h_s48, c_s48), (h_s96, c_s96),
              (h_sums, c_sums), (h_sums_kv, c_sums_kv), (h_upT, c_upT)]
    const_copies = [pltpu.make_async_copy(h, v, const_sem.at[i]) for i, (h, v) in enumerate(consts)]
    for cp in const_copies:
        cp.start()

    bar = pltpu.get_barrier_semaphore()
    line = [(dx, dc) for dx in range(4) for dc in range(2) if (dx, dc) != (0, 0)]
    partners = [me.dev(dx=dx, dc=dc) for dx, dc in line]
    partners += [me.dev(dy=d) for d in (1, 2, 3)] + [me.dev(dz=d) for d in (1, 2, 3)]
    for d in partners:
        pl.semaphore_signal(bar, inc=1, device_id=d, device_id_type=MESH)
    sibling = me.dev(dc=1)

    def to_sibling(i, src, dst):
        return pltpu.make_async_remote_copy(
            src_ref=src, dst_ref=dst, send_sem=pair_send.at[i], recv_sem=pair_recv.at[i],
            device_id=sibling, device_id_type=MESH)

    def lane_place():
        r = lax.broadcasted_iota(jnp.int32, (128, HALF), 0)
        m = lax.broadcasted_iota(jnp.int32, (128, HALF), 1)
        small = (r < 6) & (m == r + 6 * s_me)
        wide = (r >= 8) & (r < 32) & (m == r - 8 + 128 + 24 * x)
        return jnp.where(small | wide, 1.0, 0.0).astype(BF16)

    def line_copies(l, bufs, into, bufu, intou, sems):
        out = []
        for dx, dc in line:
            t = (c + dc) % 2
            s_to = ((x + dx) % 4) * 2 + t
            out.append(pltpu.make_async_remote_copy(
                src_ref=bufs(s_to, t), dst_ref=into.at[l, s_me], send_sem=sems.at[0], recv_sem=sems.at[1],
                device_id=me.dev(dx=dx, dc=dc), device_id_type=MESH))
        for dx in range(1, 4):
            out.append(pltpu.make_async_remote_copy(
                src_ref=bufu((x + dx) % 4), dst_ref=intou.at[l, x], send_sem=sems.at[2],
                recv_sem=sems.at[3], device_id=me.dev(dx=dx), device_id_type=MESH))
        for cp in out:
            cp.start()

    def line_wait(sems, rows=CHUNK):
        seven, three = W.at[0, 0, 0, pl.ds(0, 7 * rows)], W.at[0, 0, 0, pl.ds(0, 144)]
        for i, ref in enumerate((seven, seven, three, three)):
            pltpu.make_async_copy(ref, ref, sems.at[i]).wait()

    h1[0:2 * CHUNK, :] = jnp.zeros((2 * CHUNK, D), F32)
    for l in range(2):
        h1[7 * l:7 * l + 2, 0:6] = w_gain[l].astype(F32)
        h1[7 * l + 2:7 * l + 4, 0:6] = w_nbias[l].astype(F32)
        for k, ref in ((4, w_qb), (5, w_ob), (6, w_db)):
            h1[7 * l + k:7 * l + k + 1, 0:6] = ref[...].astype(F32)[l:l + 1]
    h1[0:2, 8:32] = w_ub[...].astype(F32)
    h1[16:22, 0:128] = w_kv[...].astype(F32)
    for i in range(6):
        q2, o2, d2 = w_q[i].astype(F32), w_o[i].astype(F32), w_down[i].astype(F32)
        for l in range(2):
            at = CHUNK * l
            h1[at + 22 + i:at + 23 + i, :] = q2[l:l + 1]
            h1[at + 28 + i:at + 29 + i, :] = o2[l:l + 1]
            for g in range(4):
                h1[at + 34 + 4 * i + g:at + 35 + 4 * i + g, :] = d2[l:l + 1, g * D:(g + 1) * D]
    for l in range(2):
        u = w_up[l].astype(F32)
        rawu[l] = jnp.concatenate([u[:, 0:HALF], u[:, HALF:]], axis=0).astype(BF16)

    const_copies[0].wait()
    place = lane_place()

    def prepare(l):
        vf = h1[CHUNK * l:CHUNK * l + CHUNK, :]
        v = vf.astype(BF16)
        vp = nn(v, c_perm[...]).astype(BF16).astype(F32)
        row = lax.broadcasted_iota(jnp.int32, (CHUNK, HALF), 0)
        lane = lax.broadcasted_iota(jnp.int32, (CHUNK, HALF), 1)
        if l == 0:
            head = jnp.where(row < 16, nn(v[:, 0:128], place), jnp.where(lane < 128, vf[:, 0:HALF], 0.0))
        for t in range(2):
            part = jnp.where(row < 34, vf[:, t * HALF:(t + 1) * HALF], vp[:, t * HALF:(t + 1) * HALF])
            if l == 0:
                ours = jnp.where((lane < 128) | (c == t), head, 0.0)
                part = jnp.where(row < 22, ours, part)
            chunk[l, t] = part.astype(BF16)

    def send_chunks(l):
        line_copies(l, lambda s, t: chunk.at[l, t], got, lambda xx: rawu.at[l], gotu, line_sem.at[l])
        got[l, s_me] = chunk[l, c]
        gotu[l, x] = rawu[l]

    prepare(0)
    seg2[c] = jnp.broadcast_to(seg[...], (8, TOK))
    own = pl.ds(pl.multiple_of(c * TOK, TOK), TOK)

    pl.semaphore_wait(bar, len(partners))

    def to_sibling(i, src, dst):
        return pltpu.make_async_remote_copy(
            src_ref=src, dst_ref=dst, send_sem=pair_send.at[i], recv_sem=pair_recv.at[i],
            device_id=sibling, device_id_type=MESH)

    send_chunks(0)
    seg_copy = to_sibling(0, seg2.at[c], seg2.at[c])
    seg_copy.start()
    x_copy = to_sibling(1, xin, X2.at[c])
    x_copy.start()
    c_copy = to_sibling(2, cot, gl.at[own])
    c_copy.start()
    X2[c] = xin[...]
    gl[own, :] = cot[...]
    prepare(1)
    send_chunks(1)

    half_width = HD // 8
    frequency = np.float32(rotary_base) ** (-(np.arange(half_width, dtype=np.float32) * 2.0) / (2 * half_width))
    row = lax.broadcasted_iota(jnp.int32, (half_width, TOK), 0)
    freq = jnp.zeros((half_width, TOK), F32)
    for f in range(half_width):
        freq = jnp.where(row == f, float(frequency[f]), freq)
    seg_copy.wait()
    for b in range(2):
        docs = seg2[b].astype(F32)
        over_lanes = jnp.broadcast_to(docs[0:1], (TOK, TOK))
        over_rows = over_lanes.T
        earlier = jnp.sum(jnp.where(over_rows < over_lanes, 1.0, 0.0), axis=0, keepdims=True)
        place = lax.broadcasted_iota(jnp.int32, (1, TOK), 1).astype(F32) - earlier
        angle = jnp.broadcast_to(place, (8, TOK)) * freq
        cosT[:, b * TOK:(b + 1) * TOK] = jnp.cos(angle)
        sinT[:, b * TOK:(b + 1) * TOK] = jnp.sin(angle)
        kk = lax.broadcasted_iota(jnp.int32, (TOK, TOK), 0)
        qq = lax.broadcasted_iota(jnp.int32, (TOK, TOK), 1)
        mbias[b] = jnp.where((over_rows == over_lanes) & (kk <= qq), 0.0, masked_score)
    x_copy.wait()
    c_copy.wait()

    CH = 64

    def norm_of(h):
        centred = h - jnp.mean(h, axis=-1, keepdims=True)
        inverse = lax.rsqrt(jnp.mean(centred * centred, axis=-1, keepdims=True) + norm_epsilon)
        return centred * inverse, inverse

    def normalise(i, h):
        rows = pl.ds(pl.multiple_of(i * CH, CH), CH)
        n, inverse = norm_of(h)
        n_[rows, :] = n
        r_[rows, :] = jnp.broadcast_to(inverse, (CH, 128))

    def input_rows(i):
        return X2[i // 4, pl.ds(pl.multiple_of((i % 4) * CH, CH), CH), :].astype(F32)

    @pl.loop(0, 8)
    def _(i):
        normalise(i, input_rows(i))

    glT[...] = gl[...].T
    for cp in const_copies[1:]:
        cp.wait()

    def quarter(k):
        return pl.multiple_of(D0 + 48 * k, 16)

    def assemble(l):
        line_wait(line_sem.at[l])
        stack = got[l].reshape(512, HALF)
        W[l, z, y, Q0:D0, :] = nn(c_qod[0:96, :], stack).astype(BF16)
        down = nn(c_qod[pl.ds(pl.multiple_of(96 + 48 * x, 16), 48), :], stack).astype(BF16)
        W[l, z, y, pl.ds(quarter(x), 48), :] = down
        if l == 0:
            kv = nn(c_kv[...], stack[:, 0:128]).astype(BF16)
            W[0, z, y, KV0:KV0 + 16, :] = jnp.concatenate([kv[0:16], kv[16:32], kv[32:48]], axis=1)
            vec = got[0, 0, 0:16, :].astype(F32)
            for s in range(1, 8):
                vec = vec + got[0, s, 0:16, :].astype(F32)
            W[0, z, y, VEC0:VEC0 + 16, :] = vec.astype(BF16)
        W[l, z, y, U0:ROWS, :] = nn(c_up[...], gotu[l].reshape(192, HALF)).astype(BF16)

    def many(n, wide):
        if wide:
            return lambda count: W.at[0, pl.ds(0, count), :, pl.ds(0, n), :]
        return lambda count: W.at[0, 0, pl.ds(0, count), pl.ds(0, n), :]

    def cut(row0, n, h):
        first = halves(n)[0]
        return pl.ds(row0 if h == 0 else pl.multiple_of(row0 + first, 16), first if h == 0 else n - first)

    def halves(n):
        first = (n + 31) // 32 * 16
        return (first, n - first)

    def gathers(l):
        g = {}

        def y_then_z(i, name, row0, n):
            g[name + "2"] = Gather(me, "y", lambda k, h: W.at[l, z, k, cut(row0, n, h), :], ag_sem.at[l, i], many(n, False))
            g[name + "3"] = Gather(me, "z", lambda k, h: W.at[l, k, pl.ds(2 * h, 2), pl.ds(row0, n), :], ag_sem.at[l, i + 1],
                                   many(n, True))

        def z_then_y(i, name, row0, n):
            g[name + "2"] = Gather(me, "z", lambda k, h: W.at[l, k, y, cut(row0, n, h), :], ag_sem.at[l, i], many(n, False))
            g[name + "3"] = Gather(me, "y", lambda k, h: W.at[l, pl.ds(2 * h, 2), k, pl.ds(row0, n), :], ag_sem.at[l, i + 1],
                                   many(n, True))

        e0 = 0 if l == 0 else Q0
        en = (D0 - e0) // 2
        y_then_z(0, "E", e0, en)
        z_then_y(2, "F", e0 + en, en)
        z_then_y(4, "D", quarter(x), 48)
        y_then_z(6, "U", U0, 112)
        z_then_y(8, "V", U0 + 112, 80)
        for i, dy in enumerate((0, 1, 3, 2)):
            g["D4", i] = Gather(me, "x", lambda k, h, dy=dy: W.at[l, pl.ds(2 * h, 2), (y + dy) % 4, pl.ds(quarter(k), 48), :],
                                ag_sem.at[l, 10 + i], many(48, True))
        return g

    g0, g1 = gathers(0), gathers(1)

    def second_stage(l, g):
        assemble(l)
        for n in "EFDUV":
            g[n + "2"].start()

    def forward_on(r, *names):
        for n in names:
            r[n].forward()

    def third_stage(g, first="EFD", rest="UV"):
        for n in first:
            g[n + "2"].finish()
            g[n + "3"].start()
        g["D4", 0].start()
        for n in rest:
            g[n + "2"].finish()
            g[n + "3"].start()

    def first_quarters(g):
        g["D3"].forward()
        g["D4", 0].forward()
        g["D3"].near()
        g["D4", 1].start()
        g["D4", 2].start()

    def heads_ready(g):
        g["E3"].finish()
        g["F3"].finish()

    def last_quarter(g):
        g["D3"].far()
        g["D4", 3].start()
        g["D4", 1].forward()
        g["D4", 2].forward()

    def hidden_ready(g):
        g["U3"].finish()
        g["V3"].finish()

    def down_ready(g):
        g["D3"].sent()
        for i in range(4):
            g["D4", i].finish()

    second_stage(0, g0)
    forward_on(g0, "E2", "F2", "D2", "U2", "V2")
    third_stage(g0, rest="")
    g0["U2"].finish()
    g0["V2"].finish()
    forward_on(g0, "E3", "F3")
    g0["U3"].start()
    g0["V3"].start()
    second_stage(1, g1)
    heads_ready(g0)

    tile = W[0, :, :, VEC0:VEC0 + 16, :].reshape(256, HALF)
    wide = nn(tile[:, 0:128], c_s48[...])
    at = lax.broadcasted_iota(jnp.int32, (16, D), 1)
    total = jnp.zeros((16, D), F32)
    for m in range(16):
        total = total + jnp.where((at >= 48 * m) & (at < 48 * m + 48), wide[16 * m:16 * m + 16], 0.0)
    vecs[...] = total
    wide = nn(tile[:, 128:256], c_s96[...])
    at = lax.broadcasted_iota(jnp.int32, (16, 1536), 1)
    total = jnp.zeros((16, 1536), F32)
    for m in range(16):
        total = total + jnp.where((at >= 96 * m) & (at < 96 * m + 96), wide[16 * m:16 * m + 16], 0.0)
    for l in range(2):
        for k in range(4):
            ubv[l, k] = jnp.broadcast_to(total[l:l + 1, k * HALF:(k + 1) * HALF], (8, HALF))

    def vec(l, k):
        return vecs[7 * l + k:7 * l + k + 1, :]

    def norm_inputs(l, again=False):
        @pl.loop(0, 8)
        def _(i):
            rows = pl.ds(pl.multiple_of(i * CH, CH), CH)
            n = norm_of(input_rows(i))[0] if again else n_[rows, :]
            attn[rows, :] = (n * vec(l, 0) + vec(l, 2)).astype(BF16)
            mlp[rows, :] = (n * vec(l, 1) + vec(l, 3)).astype(BF16)

    def key_weight():
        kvw = W[0, :, :, KV0:KV0 + 16, :]
        return jnp.concatenate([kvw[..., 0:128], kvw[..., 128:256], kvw[..., 256:384]], axis=2).reshape(D, 128)

    def weight(l, row0, n=48):
        return W[l, :, :, pl.ds(row0, n), :].reshape(16 * n, HALF)

    def up_weight(l, k, h):
        return W[l, k, :, U0 + 96 * h:U0 + 96 * h + 96, :].reshape(HALF, HALF)

    def down_weight(l, k):
        return weight(l, pl.multiple_of(D0 + 48 * k, 16))

    def rotate_heads(v, heads):
        v = v.reshape(heads, HD, 512)
        cs, sn = cosT[...][None], sinT[...][None]
        u1, u2 = v[:, 0:8, :], v[:, 8:16, :]
        return jnp.concatenate([u1 * cs - u2 * sn, u2 * cs + u1 * sn, v[:, 16:, :]], axis=1).reshape(heads * HD, 512)

    def rotate_heads_back(v, heads):
        v = v.reshape(heads, HD, 512)
        cs, sn = cosT[...][None], sinT[...][None]
        u1, u2 = v[:, 0:8, :], v[:, 8:16, :]
        return jnp.concatenate([u1 * cs + u2 * sn, u2 * cs - u1 * sn, v[:, 16:, :]], axis=1).reshape(heads * HD, 512)

    def far_first(p, i):
        return (p + jnp.where(i == 0, 2, jnp.where(i == 1, 1, jnp.where(i == 2, 3, 0)))) % 4

    def serve(i, points):
        for at, step in points.items():
            pl.when(i == at)(step)

    def steps(*todo):
        def run():
            for step, *args in todo:
                step(*args)

        return run

    def down_block(l, rows):
        acc[rows, :] = nt(mixed[l, rows, :], weight(l, O0))
        for k in range(4):
            acc[rows, :] += nt(act[l, k, rows, :], down_weight(l, k))

    def forward(l, in_heads, before_ffn, in_ffn, after_hidden):
        norm_inputs(l)
        if l == 0:
            kv = nn(attn[...], key_weight()).T
            keys = rotate_heads(kv[0:HD], 1)
            kvT[0:HD, :] = keys.astype(BF16)
            kvT[HD:, :] = kv[HD:].astype(BF16)
            k_[...] = keys.T.astype(BF16)
            v_[...] = kv[HD:].T.astype(BF16)
        qb = vec(l, 4)
        qb = jnp.where(c == 0, qb[:, 0:HALF], qb[:, HALF:])
        q = nn(attn[...], weight(l, Q0)) + qb
        qT[l] = rotate_heads(q.T, 6).astype(BF16)

        @pl.loop(0, 6)
        def _(h):
            serve(h, in_heads)
            hs = pl.ds(pl.multiple_of(h * HD, HD), HD)
            for b in range(2):
                bs = slice(b * TOK, (b + 1) * TOK)
                s = nn(k_[bs, :], qT[l, hs, bs]) * scale + mbias[b]
                e = jnp.exp(s - jnp.max(s, axis=0, keepdims=True))
                low = (e * (1.0 / jnp.sum(e, axis=0, keepdims=True))).astype(BF16)
                p_[l, h, b] = low
                mixT[hs, bs] = nn(kvT[HD:, bs], low).astype(BF16)

        mixed[l] = mixT[...].T
        before_ffn()

        @pl.loop(0, 4)
        def _(i):
            k = far_first(x, i) if l == 1 else i
            serve(i, in_ffn)
            for b in range(2):
                rows = slice(b * TOK, (b + 1) * TOK)
                hid = nt(mlp[rows, 0:HALF], up_weight(l, k, 0)) + nt(mlp[rows, HALF:], up_weight(l, k, 1))
                hid = hid + ubv[l, k, 0:1, :]
                phi = 0.5 * (1.0 + lax.erf(hid * root_half))
                low = (hid * phi).astype(BF16)
                act[l, k, rows, :] = low
                slope[l, k, rows, :] = (phi + hid * jnp.exp(-0.5 * hid * hid) * inverse_root_tau).astype(BF16)
            after_hidden(i, k)

    forward(
        0,
        {
            0: steps((first_quarters, g0)),
            2: steps((forward_on, g0, "U3", "V3"), (forward_on, g1, "E2", "F2", "D2", "U2", "V2")),
            3: steps((last_quarter, g0)),
            5: steps((third_stage, g1)),
        },
        steps((forward_on, g0, ("D4", 3)), (hidden_ready, g0)),
        {
            1: steps((forward_on, g1, "E3", "F3")),
            2: steps((first_quarters, g1)),
            3: steps((forward_on, g1, "U3", "V3")),
        },
        lambda i, k: None,
    )
    down_ready(g0)
    swap = [to_sibling(3 + b, xs.at[b], xr.at[b]) for b in range(2)]
    for b in range(2):
        down_block(0, slice(b * TOK, (b + 1) * TOK))
        xs[b] = acc[b * TOK:(b + 1) * TOK, :].astype(BF16)
        swap[b].start()
        if b == 0:
            last_quarter(g1)
    heads_ready(g1)
    for cp in swap:
        cp.wait()

    @pl.loop(0, 8)
    def _(i):
        b = i // 4
        rows = pl.ds(pl.multiple_of((i % 4) * CH, CH), CH)
        h = X2[b, rows, :].astype(F32) + (vec(0, 5) + vec(0, 6))
        h = h + (xs[b, rows, :].astype(F32) + xr[b, rows, :].astype(F32))
        normalise(i, h)

        @pl.when(b == c)
        def _():
            h1[rows, :] = h

    def scatters(l):
        gslot = 2 if l == 1 else 1
        g = {}

        def y_then_z(i, name, row0, n, b2, b3):
            g[name + "2"] = Scatter(me, "y", lambda k, h: W.at[gslot, pl.ds(2 * h, 2), k, pl.ds(row0, n), :],
                                    rs_sem.at[l, i], many(n, True), b2.at[l], (2,), (n, n))
            g[name + "3"] = Direct(me, "z", lambda k: W.at[gslot, k, y, pl.ds(row0, n), :], rs_sem.at[l, i + 1],
                                   many(n, False), b3.at[l, :, pl.ds(0, n)])

        for i, dy in enumerate((2, 1, 3, 0)):
            g["D1", i] = Scatter(me, "x", lambda k, h, dy=dy: W.at[gslot, pl.ds(2 * h, 2), (y + dy) % 4, pl.ds(quarter(k), 48), :],
                                 rs_sem.at[l, i], many(48, True), bD1.at[l, i], (2,), (48, 48))
        y_then_z(4, "D", quarter(x), 48, bD2, bD3)
        y_then_z(6, "O", O0, 48, bO2, bO3)
        a0 = 0 if l == 0 else VEC0
        y_then_z(8, "A", a0, 48 - a0, bA2, bA3)
        y_then_z(10, "B", 48, 32, bB2, bB3)
        g["U2"] = Scatter(me, "z", lambda k, h: W.at[gslot, k, pl.ds(2 * h, 2), pl.ds(U0, 192), :], rs_sem.at[l, 12],
                          many(192, True), bU2.at[l], (2,), (192, 192))
        g["U3"] = Scatter(me, "y", lambda k, h: W.at[gslot, z, k, cut(U0, 192, h), :], rs_sem.at[l, 13],
                          many(192, False), bU3.at[l], (), (96, 96))
        return g

    def finish_line(l):
        B = W.at[2 if l == 1 else 1, z, y]
        rows = jnp.concatenate([B[Q0:D0, :], B[pl.ds(quarter(x), 48), :], B[VEC0:VEC0 + 16, :]], axis=0)
        stack = nn(c_sums[...], rows)
        if l == 0:
            kv = B[KV0:KV0 + 16, :]
            kv = jnp.concatenate([kv[:, 0:128], kv[:, 128:256], kv[:, 256:384]], axis=0)
            stack = stack + jnp.concatenate([nn(c_sums_kv[...], kv), jnp.zeros((256, 256), F32)], axis=1)
        back[l] = stack.astype(BF16).reshape(8, 32, HALF)
        gotu[l] = nn(c_upT[...], B[U0:ROWS, :]).astype(BF16).reshape(4, 48, HALF)
        line_copies(l, lambda s, t: back.at[l, s], rgot, lambda xx: gotu.at[l, xx], rgotu, line_sem.at[2 + l])
        rgot[l, s_me] = back[l, s_me]
        rgotu[l, x] = gotu[l, x]

    def last_sums(l):
        line_wait(line_sem.at[2 + l], 32)
        halves, tiles = [], []
        for t in range(2):
            parts = [rgot[l, 2 * xx + t].astype(F32) for xx in range(4)]
            halves.append(parts[0] + parts[1] + parts[2] + parts[3])
        for xx in range(4):
            tiles.append(jnp.concatenate([rgot[l, 2 * xx, 0:32, :], rgot[l, 2 * xx + 1, 0:32, :]], axis=1))
        unperm = nt(jnp.concatenate(tiles, axis=0), c_perm[...])
        row = lax.broadcasted_iota(jnp.int32, (32, HALF), 0)
        lane = lax.broadcasted_iota(jnp.int32, (32, HALF), 1)
        both = halves[0] + halves[1]
        mine = jnp.where(lane < 128, both, jnp.where(c == 0, halves[0], halves[1]))
        hi = mine.astype(BF16)
        lo = (mine - hi.astype(F32)).astype(BF16)
        spot = lane_place()
        small = nt(hi, spot) + nt(lo, spot)
        out_v[l, 0:32, 0:HALF] = jnp.where(row < 18, halves[0], both)
        out_v[l, 0:32, HALF:] = halves[1]
        out_v[l, 24:32, 0:128] = small[24:32]
        for xx in range(4):
            out_v[l, 32 + 16 * xx:48 + 16 * xx, :] = unperm[32 * xx + 8:32 * xx + 24]
        u = rgotu[l, 0].astype(F32)
        for xx in range(1, 4):
            u = u + rgotu[l, xx].astype(F32)
        out_u[l] = u

    r1, r0 = scatters(1), scatters(0)

    def first_sums(r):
        for i in range(4):
            r["D1", i].start()
        r["O2"].start()

    def next_ring(r, *names):
        for n in names:
            r[n + "2"].finish()
            r[n + "3"].start()

    def down_second(r):
        r["D1", 0].finish()
        r["D2"].start_far()
        r["D1", 1].finish()
        r["D1", 2].finish()
        r["D2"].start_near()
        r["D1", 3].finish()

    def finish_third(r, names):
        for n in names:
            r[n].finish()

    def out_grad(l):
        for b in range(2):
            rows = slice(b * HALF, (b + 1) * HALF)
            part = nn(glT[rows, :], mixed[l]).astype(BF16).reshape(2, 4, 48, HALF)
            W[2 if l == 1 else 1, 2 * b:2 * b + 2, :, O0:O0 + 48, :] = part

    def down_grad(l, r, i, k):
        rows_d = pl.ds(pl.multiple_of(D0 + 48 * k, 16), 48)
        for b in range(2):
            rows = slice(b * HALF, (b + 1) * HALF)
            part = nn(glT[rows, :], act[l, k]).astype(BF16).reshape(2, 4, 48, HALF)
            W[2 if l == 1 else 1, 2 * b:2 * b + 2, :, rows_d, :] = part
        rings = [r["D1", j] for j in range(4)]
        serve(i, {0: steps(*((ring.start_far,) for ring in rings)), 2: steps(*((ring.start_near,) for ring in rings))})

    def backward(l, r, in_ffn, before_heads, in_heads, before_query):
        G = W.at[2 if l == 1 else 1]
        vg[5:6, :] = jnp.sum(gl[own, :].astype(F32), axis=0, keepdims=True)
        acc[...] = jnp.zeros_like(acc)

        @pl.loop(0, 4)
        def _(i):
            k = far_first(z, i)
            serve(i, in_ffn)
            sums = jnp.zeros((1, HALF), F32)
            for b in range(2):
                rows = slice(b * TOK, (b + 1) * TOK)
                gh = nn(gl[rows, :], down_weight(l, k)) * slope[l, k, rows, :].astype(F32)
                gh = gh.astype(BF16)
                slope[l, k, rows, :] = gh
                sums = sums + jnp.sum(gh.astype(F32), axis=0, keepdims=True)
                for h in range(2):
                    acc[rows, h * HALF:(h + 1) * HALF] += nn(gh, up_weight(l, k, h))
            ubg[k] = jnp.broadcast_to(sums, (8, HALF))
            ghT = slope[l, k].T
            for h in range(2):
                part = nn(ghT, mlp[:, h * HALF:(h + 1) * HALF]).astype(BF16).reshape(4, 96, HALF)
                G[k, :, U0 + 96 * h:U0 + 96 * h + 96, :] = part
            serve(i, {0: r["U2"].start_far, 2: r["U2"].start_near})

        before_heads()

        for b in range(2):
            rows = slice(b * TOK, (b + 1) * TOK)
            gm[rows, :] = nn(gl[rows, :], weight(l, O0)).astype(BF16)
        gmT[...] = gm[...].T

        if l == 1:
            dk[...] = jnp.zeros_like(dk)
            dv[...] = jnp.zeros_like(dv)

        @pl.loop(0, 6)
        def _(h):
            serve(h, in_heads)
            hs = pl.ds(pl.multiple_of(h * HD, HD), HD)
            for b in range(2):
                bs = slice(b * TOK, (b + 1) * TOK)
                low = p_[l, h, b]
                probs = low.astype(F32)
                t = probs * nn(v_[bs, :], gmT[hs, bs])
                grad = (t - probs * jnp.sum(t, axis=0, keepdims=True)).astype(BF16)
                dq = nn(kvT[0:HD, bs], grad) * scale
                cs, sn = cosT[:, bs], sinT[:, bs]
                u1, u2 = dq[0:8], dq[8:16]
                dq = jnp.concatenate([u1 * cs + u2 * sn, u2 * cs - u1 * sn, dq[16:]], axis=0)
                mixT[hs, bs] = dq.astype(BF16)
                dk[bs, :] += nt(grad, qT[l, hs, bs])
                dv[bs, :] += nt(low, gmT[hs, bs])

        before_query()
        low = mixT[...].T
        gm[...] = low
        qsum = jnp.sum(low.astype(F32), axis=0, keepdims=True)
        zero = jnp.zeros_like(qsum)
        vg[4:5, :] = jnp.concatenate([jnp.where(c == 0, qsum, zero), jnp.where(c == 0, zero, qsum)], axis=1)
        if l == 0:
            keys = rotate_heads_back((dk[...] * scale).T, 1).T
            gs[...] = jnp.concatenate([keys, dv[...]], axis=1).astype(BF16)

    def query_grad(l, r):
        G = W.at[2 if l == 1 else 1]
        for b in range(2):
            rows = slice(b * HALF, (b + 1) * HALF)
            part = nn(attnT[rows, :], gm[...]).astype(BF16).reshape(2, 4, 48, HALF)
            G[2 * b:2 * b + 2, :, Q0:Q0 + 48, :] = part
        r["B2"].start()
        if l == 0:
            dkv = nn(attnT[...], gs[...]).astype(BF16).reshape(4, 4, 48, 128)
            G[:, :, KV0:KV0 + 16, :] = jnp.concatenate([dkv[:, :, 0:16], dkv[:, :, 16:32], dkv[:, :, 32:48]], axis=3)

    def fold_block(l, b, sums):
        hold = g_ if l == 1 else h1
        rows = slice(b * TOK, (b + 1) * TOK)
        ea = nt(gm[rows, :], weight(l, Q0))
        if l == 0:
            ea = ea + nt(gs[rows, :], key_weight())
        hold[...] = ea

        def fold(i, sums):
            rows = pl.ds(pl.multiple_of(i * CH, CH), CH)
            all_rows = pl.ds(pl.multiple_of(b * TOK + i * CH, CH), CH)
            n = n_[all_rows, :] if l == 1 else norm_of(X2[b, rows, :].astype(F32))[0]
            ea, em = hold[rows, :], acc[all_rows, :]
            xs[b, rows, :] = (ea * vec(l, 0) + em * vec(l, 1)).astype(BF16)
            add = [ea * n, em * n, ea, em]
            return tuple(s + jnp.sum(a, axis=0, keepdims=True) for s, a in zip(sums, add))

        return lax.fori_loop(0, 4, fold, sums)

    def vector_grad(l, r, sums):
        G = W.at[2 if l == 1 else 1]
        for k in range(4):
            vg[k:k + 1, :] = sums[k]
        at = lax.broadcasted_iota(jnp.int32, (16, D), 1)
        rowk = lax.broadcasted_iota(jnp.int32, (16, D), 0)
        vv = jnp.where(rowk < 6, vg[...], 0.0)
        parts = [jnp.where((at >= 48 * m) & (at < 48 * m + 48), vv, 0.0).astype(BF16) for m in range(16)]
        small = nt(jnp.concatenate(parts, axis=0), c_s48[...]).astype(BF16)
        ub = jnp.concatenate([ubg[k][0:1, :] for k in range(4)], axis=1)
        at = lax.broadcasted_iota(jnp.int32, (16, 1536), 1)
        rowk = lax.broadcasted_iota(jnp.int32, (16, 1536), 0)
        ub = jnp.where(rowk == 6, jnp.broadcast_to(ub, (16, 1536)), 0.0)
        parts = [jnp.where((at >= 96 * m) & (at < 96 * m + 96), ub, 0.0).astype(BF16) for m in range(16)]
        wide = nt(jnp.concatenate(parts, axis=0), c_s96[...]).astype(BF16)
        both = jnp.concatenate([small, wide, jnp.zeros((256, 128), BF16)], axis=1)
        G[:, :, VEC0:VEC0 + 16, :] = both.reshape(4, 4, 16, HALF)
        r["A2"].start()

    def through_norm(n, inverse, g, s):
        m1 = jnp.mean(s, axis=-1, keepdims=True)
        m2 = jnp.mean(s * n, axis=-1, keepdims=True)
        return g + inverse * (s - m1 - n * m2)

    no_sums = (jnp.zeros((1, D), F32),) * 4

    forward(
        1,
        {1: steps((g1["D4", 3].forward,))},
        steps((out_grad, 1), (r1["O2"].start,), (hidden_ready, g1)),
        {},
        lambda i, k: down_grad(1, r1, i, k),
    )
    attnT[...] = attn[...].T
    down_ready(g1)
    backward(
        1, r1,
        {1: steps((forward_on, r1, "O2")), 3: steps((forward_on, r1, ("D1", 0)))},
        steps((forward_on, r1, ("D1", 1)), (next_ring, r1, "O")),
        {2: steps((forward_on, r1, ("D1", 2))), 4: steps((forward_on, r1, ("D1", 3)))},
        steps((forward_on, r1, "U2")),
    )
    swap = [to_sibling(6 + b, xs.at[b], xr.at[2 + b]) for b in range(2)]
    sums = no_sums
    for b in range(2):
        sums = fold_block(1, b, sums)
        swap[b].start()
    query_grad(1, r1)
    vector_grad(1, r1, sums)
    other = pl.ds(pl.multiple_of((1 - c) * TOK, TOK), TOK)
    down_block(1, other)
    xs[2] = acc[other, :].astype(BF16)
    y_copy = to_sibling(5, xs.at[2], xr.at[0])
    down_block(1, own)
    for cp in swap:
        cp.wait()
    y_copy.start()

    @pl.loop(0, 8)
    def _(i):
        b = i // 4
        rows = pl.ds(pl.multiple_of((i % 4) * CH, CH), CH)
        s = xs[b, rows, :].astype(F32) + xr[2 + b, rows, :].astype(F32)
        all_rows = pl.ds(pl.multiple_of(i * CH, CH), CH)
        g = through_norm(n_[all_rows, :], r_[all_rows, 0:1], gl[all_rows, :].astype(F32), s)
        gl[all_rows, :] = g.astype(BF16)

        @pl.when(b == c)
        def _():
            g_[rows, :] = g

    down_second(r1)
    forward_on(r1, "A2", "B2")
    glT[...] = gl[...].T

    @pl.loop(0, 4)
    def _(i):
        down_grad(0, r0, i, far_first(x, i))

    out_grad(0)
    r0["O2"].start()
    norm_inputs(0, again=True)
    attnT[...] = attn[...].T
    y_copy.wait()
    out_y[...] = (h1[...] + (vec(1, 5) + vec(1, 6)) + acc[own, :] + xr[0].astype(F32)).astype(BF16)
    backward(
        0, r0,
        {
            1: steps((forward_on, r0, "O2")),
            2: steps((next_ring, r1, "U"), (forward_on, r1, "D2")),
            3: steps((next_ring, r1, "A", "B"), (forward_on, r0, ("D1", 0))),
        },
        steps((forward_on, r0, ("D1", 1))),
        {
            0: steps((next_ring, r0, "O")),
            1: steps((forward_on, r0, ("D1", 2))),
            2: steps((next_ring, r1, "D"), (forward_on, r1, "U3")),
            3: steps((forward_on, r0, "U2", ("D1", 3))),
        },
        steps(),
    )
    query_grad(0, r0)
    sums = no_sums
    for b in range(2):
        sums = fold_block(0, b, sums)
    swap = to_sibling(8, xs.at[1 - c], xr.at[1])
    swap.start()
    r0["D1", 0].finish()
    r0["D2"].start_far()
    vector_grad(0, r0, sums)
    r0["D1", 1].finish()
    r0["D1", 2].finish()
    r0["D2"].start_near()
    r0["D1", 3].finish()
    forward_on(r0, "B2")
    next_ring(r0, "U")
    finish_third(r1, ("O3", "A3", "B3", "D3", "U3"))
    finish_line(1)
    forward_on(r0, "A2", "D2")
    next_ring(r0, "B", "A", "D")
    forward_on(r0, "U3")
    swap.wait()

    @pl.loop(0, 4)
    def _(i):
        rows = pl.ds(pl.multiple_of(i * CH, CH), CH)
        s = xs[c, rows, :].astype(F32) + xr[1, rows, :].astype(F32)
        n, inverse = norm_of(X2[c, rows, :].astype(F32))
        out_gx[rows, :] = through_norm(n, inverse, g_[rows, :], s).astype(BF16)

    last_sums(1)
    finish_third(r0, ("O3", "U3", "B3", "A3", "D3"))
    finish_line(0)
    last_sums(0)


def vmem(*shape, dtype=BF16):
    return pltpu.VMEM(shape, dtype)


def make_call():
    T2 = 2 * TOK
    scratch = [
        vmem(3, 4, 4, ROWS, HALF), vmem(2, 2, CHUNK, HALF), vmem(2, 48, HALF), vmem(2, 8, CHUNK, HALF), vmem(2, 4, 48, HALF),
        vmem(16, D, dtype=F32), vmem(2, 4, 8, HALF, dtype=F32),
        vmem(2, TOK, D), vmem(T2, D), vmem(2, 8, TOK, dtype=jnp.int32), vmem(8, T2, dtype=F32), vmem(8, T2, dtype=F32),
        vmem(2, TOK, TOK, dtype=F32), vmem(T2, D, dtype=F32), vmem(T2, 128, dtype=F32), vmem(TOK, D, dtype=F32),
        vmem(T2, D), vmem(T2, D), vmem(128, T2), vmem(T2, HD), vmem(T2, HD), vmem(2, HALF, T2), vmem(2, 6, 2, TOK, TOK),
        vmem(HALF, T2), vmem(2, T2, HALF), vmem(2, 4, T2, HALF), vmem(2, 4, T2, HALF),
        vmem(T2, D, dtype=F32), vmem(D, T2), vmem(D, T2), vmem(T2, HALF), vmem(HALF, T2),
        vmem(T2, HD, dtype=F32), vmem(T2, HD, dtype=F32), vmem(T2, 128), vmem(16, D, dtype=F32),
        vmem(4, 8, HALF, dtype=F32), vmem(TOK, D, dtype=F32), vmem(3, TOK, D), vmem(4, TOK, D),
        vmem(2, 6, 2, 48, HALF), vmem(2, 6, 2, 32, HALF), vmem(2, 6, 2, 48, HALF), vmem(2, 6, 2, 192, HALF),
        vmem(2, 4, 6, 2, 48, HALF), vmem(2, 6, 2, 48, HALF),
        vmem(2, 3, 48, HALF), vmem(2, 3, 32, HALF), vmem(2, 3, 48, HALF), vmem(2, 6, 96, HALF), vmem(2, 3, 48, HALF),
        vmem(2, 8, 32, HALF), vmem(2, 8, 32, HALF), vmem(2, 4, 48, HALF),
        *[vmem(*v.shape) for v in (CONSTS[i] for i in range(9))],
        pltpu.SemaphoreType.DMA((9,)), pltpu.SemaphoreType.DMA((9,)), pltpu.SemaphoreType.DMA((9,)),
        pltpu.SemaphoreType.DMA((4, 4)), pltpu.SemaphoreType.DMA((2, 14, 5)), pltpu.SemaphoreType.DMA((2, 14, 4)),
    ]
    whole = pl.BlockSpec(memory_space=pltpu.VMEM)
    return pl.pallas_call(
        kernel,
        out_shape=(
            jax.ShapeDtypeStruct((TOK, D), BF16),
            jax.ShapeDtypeStruct((TOK, D), BF16),
            jax.ShapeDtypeStruct((2, 96, D), F32),
            jax.ShapeDtypeStruct((2, 48, HALF), F32),
        ),
        in_specs=[whole] * 14 + [pl.BlockSpec(memory_space=pl.ANY)] * 9,
        out_specs=(whole,) * 4,
        scratch_shapes=scratch,
        compiler_params=pltpu.CompilerParams(
            collective_id=0, has_side_effects=True, vmem_limit_bytes=64 * 2**20 - 65536
        ),
        name="two_layers",
    )


def pack_kernel(
    y, gx, v, u,
    o_y, o_gx, o_gain, o_nbias, o_q, o_qb, o_kv, o_o, o_ob, o_up, o_ub, o_down, o_db,
):
    o_y[...] = y[...]
    o_gx[...] = gx[...]
    for l in range(2):
        o_gain[l] = v[l, 24:26, 0:6]
        o_nbias[l] = v[l, 26:28, 0:6]
        o_qb[l:l + 1, :] = v[l, 28:29, 0:6]
        o_ob[l:l + 1, :] = v[l, 29:30, 0:6]
        o_db[l:l + 1, :] = v[l, 29:30, 0:6]
        o_ub[l:l + 1, :] = v[l, 30:31, 8:32]
        for h in range(2):
            o_up[l, :, h * HALF:(h + 1) * HALF] = u[l, 24 * h:24 * h + 24, :]
        for i in range(6):
            o_q[i, l:l + 1, :] = v[l, i:i + 1, :]
            o_o[i, l:l + 1, :] = v[l, 6 + i:7 + i, :]
            for g in range(4):
                at = 32 + 16 * g + 4 + i
                o_down[i, l:l + 1, g * D:(g + 1) * D] = v[l, at:at + 1, :]
    o_kv[...] = v[0, 18:24, 0:128]


def pack(y, gx, v, u):
    whole = pl.BlockSpec(memory_space=pltpu.VMEM)
    shapes = [(2, 2, 6), (2, 2, 6), (6, 2, D), (2, 6), (6, 128), (6, 2, D), (2, 6), (2, 24, D), (2, 24), (6, 2, FF), (2, 6)]
    return pl.pallas_call(
        pack_kernel,
        out_shape=tuple(
            [jax.ShapeDtypeStruct((TOK, D), BF16)] * 2 + [jax.ShapeDtypeStruct(shape, F32) for shape in shapes]),
        in_specs=[whole] * 4,
        out_specs=(whole,) * 13,
        name="results",
    )(y, gx, v, u)


def on_device(
    layer_input, segments, norm_gain, norm_bias, query_weight, query_bias, keyval_weight, output_weight,
    output_bias, upward_weight, upward_bias, downward_weight, downward_bias, cotangent,
):
    consts = [jnp.asarray(v, BF16) for v in CONSTS]
    y, gx, gain, nbias, q, qb, kv, o, ob, up, ub, down, db = pack(*make_call()(
        layer_input, segments, cotangent, norm_gain, norm_bias, query_weight.transpose(1, 0, 2), query_bias,
        keyval_weight, output_weight.transpose(2, 0, 1), output_bias, upward_weight.transpose(0, 2, 1), upward_bias,
        downward_weight.transpose(2, 0, 1), downward_bias, *consts))
    return (
        y, gx, gain, nbias, q.transpose(1, 0, 2), qb, kv, o.transpose(1, 2, 0), ob, up.transpose(0, 2, 1), ub,
        down.transpose(1, 2, 0), db,
    )


def solution(mesh):
    in_specs = (
        P(("dp", "fsdp"), None),
        P(("dp", "fsdp"), None),
        P(None, None, ("dp", "fsdp")),
        P(None, None, ("dp", "fsdp")),
        P(None, ("dp", "fsdp"), None),
        P(None, ("dp", "fsdp")),
        P(("dp", "fsdp"), None),
        P(None, None, ("dp", "fsdp")),
        P(None, ("dp", "fsdp")),
        P(None, None, ("dp", "fsdp")),
        P(None, ("dp", "fsdp")),
        P(None, None, ("dp", "fsdp")),
        P(None, ("dp", "fsdp")),
        P(("dp", "fsdp"), None),
    )
    out_specs = (
        P(("dp", "fsdp"), None),
        P(("dp", "fsdp"), None),
        P(None, None, ("dp", "fsdp")),
        P(None, None, ("dp", "fsdp")),
        P(None, ("dp", "fsdp"), None),
        P(None, ("dp", "fsdp")),
        P(("dp", "fsdp"), None),
        P(None, None, ("dp", "fsdp")),
        P(None, ("dp", "fsdp")),
        P(None, None, ("dp", "fsdp")),
        P(None, ("dp", "fsdp")),
        P(None, None, ("dp", "fsdp")),
        P(None, ("dp", "fsdp")),
    )
    return jax.shard_map(on_device, mesh=mesh, in_specs=in_specs, out_specs=out_specs, check_vma=False)
```

```python
import functools

import jax
import jax.numpy as jnp
import numpy as np
from jax import lax
from jax.experimental import pallas as pl
from jax.experimental.pallas import tpu as pltpu
from jax.sharding import PartitionSpec as P

MESH = pl.DeviceIdType.MESH
F32 = jnp.float32
BF16 = jnp.bfloat16

H = 12
HD = 64
D = 768
FF = 3072
TOK = 256
HALF = 384
ROWS = 512
KV0, VEC0, Q0, O0, D0, U0 = 0, 16, 32, 80, 128, 320
CHUNK = 64

norm_epsilon = 1e-05
masked_score = -1e30
rotary_base = 10000.0
root_half = 0.7071067811865476
inverse_root_tau = 0.3989422804014327
scale = HD**-0.5


def place_constants():
    qod = np.zeros((288, 512), np.float32)
    kv = np.zeros((48, 512), np.float32)
    for s in range(8):
        for i in range(6):
            r = s * 6 + i
            qod[r, s * CHUNK + 22 + i] = 1
            qod[48 + r, s * CHUNK + 28 + i] = 1
            for g in range(4):
                qod[96 + 48 * g + r, s * CHUNK + 34 + 4 * i + g] = 1
            kv[r, s * CHUNK + 16 + i] = 1
    sums = np.zeros((256, 160), np.float32)
    sums_kv = np.zeros((256, 48), np.float32)
    for s in range(8):
        for i in range(6):
            for kind in range(3):
                sums[s * 32 + 6 * kind + i, 48 * kind + s * 6 + i] = 1
            sums_kv[s * 32 + 18 + i, s * 6 + i] = 1
        for k in range(8):
            sums[s * 32 + 24 + k, 144 + k] = 1
    up = np.zeros((192, 192), np.float32)
    for h in range(2):
        for x in range(4):
            for j in range(24):
                up[h * 96 + x * 24 + j, x * 48 + h * 24 + j] = 1
    perm = np.zeros((768, 768), np.float32)
    for chip in range(16):
        for c in range(2):
            for j in range(24):
                perm[chip * 48 + c * 24 + j, c * 384 + chip * 24 + j] = 1
    spread48 = np.zeros((128, 768), np.float32)
    spread48[np.arange(768) % 48, np.arange(768)] = 1
    spread96 = np.zeros((128, 1536), np.float32)
    spread96[np.arange(1536) % 96, np.arange(1536)] = 1
    return qod, kv, up, perm, spread48, spread96, sums, sums_kv, up.T


CONSTS = place_constants()


def nn(a, b):
    return jnp.dot(a, b, preferred_element_type=F32)


def nt(a, b):
    return lax.dot_general(a, b, (((1,), (1,)), ((), ())), preferred_element_type=F32)


def tn(a, b):
    return lax.dot_general(a, b, (((0,), (0,)), ((), ())), preferred_element_type=F32)


def ranges(lengths):
    at, out = 0, []
    for n in lengths:
        out.append((at, n))
        at += n
    return out


class Place:
    def __init__(self):
        self.z = lax.axis_index("dp")
        f = lax.axis_index("fsdp")
        self.y = f // 8
        self.x = (f // 2) % 4
        self.c = f % 2

    def dev(self, dz=0, dy=0, dx=0, dc=0):
        z = (self.z + dz) % 4
        y = (self.y + dy) % 4
        x = (self.x + dx) % 4
        c = (self.c + dc) % 2
        return (z, y * 8 + x * 2 + c)

    def along(self, axis, d):
        return self.dev(**{"d" + axis: d})

    def pos(self, axis):
        return getattr(self, axis)


class Ring:
    def __init__(self, me, axis, view, sems, many):
        self.me, self.axis, self.view, self.sems, self.many = me, axis, view, sems, many
        self.p = me.pos(axis)

    def _copy(self, to, src, dst, sem):
        return pltpu.make_async_remote_copy(
            src_ref=src,
            dst_ref=dst,
            send_sem=self.sems.at[0],
            recv_sem=self.sems.at[sem],
            device_id=self.me.along(self.axis, to),
            device_id_type=MESH,
        )

    def _await(self, ref, sem):
        pltpu.make_async_copy(ref, ref, self.sems.at[sem]).wait()

    def sent(self):
        self._await(self.many(3), 0)


class Gather(Ring):
    def _pass(self, to, k, h, sem):
        block = self.view(k % 4, h)
        self._copy(to, block, block, sem).start()

    def start(self):
        p = self.p
        self._pass(1, p, 0, 1)
        self._pass(-1, p, 1, 2)
        self._pass(1, p, 1, 3)
        self._pass(-1, p, 0, 3)

    def forward(self):
        p = self.p
        self._await(self.view((p + 3) % 4, 0), 1)
        self._pass(1, p + 3, 0, 4)
        self._await(self.view((p + 1) % 4, 1), 2)
        self._pass(-1, p + 1, 1, 4)

    def near(self):
        self._await(self.many(1), 3)

    def far(self):
        self._await(self.many(1), 4)

    def finish(self):
        self.near()
        self.far()
        self.sent()


class Scatter(Ring):
    def __init__(self, me, axis, view, sems, many, buf, leads, rows):
        super().__init__(me, axis, view, sems, many)
        self.buf, self.leads, self.rows = buf, leads, rows

    def _slot(self, j, h):
        ref = self.buf.at[j]
        n = self.rows[h]
        if n != ref.shape[-2]:
            ref = ref.at[tuple(slice(None) for _ in self.leads) + (pl.ds(0, n),)]
        return ref

    def _pass(self, to, k, h, slot, sem):
        self._copy(to, self.view(k % 4, h), self._slot(slot, h), sem).start()

    def _add(self, k, h, slots):
        target = self.view(k, h)
        srcs = [self._slot(s, h) for s in slots]

        def one(idx):
            total = target[idx].astype(F32)
            for s in srcs:
                total = total + s[idx].astype(F32)
            target[idx] = total.astype(BF16)

        if not self.leads:
            one((slice(None), slice(None)))
        else:

            @pl.loop(0, self.leads[0])
            def _(i):
                one((i,))

    def start_far(self):
        p = self.p
        self._pass(1, p + 2, 0, 0, 1)
        self._pass(-1, p + 2, 1, 1, 2)

    def start_near(self):
        p = self.p
        self._pass(1, p + 1, 1, 3, 3)
        self._pass(-1, p + 3, 0, 4, 3)

    def start(self):
        self.start_far()
        self.start_near()

    def forward(self):
        p = self.p
        self._await(self._slot(0, 0), 1)
        self._add((p + 1) % 4, 0, [0])
        self._pass(1, p + 1, 0, 2, 3)
        self._await(self._slot(1, 1), 2)
        self._add((p + 3) % 4, 1, [1])
        self._pass(-1, p + 3, 1, 5, 3)

    def finish(self):
        self._await(self.many(2), 3)
        self._add(self.p, 0, [2, 4])
        self._add(self.p, 1, [3, 5])
        self.sent()


class Direct(Ring):
    def __init__(self, me, axis, view, sems, many, buf):
        super().__init__(me, axis, view, sems, many)
        self.buf = buf

    def start(self):
        for j, to in enumerate((2, 1, -1)):
            self._copy(to, self.view((self.p + to) % 4), self.buf.at[j], 1).start()

    def finish(self):
        self._await(self.many(3), 1)
        target = self.view(self.p)
        total = target[...].astype(F32)
        for j in range(3):
            total = total + self.buf[j].astype(F32)
        target[...] = total.astype(BF16)
        self.sent()


def kernel(
    xin, seg, cot, w_gain, w_nbias, w_q, w_qb, w_kv, w_o, w_ob, w_up, w_ub, w_down, w_db, h_qod, h_kv, h_up, h_perm, h_s48, h_s96, h_sums, h_sums_kv, h_upT,
    out_y, out_gx, out_v, out_u,
    W, chunk, rawu, got, gotu, vecs, ubv,
    X2, gl, seg2, cosT, sinT, mbias, n_, r_, h1, attn, mlp, kvT, k_, v_, qT, p_, mixT, mixed, act, slope,
    acc, glT, attnT, gm, gmT, dk, dv, gs, vg, ubg, g_, xs, xr,
    bA2, bB2, bO2, bU2, bD1, bD2, bA3, bB3, bO3, bU3, bD3, back, rgot, rgotu,
    c_qod, c_kv, c_up, c_perm, c_s48, c_s96, c_sums, c_sums_kv, c_upT,
    const_sem, pair_send, pair_recv, line_sem, ag_sem, rs_sem,
):
    me = Place()
    z, y, x, c = me.z, me.y, me.x, me.c
    s_me = x * 2 + c

    consts = [(h_perm, c_perm), (h_qod, c_qod), (h_kv, c_kv), (h_up, c_up), (h_s48, c_s48), (h_s96, c_s96),
              (h_sums, c_sums), (h_sums_kv, c_sums_kv), (h_upT, c_upT)]
    const_copies = [pltpu.make_async_copy(h, v, const_sem.at[i]) for i, (h, v) in enumerate(consts)]
    for cp in const_copies:
        cp.start()

    bar = pltpu.get_barrier_semaphore()
    line = [(dx, dc) for dx in range(4) for dc in range(2) if (dx, dc) != (0, 0)]
    partners = [me.dev(dx=dx, dc=dc) for dx, dc in line]
    partners += [me.dev(dy=d) for d in (1, 2, 3)] + [me.dev(dz=d) for d in (1, 2, 3)]
    for d in partners:
        pl.semaphore_signal(bar, inc=1, device_id=d, device_id_type=MESH)
    sibling = me.dev(dc=1)

    def to_sibling(i, src, dst):
        return pltpu.make_async_remote_copy(
            src_ref=src, dst_ref=dst, send_sem=pair_send.at[i], recv_sem=pair_recv.at[i],
            device_id=sibling, device_id_type=MESH)

    def lane_place():
        r = lax.broadcasted_iota(jnp.int32, (128, HALF), 0)
        m = lax.broadcasted_iota(jnp.int32, (128, HALF), 1)
        small = (r < 6) & (m == r + 6 * s_me)
        wide = (r >= 8) & (r < 32) & (m == r - 8 + 128 + 24 * x)
        return jnp.where(small | wide, 1.0, 0.0).astype(BF16)

    def line_copies(l, bufs, into, bufu, intou, sems):
        out = []
        for dx, dc in line:
            t = (c + dc) % 2
            s_to = ((x + dx) % 4) * 2 + t
            out.append(pltpu.make_async_remote_copy(
                src_ref=bufs(s_to, t), dst_ref=into.at[l, s_me], send_sem=sems.at[0], recv_sem=sems.at[1],
                device_id=me.dev(dx=dx, dc=dc), device_id_type=MESH))
        for dx in range(1, 4):
            out.append(pltpu.make_async_remote_copy(
                src_ref=bufu((x + dx) % 4), dst_ref=intou.at[l, x], send_sem=sems.at[2],
                recv_sem=sems.at[3], device_id=me.dev(dx=dx), device_id_type=MESH))
        for cp in out:
            cp.start()

    def line_wait(sems, rows=CHUNK):
        seven, three = W.at[0, 0, 0, pl.ds(0, 7 * rows)], W.at[0, 0, 0, pl.ds(0, 144)]
        for i, ref in enumerate((seven, seven, three, three)):
            pltpu.make_async_copy(ref, ref, sems.at[i]).wait()

    h1[0:2 * CHUNK, :] = jnp.zeros((2 * CHUNK, D), F32)
    for l in range(2):
        h1[7 * l:7 * l + 2, 0:6] = w_gain[l].astype(F32)
        h1[7 * l + 2:7 * l + 4, 0:6] = w_nbias[l].astype(F32)
        for k, ref in ((4, w_qb), (5, w_ob), (6, w_db)):
            h1[7 * l + k:7 * l + k + 1, 0:6] = ref[...].astype(F32)[l:l + 1]
    h1[0:2, 8:32] = w_ub[...].astype(F32)
    h1[16:22, 0:128] = w_kv[...].astype(F32)
    for i in range(6):
        q2, o2, d2 = w_q[i].astype(F32), w_o[i].astype(F32), w_down[i].astype(F32)
        for l in range(2):
            at = CHUNK * l
            h1[at + 22 + i:at + 23 + i, :] = q2[l:l + 1]
            h1[at + 28 + i:at + 29 + i, :] = o2[l:l + 1]
            for g in range(4):
                h1[at + 34 + 4 * i + g:at + 35 + 4 * i + g, :] = d2[l:l + 1, g * D:(g + 1) * D]
    for l in range(2):
        u = w_up[l].astype(F32)
        rawu[l] = jnp.concatenate([u[:, 0:HALF], u[:, HALF:]], axis=0).astype(BF16)

    const_copies[0].wait()
    place = lane_place()

    def prepare(l):
        vf = h1[CHUNK * l:CHUNK * l + CHUNK, :]
        v = vf.astype(BF16)
        vp = nn(v, c_perm[...]).astype(BF16).astype(F32)
        row = lax.broadcasted_iota(jnp.int32, (CHUNK, HALF), 0)
        lane = lax.broadcasted_iota(jnp.int32, (CHUNK, HALF), 1)
        if l == 0:
            head = jnp.where(row < 16, nn(v[:, 0:128], place), jnp.where(lane < 128, vf[:, 0:HALF], 0.0))
        for t in range(2):
            part = jnp.where(row < 34, vf[:, t * HALF:(t + 1) * HALF], vp[:, t * HALF:(t + 1) * HALF])
            if l == 0:
                ours = jnp.where((lane < 128) | (c == t), head, 0.0)
                part = jnp.where(row < 22, ours, part)
            chunk[l, t] = part.astype(BF16)

    def send_chunks(l):
        line_copies(l, lambda s, t: chunk.at[l, t], got, lambda xx: rawu.at[l], gotu, line_sem.at[l])
        got[l, s_me] = chunk[l, c]
        gotu[l, x] = rawu[l]

    prepare(0)
    seg2[c] = jnp.broadcast_to(seg[...], (8, TOK))
    own = pl.ds(pl.multiple_of(c * TOK, TOK), TOK)

    pl.semaphore_wait(bar, len(partners))

    def to_sibling(i, src, dst):
        return pltpu.make_async_remote_copy(
            src_ref=src, dst_ref=dst, send_sem=pair_send.at[i], recv_sem=pair_recv.at[i],
            device_id=sibling, device_id_type=MESH)

    send_chunks(0)
    seg_copy = to_sibling(0, seg2.at[c], seg2.at[c])
    seg_copy.start()
    x_copy = to_sibling(1, xin, X2.at[c])
    x_copy.start()
    c_copy = to_sibling(2, cot, gl.at[own])
    c_copy.start()
    X2[c] = xin[...]
    gl[own, :] = cot[...]
    prepare(1)
    send_chunks(1)

    half_width = HD // 8
    frequency = np.float32(rotary_base) ** (-(np.arange(half_width, dtype=np.float32) * 2.0) / (2 * half_width))
    row = lax.broadcasted_iota(jnp.int32, (half_width, TOK), 0)
    freq = jnp.zeros((half_width, TOK), F32)
    for f in range(half_width):
        freq = jnp.where(row == f, float(frequency[f]), freq)
    seg_copy.wait()
    for b in range(2):
        docs = seg2[b].astype(F32)
        over_lanes = jnp.broadcast_to(docs[0:1], (TOK, TOK))
        over_rows = over_lanes.T
        earlier = jnp.sum(jnp.where(over_rows < over_lanes, 1.0, 0.0), axis=0, keepdims=True)
        place = lax.broadcasted_iota(jnp.int32, (1, TOK), 1).astype(F32) - earlier
        angle = jnp.broadcast_to(place, (8, TOK)) * freq
        cosT[:, b * TOK:(b + 1) * TOK] = jnp.cos(angle)
        sinT[:, b * TOK:(b + 1) * TOK] = jnp.sin(angle)
        kk = lax.broadcasted_iota(jnp.int32, (TOK, TOK), 0)
        qq = lax.broadcasted_iota(jnp.int32, (TOK, TOK), 1)
        mbias[b] = jnp.where((over_rows == over_lanes) & (kk <= qq), 0.0, masked_score)
    x_copy.wait()
    c_copy.wait()

    CH = 64

    def norm_of(h):
        centred = h - jnp.mean(h, axis=-1, keepdims=True)
        inverse = lax.rsqrt(jnp.mean(centred * centred, axis=-1, keepdims=True) + norm_epsilon)
        return centred * inverse, inverse

    def normalise(i, h):
        rows = pl.ds(pl.multiple_of(i * CH, CH), CH)
        n, inverse = norm_of(h)
        n_[rows, :] = n
        r_[rows, :] = jnp.broadcast_to(inverse, (CH, 128))

    def input_rows(i):
        return X2[i // 4, pl.ds(pl.multiple_of((i % 4) * CH, CH), CH), :].astype(F32)

    @pl.loop(0, 8)
    def _(i):
        normalise(i, input_rows(i))

    glT[...] = gl[...].T
    for cp in const_copies[1:]:
        cp.wait()

    def quarter(k):
        return pl.multiple_of(D0 + 48 * k, 16)

    def assemble(l):
        line_wait(line_sem.at[l])
        stack = got[l].reshape(512, HALF)
        W[l, z, y, Q0:D0, :] = nn(c_qod[0:96, :], stack).astype(BF16)
        down = nn(c_qod[pl.ds(pl.multiple_of(96 + 48 * x, 16), 48), :], stack).astype(BF16)
        W[l, z, y, pl.ds(quarter(x), 48), :] = down
        if l == 0:
            kv = nn(c_kv[...], stack[:, 0:128]).astype(BF16)
            W[0, z, y, KV0:KV0 + 16, :] = jnp.concatenate([kv[0:16], kv[16:32], kv[32:48]], axis=1)
            vec = got[0, 0, 0:16, :].astype(F32)
            for s in range(1, 8):
                vec = vec + got[0, s, 0:16, :].astype(F32)
            W[0, z, y, VEC0:VEC0 + 16, :] = vec.astype(BF16)
        W[l, z, y, U0:ROWS, :] = nn(c_up[...], gotu[l].reshape(192, HALF)).astype(BF16)

    def many(n, wide):
        if wide:
            return lambda count: W.at[0, pl.ds(0, count), :, pl.ds(0, n), :]
        return lambda count: W.at[0, 0, pl.ds(0, count), pl.ds(0, n), :]

    def cut(row0, n, h):
        first = halves(n)[0]
        return pl.ds(row0 if h == 0 else pl.multiple_of(row0 + first, 16), first if h == 0 else n - first)

    def halves(n):
        first = (n + 31) // 32 * 16
        return (first, n - first)

    def gathers(l):
        g = {}

        def y_then_z(i, name, row0, n):
            g[name + "2"] = Gather(me, "y", lambda k, h: W.at[l, z, k, cut(row0, n, h), :], ag_sem.at[l, i], many(n, False))
            g[name + "3"] = Gather(me, "z", lambda k, h: W.at[l, k, pl.ds(2 * h, 2), pl.ds(row0, n), :], ag_sem.at[l, i + 1],
                                   many(n, True))

        def z_then_y(i, name, row0, n):
            g[name + "2"] = Gather(me, "z", lambda k, h: W.at[l, k, y, cut(row0, n, h), :], ag_sem.at[l, i], many(n, False))
            g[name + "3"] = Gather(me, "y", lambda k, h: W.at[l, pl.ds(2 * h, 2), k, pl.ds(row0, n), :], ag_sem.at[l, i + 1],
                                   many(n, True))

        e0 = 0 if l == 0 else Q0
        en = (D0 - e0) // 2
        y_then_z(0, "E", e0, en)
        z_then_y(2, "F", e0 + en, en)
        z_then_y(4, "D", quarter(x), 48)
        y_then_z(6, "U", U0, 112)
        z_then_y(8, "V", U0 + 112, 80)
        for i, dy in enumerate((0, 1, 3, 2)):
            g["D4", i] = Gather(me, "x", lambda k, h, dy=dy: W.at[l, pl.ds(2 * h, 2), (y + dy) % 4, pl.ds(quarter(k), 48), :],
                                ag_sem.at[l, 10 + i], many(48, True))
        return g

    g0, g1 = gathers(0), gathers(1)

    def second_stage(l, g):
        assemble(l)
        for n in "EFDUV":
            g[n + "2"].start()

    def forward_on(r, *names):
        for n in names:
            r[n].forward()

    def third_stage(g, first="EFD", rest="UV"):
        for n in first:
            g[n + "2"].finish()
            g[n + "3"].start()
        g["D4", 0].start()
        for n in rest:
            g[n + "2"].finish()
            g[n + "3"].start()

    def first_quarters(g):
        g["D3"].forward()
        g["D4", 0].forward()
        g["D3"].near()
        g["D4", 1].start()
        g["D4", 2].start()

    def heads_ready(g):
        g["E3"].finish()
        g["F3"].finish()

    def last_quarter(g):
        g["D3"].far()
        g["D4", 3].start()
        g["D4", 1].forward()
        g["D4", 2].forward()

    def hidden_ready(g):
        g["U3"].finish()
        g["V3"].finish()

    def down_ready(g):
        g["D3"].sent()
        for i in range(4):
            g["D4", i].finish()

    second_stage(0, g0)
    forward_on(g0, "E2", "F2", "D2", "U2", "V2")
    third_stage(g0, rest="")
    g0["U2"].finish()
    g0["V2"].finish()
    forward_on(g0, "E3", "F3")
    g0["U3"].start()
    g0["V3"].start()
    second_stage(1, g1)
    heads_ready(g0)

    tile = W[0, :, :, VEC0:VEC0 + 16, :].reshape(256, HALF)
    wide = nn(tile[:, 0:128], c_s48[...])
    at = lax.broadcasted_iota(jnp.int32, (16, D), 1)
    total = jnp.zeros((16, D), F32)
    for m in range(16):
        total = total + jnp.where((at >= 48 * m) & (at < 48 * m + 48), wide[16 * m:16 * m + 16], 0.0)
    vecs[...] = total
    wide = nn(tile[:, 128:256], c_s96[...])
    at = lax.broadcasted_iota(jnp.int32, (16, 1536), 1)
    total = jnp.zeros((16, 1536), F32)
    for m in range(16):
        total = total + jnp.where((at >= 96 * m) & (at < 96 * m + 96), wide[16 * m:16 * m + 16], 0.0)
    for l in range(2):
        for k in range(4):
            ubv[l, k] = jnp.broadcast_to(total[l:l + 1, k * HALF:(k + 1) * HALF], (8, HALF))

    def vec(l, k):
        return vecs[7 * l + k:7 * l + k + 1, :]

    def norm_inputs(l, again=False):
        @pl.loop(0, 8)
        def _(i):
            rows = pl.ds(pl.multiple_of(i * CH, CH), CH)
            n = norm_of(input_rows(i))[0] if again else n_[rows, :]
            attn[rows, :] = (n * vec(l, 0) + vec(l, 2)).astype(BF16)
            mlp[rows, :] = (n * vec(l, 1) + vec(l, 3)).astype(BF16)

    def key_weight():
        kvw = W[0, :, :, KV0:KV0 + 16, :]
        return jnp.concatenate([kvw[..., 0:128], kvw[..., 128:256], kvw[..., 256:384]], axis=2).reshape(D, 128)

    def weight(l, row0, n=48):
        return W[l, :, :, pl.ds(row0, n), :].reshape(16 * n, HALF)

    def up_weight(l, k, h):
        return W[l, k, :, U0 + 96 * h:U0 + 96 * h + 96, :].reshape(HALF, HALF)

    def down_weight(l, k):
        return weight(l, pl.multiple_of(D0 + 48 * k, 16))

    def rotate_heads(v, heads):
        v = v.reshape(heads, HD, 512)
        cs, sn = cosT[...][None], sinT[...][None]
        u1, u2 = v[:, 0:8, :], v[:, 8:16, :]
        return jnp.concatenate([u1 * cs - u2 * sn, u2 * cs + u1 * sn, v[:, 16:, :]], axis=1).reshape(heads * HD, 512)

    def rotate_heads_back(v, heads):
        v = v.reshape(heads, HD, 512)
        cs, sn = cosT[...][None], sinT[...][None]
        u1, u2 = v[:, 0:8, :], v[:, 8:16, :]
        return jnp.concatenate([u1 * cs + u2 * sn, u2 * cs - u1 * sn, v[:, 16:, :]], axis=1).reshape(heads * HD, 512)

    def far_first(p, i):
        return (p + jnp.where(i == 0, 2, jnp.where(i == 1, 1, jnp.where(i == 2, 3, 0)))) % 4

    def serve(i, points):
        for at, step in points.items():
            pl.when(i == at)(step)

    def steps(*todo):
        def run():
            for step, *args in todo:
                step(*args)

        return run

    def down_block(l, rows):
        acc[rows, :] = nt(mixed[l, rows, :], weight(l, O0))
        for k in range(4):
            acc[rows, :] += nt(act[l, k, rows, :], down_weight(l, k))

    def forward(l, in_heads, before_ffn, in_ffn, after_hidden):
        norm_inputs(l)
        if l == 0:
            kv = nn(attn[...], key_weight()).T
            keys = rotate_heads(kv[0:HD], 1)
            kvT[0:HD, :] = keys.astype(BF16)
            kvT[HD:, :] = kv[HD:].astype(BF16)
            k_[...] = keys.T.astype(BF16)
            v_[...] = kv[HD:].T.astype(BF16)
        qb = vec(l, 4)
        qb = jnp.where(c == 0, qb[:, 0:HALF], qb[:, HALF:])
        q = nn(attn[...], weight(l, Q0)) + qb
        qT[l] = rotate_heads(q.T, 6).astype(BF16)

        @pl.loop(0, 3)
        def _(pair):
          serve(2 * pair, in_heads)
          serve(2 * pair + 1, in_heads)
          for h in (2 * pair, 2 * pair + 1):
            hs = pl.ds(pl.multiple_of(h * HD, HD), HD)
            for b in range(2):
                bs = slice(b * TOK, (b + 1) * TOK)
                s = nn(k_[bs, :], qT[l, hs, bs]) * scale + mbias[b]
                e = jnp.exp(s - jnp.max(s, axis=0, keepdims=True))
                low = (e * (1.0 / jnp.sum(e, axis=0, keepdims=True))).astype(BF16)
                p_[l, h, b] = low
                mixT[hs, bs] = nn(kvT[HD:, bs], low).astype(BF16)

        mixed[l] = mixT[...].T
        before_ffn()

        @pl.loop(0, 4)
        def _(i):
            k = far_first(x, i) if l == 1 else i
            serve(i, in_ffn)
            for b in range(2):
                rows = slice(b * TOK, (b + 1) * TOK)
                hid = nt(mlp[rows, 0:HALF], up_weight(l, k, 0)) + nt(mlp[rows, HALF:], up_weight(l, k, 1))
                hid = hid + ubv[l, k, 0:1, :]
                phi = 0.5 * (1.0 + lax.erf(hid * root_half))
                low = (hid * phi).astype(BF16)
                act[l, k, rows, :] = low
                slope[l, k, rows, :] = (phi + hid * jnp.exp(-0.5 * hid * hid) * inverse_root_tau).astype(BF16)
            after_hidden(i, k)

    forward(
        0,
        {
            0: steps((first_quarters, g0)),
            2: steps((forward_on, g0, "U3", "V3"), (forward_on, g1, "E2", "F2", "D2", "U2", "V2")),
            3: steps((last_quarter, g0)),
            4: steps((third_stage, g1)),
        },
        steps((forward_on, g0, ("D4", 3)), (hidden_ready, g0)),
        {
            1: steps((forward_on, g1, "E3", "F3")),
            2: steps((first_quarters, g1)),
            3: steps((forward_on, g1, "U3", "V3")),
        },
        lambda i, k: None,
    )
    down_ready(g0)
    swap = [to_sibling(3 + b, xs.at[b], xr.at[b]) for b in range(2)]
    for b in range(2):
        down_block(0, slice(b * TOK, (b + 1) * TOK))
        xs[b] = acc[b * TOK:(b + 1) * TOK, :].astype(BF16)
        swap[b].start()
        if b == 0:
            last_quarter(g1)
    heads_ready(g1)
    for cp in swap:
        cp.wait()

    @pl.loop(0, 8)
    def _(i):
        b = i // 4
        rows = pl.ds(pl.multiple_of((i % 4) * CH, CH), CH)
        h = X2[b, rows, :].astype(F32) + (vec(0, 5) + vec(0, 6))
        h = h + (xs[b, rows, :].astype(F32) + xr[b, rows, :].astype(F32))
        normalise(i, h)

        @pl.when(b == c)
        def _():
            h1[rows, :] = h

    def scatters(l):
        gslot = 2 if l == 1 else 1
        g = {}

        def y_then_z(i, name, row0, n, b2, b3):
            g[name + "2"] = Scatter(me, "y", lambda k, h: W.at[gslot, pl.ds(2 * h, 2), k, pl.ds(row0, n), :],
                                    rs_sem.at[l, i], many(n, True), b2.at[l], (2,), (n, n))
            g[name + "3"] = Direct(me, "z", lambda k: W.at[gslot, k, y, pl.ds(row0, n), :], rs_sem.at[l, i + 1],
                                   many(n, False), b3.at[l, :, pl.ds(0, n)])

        for i, dy in enumerate((2, 1, 3, 0)):
            g["D1", i] = Scatter(me, "x", lambda k, h, dy=dy: W.at[gslot, pl.ds(2 * h, 2), (y + dy) % 4, pl.ds(quarter(k), 48), :],
                                 rs_sem.at[l, i], many(48, True), bD1.at[l, i], (2,), (48, 48))
        y_then_z(4, "D", quarter(x), 48, bD2, bD3)
        y_then_z(6, "O", O0, 48, bO2, bO3)
        a0 = 0 if l == 0 else VEC0
        y_then_z(8, "A", a0, 48 - a0, bA2, bA3)
        y_then_z(10, "B", 48, 32, bB2, bB3)
        g["U2"] = Scatter(me, "z", lambda k, h: W.at[gslot, k, pl.ds(2 * h, 2), pl.ds(U0, 192), :], rs_sem.at[l, 12],
                          many(192, True), bU2.at[l], (2,), (192, 192))
        g["U3"] = Scatter(me, "y", lambda k, h: W.at[gslot, z, k, cut(U0, 192, h), :], rs_sem.at[l, 13],
                          many(192, False), bU3.at[l], (), (96, 96))
        return g

    def finish_line(l):
        B = W.at[2 if l == 1 else 1, z, y]
        rows = jnp.concatenate([B[Q0:D0, :], B[pl.ds(quarter(x), 48), :], B[VEC0:VEC0 + 16, :]], axis=0)
        stack = nn(c_sums[...], rows)
        if l == 0:
            kv = B[KV0:KV0 + 16, :]
            kv = jnp.concatenate([kv[:, 0:128], kv[:, 128:256], kv[:, 256:384]], axis=0)
            stack = stack + jnp.concatenate([nn(c_sums_kv[...], kv), jnp.zeros((256, 256), F32)], axis=1)
        back[l] = stack.astype(BF16).reshape(8, 32, HALF)
        gotu[l] = nn(c_upT[...], B[U0:ROWS, :]).astype(BF16).reshape(4, 48, HALF)
        line_copies(l, lambda s, t: back.at[l, s], rgot, lambda xx: gotu.at[l, xx], rgotu, line_sem.at[2 + l])
        rgot[l, s_me] = back[l, s_me]
        rgotu[l, x] = gotu[l, x]

    def last_sums(l):
        line_wait(line_sem.at[2 + l], 32)
        halves, tiles = [], []
        for t in range(2):
            parts = [rgot[l, 2 * xx + t].astype(F32) for xx in range(4)]
            halves.append(parts[0] + parts[1] + parts[2] + parts[3])
        for xx in range(4):
            tiles.append(jnp.concatenate([rgot[l, 2 * xx, 0:32, :], rgot[l, 2 * xx + 1, 0:32, :]], axis=1))
        unperm = nt(jnp.concatenate(tiles, axis=0), c_perm[...])
        row = lax.broadcasted_iota(jnp.int32, (32, HALF), 0)
        lane = lax.broadcasted_iota(jnp.int32, (32, HALF), 1)
        both = halves[0] + halves[1]
        mine = jnp.where(lane < 128, both, jnp.where(c == 0, halves[0], halves[1]))
        hi = mine.astype(BF16)
        lo = (mine - hi.astype(F32)).astype(BF16)
        spot = lane_place()
        small = nt(hi, spot) + nt(lo, spot)
        out_v[l, 0:32, 0:HALF] = jnp.where(row < 18, halves[0], both)
        out_v[l, 0:32, HALF:] = halves[1]
        out_v[l, 24:32, 0:128] = small[24:32]
        for xx in range(4):
            out_v[l, 32 + 16 * xx:48 + 16 * xx, :] = unperm[32 * xx + 8:32 * xx + 24]
        u = rgotu[l, 0].astype(F32)
        for xx in range(1, 4):
            u = u + rgotu[l, xx].astype(F32)
        out_u[l] = u

    r1, r0 = scatters(1), scatters(0)

    def first_sums(r):
        for i in range(4):
            r["D1", i].start()
        r["O2"].start()

    def next_ring(r, *names):
        for n in names:
            r[n + "2"].finish()
            r[n + "3"].start()

    def down_second(r):
        r["D1", 0].finish()
        r["D2"].start_far()
        r["D1", 1].finish()
        r["D1", 2].finish()
        r["D2"].start_near()
        r["D1", 3].finish()

    def finish_third(r, names):
        for n in names:
            r[n].finish()

    def out_grad(l):
        for b in range(2):
            rows = slice(b * HALF, (b + 1) * HALF)
            part = nn(glT[rows, :], mixed[l]).astype(BF16).reshape(2, 4, 48, HALF)
            W[2 if l == 1 else 1, 2 * b:2 * b + 2, :, O0:O0 + 48, :] = part

    def down_grad(l, r, i, k):
        rows_d = pl.ds(pl.multiple_of(D0 + 48 * k, 16), 48)
        for b in range(2):
            rows = slice(b * HALF, (b + 1) * HALF)
            part = nn(glT[rows, :], act[l, k]).astype(BF16).reshape(2, 4, 48, HALF)
            W[2 if l == 1 else 1, 2 * b:2 * b + 2, :, rows_d, :] = part
        rings = [r["D1", j] for j in range(4)]
        serve(i, {0: steps(*((ring.start_far,) for ring in rings)), 2: steps(*((ring.start_near,) for ring in rings))})

    def backward(l, r, in_ffn, before_heads, in_heads, before_query):
        G = W.at[2 if l == 1 else 1]
        vg[5:6, :] = jnp.sum(gl[own, :].astype(F32), axis=0, keepdims=True)
        acc[...] = jnp.zeros_like(acc)

        @pl.loop(0, 4)
        def _(i):
            k = far_first(z, i)
            serve(i, in_ffn)
            sums = jnp.zeros((1, HALF), F32)
            for b in range(2):
                rows = slice(b * TOK, (b + 1) * TOK)
                gh = nn(gl[rows, :], down_weight(l, k)) * slope[l, k, rows, :].astype(F32)
                gh = gh.astype(BF16)
                slope[l, k, rows, :] = gh
                sums = sums + jnp.sum(gh.astype(F32), axis=0, keepdims=True)
                for h in range(2):
                    acc[rows, h * HALF:(h + 1) * HALF] += nn(gh, up_weight(l, k, h))
            ubg[k] = jnp.broadcast_to(sums, (8, HALF))
            ghT = slope[l, k].T
            for h in range(2):
                part = nn(ghT, mlp[:, h * HALF:(h + 1) * HALF]).astype(BF16).reshape(4, 96, HALF)
                G[k, :, U0 + 96 * h:U0 + 96 * h + 96, :] = part
            serve(i, {0: r["U2"].start_far, 2: r["U2"].start_near})

        before_heads()

        for b in range(2):
            rows = slice(b * TOK, (b + 1) * TOK)
            gm[rows, :] = nn(gl[rows, :], weight(l, O0)).astype(BF16)
        gmT[...] = gm[...].T

        if l == 1:
            dk[...] = jnp.zeros_like(dk)
            dv[...] = jnp.zeros_like(dv)

        @pl.loop(0, 3)
        def _(pair):
          serve(2 * pair, in_heads)
          serve(2 * pair + 1, in_heads)
          for h in (2 * pair, 2 * pair + 1):
            hs = pl.ds(pl.multiple_of(h * HD, HD), HD)
            for b in range(2):
                bs = slice(b * TOK, (b + 1) * TOK)
                low = p_[l, h, b]
                probs = low.astype(F32)
                t = probs * nn(v_[bs, :], gmT[hs, bs])
                grad = (t - probs * jnp.sum(t, axis=0, keepdims=True)).astype(BF16)
                dq = nn(kvT[0:HD, bs], grad) * scale
                cs, sn = cosT[:, bs], sinT[:, bs]
                u1, u2 = dq[0:8], dq[8:16]
                dq = jnp.concatenate([u1 * cs + u2 * sn, u2 * cs - u1 * sn, dq[16:]], axis=0)
                mixT[hs, bs] = dq.astype(BF16)
                dk[bs, :] += nt(grad, qT[l, hs, bs])
                dv[bs, :] += nt(low, gmT[hs, bs])

        before_query()
        low = mixT[...].T
        gm[...] = low
        qsum = jnp.sum(low.astype(F32), axis=0, keepdims=True)
        zero = jnp.zeros_like(qsum)
        vg[4:5, :] = jnp.concatenate([jnp.where(c == 0, qsum, zero), jnp.where(c == 0, zero, qsum)], axis=1)
        if l == 0:
            keys = rotate_heads_back((dk[...] * scale).T, 1).T
            gs[...] = jnp.concatenate([keys, dv[...]], axis=1).astype(BF16)

    def query_grad(l, r):
        G = W.at[2 if l == 1 else 1]
        for b in range(2):
            rows = slice(b * HALF, (b + 1) * HALF)
            part = nn(attnT[rows, :], gm[...]).astype(BF16).reshape(2, 4, 48, HALF)
            G[2 * b:2 * b + 2, :, Q0:Q0 + 48, :] = part
        r["B2"].start()
        if l == 0:
            dkv = nn(attnT[...], gs[...]).astype(BF16).reshape(4, 4, 48, 128)
            G[:, :, KV0:KV0 + 16, :] = jnp.concatenate([dkv[:, :, 0:16], dkv[:, :, 16:32], dkv[:, :, 32:48]], axis=3)

    def fold_block(l, b, sums):
        hold = g_ if l == 1 else h1
        rows = slice(b * TOK, (b + 1) * TOK)
        ea = nt(gm[rows, :], weight(l, Q0))
        if l == 0:
            ea = ea + nt(gs[rows, :], key_weight())
        hold[...] = ea

        def fold(i, sums):
            rows = pl.ds(pl.multiple_of(i * CH, CH), CH)
            all_rows = pl.ds(pl.multiple_of(b * TOK + i * CH, CH), CH)
            n = n_[all_rows, :] if l == 1 else norm_of(X2[b, rows, :].astype(F32))[0]
            ea, em = hold[rows, :], acc[all_rows, :]
            xs[b, rows, :] = (ea * vec(l, 0) + em * vec(l, 1)).astype(BF16)
            add = [ea * n, em * n, ea, em]
            return tuple(s + jnp.sum(a, axis=0, keepdims=True) for s, a in zip(sums, add))

        return lax.fori_loop(0, 4, fold, sums)

    def vector_grad(l, r, sums):
        G = W.at[2 if l == 1 else 1]
        for k in range(4):
            vg[k:k + 1, :] = sums[k]
        at = lax.broadcasted_iota(jnp.int32, (16, D), 1)
        rowk = lax.broadcasted_iota(jnp.int32, (16, D), 0)
        vv = jnp.where(rowk < 6, vg[...], 0.0)
        parts = [jnp.where((at >= 48 * m) & (at < 48 * m + 48), vv, 0.0).astype(BF16) for m in range(16)]
        small = nt(jnp.concatenate(parts, axis=0), c_s48[...]).astype(BF16)
        ub = jnp.concatenate([ubg[k][0:1, :] for k in range(4)], axis=1)
        at = lax.broadcasted_iota(jnp.int32, (16, 1536), 1)
        rowk = lax.broadcasted_iota(jnp.int32, (16, 1536), 0)
        ub = jnp.where(rowk == 6, jnp.broadcast_to(ub, (16, 1536)), 0.0)
        parts = [jnp.where((at >= 96 * m) & (at < 96 * m + 96), ub, 0.0).astype(BF16) for m in range(16)]
        wide = nt(jnp.concatenate(parts, axis=0), c_s96[...]).astype(BF16)
        both = jnp.concatenate([small, wide, jnp.zeros((256, 128), BF16)], axis=1)
        G[:, :, VEC0:VEC0 + 16, :] = both.reshape(4, 4, 16, HALF)
        r["A2"].start()

    def through_norm(n, inverse, g, s):
        m1 = jnp.mean(s, axis=-1, keepdims=True)
        m2 = jnp.mean(s * n, axis=-1, keepdims=True)
        return g + inverse * (s - m1 - n * m2)

    no_sums = (jnp.zeros((1, D), F32),) * 4

    forward(
        1,
        {1: steps((g1["D4", 3].forward,))},
        steps((out_grad, 1), (r1["O2"].start,), (hidden_ready, g1)),
        {},
        lambda i, k: down_grad(1, r1, i, k),
    )
    attnT[...] = attn[...].T
    down_ready(g1)
    backward(
        1, r1,
        {1: steps((forward_on, r1, "O2")), 3: steps((forward_on, r1, ("D1", 0)))},
        steps((forward_on, r1, ("D1", 1)), (next_ring, r1, "O")),
        {2: steps((forward_on, r1, ("D1", 2))), 4: steps((forward_on, r1, ("D1", 3)))},
        steps((forward_on, r1, "U2")),
    )
    swap = [to_sibling(6 + b, xs.at[b], xr.at[2 + b]) for b in range(2)]
    sums = no_sums
    for b in range(2):
        sums = fold_block(1, b, sums)
        swap[b].start()
    query_grad(1, r1)
    vector_grad(1, r1, sums)
    other = pl.ds(pl.multiple_of((1 - c) * TOK, TOK), TOK)
    down_block(1, other)
    xs[2] = acc[other, :].astype(BF16)
    y_copy = to_sibling(5, xs.at[2], xr.at[0])
    down_block(1, own)
    for cp in swap:
        cp.wait()
    y_copy.start()

    @pl.loop(0, 8)
    def _(i):
        b = i // 4
        rows = pl.ds(pl.multiple_of((i % 4) * CH, CH), CH)
        s = xs[b, rows, :].astype(F32) + xr[2 + b, rows, :].astype(F32)
        all_rows = pl.ds(pl.multiple_of(i * CH, CH), CH)
        g = through_norm(n_[all_rows, :], r_[all_rows, 0:1], gl[all_rows, :].astype(F32), s)
        gl[all_rows, :] = g.astype(BF16)

        @pl.when(b == c)
        def _():
            g_[rows, :] = g

    down_second(r1)
    forward_on(r1, "A2", "B2")
    glT[...] = gl[...].T

    @pl.loop(0, 4)
    def _(i):
        down_grad(0, r0, i, far_first(x, i))

    out_grad(0)
    r0["O2"].start()
    norm_inputs(0, again=True)
    attnT[...] = attn[...].T
    y_copy.wait()
    out_y[...] = (h1[...] + (vec(1, 5) + vec(1, 6)) + acc[own, :] + xr[0].astype(F32)).astype(BF16)
    backward(
        0, r0,
        {
            1: steps((forward_on, r0, "O2")),
            2: steps((next_ring, r1, "U"), (forward_on, r1, "D2")),
            3: steps((next_ring, r1, "A", "B"), (forward_on, r0, ("D1", 0))),
        },
        steps((forward_on, r0, ("D1", 1))),
        {
            0: steps((next_ring, r0, "O")),
            1: steps((forward_on, r0, ("D1", 2))),
            2: steps((next_ring, r1, "D"), (forward_on, r1, "U3")),
            3: steps((forward_on, r0, "U2", ("D1", 3))),
        },
        steps(),
    )
    query_grad(0, r0)
    sums = no_sums
    for b in range(2):
        sums = fold_block(0, b, sums)
    swap = to_sibling(8, xs.at[1 - c], xr.at[1])
    swap.start()
    r0["D1", 0].finish()
    r0["D2"].start_far()
    vector_grad(0, r0, sums)
    r0["D1", 1].finish()
    r0["D1", 2].finish()
    r0["D2"].start_near()
    r0["D1", 3].finish()
    forward_on(r0, "B2")
    next_ring(r0, "U")
    finish_third(r1, ("O3", "A3", "B3", "D3", "U3"))
    finish_line(1)
    forward_on(r0, "A2", "D2")
    next_ring(r0, "B", "A", "D")
    forward_on(r0, "U3")
    swap.wait()

    @pl.loop(0, 4)
    def _(i):
        rows = pl.ds(pl.multiple_of(i * CH, CH), CH)
        s = xs[c, rows, :].astype(F32) + xr[1, rows, :].astype(F32)
        n, inverse = norm_of(X2[c, rows, :].astype(F32))
        out_gx[rows, :] = through_norm(n, inverse, g_[rows, :], s).astype(BF16)

    last_sums(1)
    finish_third(r0, ("O3", "U3", "B3", "A3", "D3"))
    finish_line(0)
    last_sums(0)


def vmem(*shape, dtype=BF16):
    return pltpu.VMEM(shape, dtype)


def make_call():
    T2 = 2 * TOK
    scratch = [
        vmem(3, 4, 4, ROWS, HALF), vmem(2, 2, CHUNK, HALF), vmem(2, 48, HALF), vmem(2, 8, CHUNK, HALF), vmem(2, 4, 48, HALF),
        vmem(16, D, dtype=F32), vmem(2, 4, 8, HALF, dtype=F32),
        vmem(2, TOK, D), vmem(T2, D), vmem(2, 8, TOK, dtype=jnp.int32), vmem(8, T2, dtype=F32), vmem(8, T2, dtype=F32),
        vmem(2, TOK, TOK, dtype=F32), vmem(T2, D, dtype=F32), vmem(T2, 128, dtype=F32), vmem(TOK, D, dtype=F32),
        vmem(T2, D), vmem(T2, D), vmem(128, T2), vmem(T2, HD), vmem(T2, HD), vmem(2, HALF, T2), vmem(2, 6, 2, TOK, TOK),
        vmem(HALF, T2), vmem(2, T2, HALF), vmem(2, 4, T2, HALF), vmem(2, 4, T2, HALF),
        vmem(T2, D, dtype=F32), vmem(D, T2), vmem(D, T2), vmem(T2, HALF), vmem(HALF, T2),
        vmem(T2, HD, dtype=F32), vmem(T2, HD, dtype=F32), vmem(T2, 128), vmem(16, D, dtype=F32),
        vmem(4, 8, HALF, dtype=F32), vmem(TOK, D, dtype=F32), vmem(3, TOK, D), vmem(4, TOK, D),
        vmem(2, 6, 2, 48, HALF), vmem(2, 6, 2, 32, HALF), vmem(2, 6, 2, 48, HALF), vmem(2, 6, 2, 192, HALF),
        vmem(2, 4, 6, 2, 48, HALF), vmem(2, 6, 2, 48, HALF),
        vmem(2, 3, 48, HALF), vmem(2, 3, 32, HALF), vmem(2, 3, 48, HALF), vmem(2, 6, 96, HALF), vmem(2, 3, 48, HALF),
        vmem(2, 8, 32, HALF), vmem(2, 8, 32, HALF), vmem(2, 4, 48, HALF),
        *[vmem(*v.shape) for v in (CONSTS[i] for i in range(9))],
        pltpu.SemaphoreType.DMA((9,)), pltpu.SemaphoreType.DMA((9,)), pltpu.SemaphoreType.DMA((9,)),
        pltpu.SemaphoreType.DMA((4, 4)), pltpu.SemaphoreType.DMA((2, 14, 5)), pltpu.SemaphoreType.DMA((2, 14, 4)),
    ]
    whole = pl.BlockSpec(memory_space=pltpu.VMEM)
    return pl.pallas_call(
        kernel,
        out_shape=(
            jax.ShapeDtypeStruct((TOK, D), BF16),
            jax.ShapeDtypeStruct((TOK, D), BF16),
            jax.ShapeDtypeStruct((2, 96, D), F32),
            jax.ShapeDtypeStruct((2, 48, HALF), F32),
        ),
        in_specs=[whole] * 14 + [pl.BlockSpec(memory_space=pl.ANY)] * 9,
        out_specs=(whole,) * 4,
        scratch_shapes=scratch,
        compiler_params=pltpu.CompilerParams(
            collective_id=0, has_side_effects=True, vmem_limit_bytes=64 * 2**20 - 65536
        ),
        name="two_layers",
    )


def pack_kernel(
    y, gx, v, u,
    o_y, o_gx, o_gain, o_nbias, o_q, o_qb, o_kv, o_o, o_ob, o_up, o_ub, o_down, o_db,
):
    o_y[...] = y[...]
    o_gx[...] = gx[...]
    for l in range(2):
        o_gain[l] = v[l, 24:26, 0:6]
        o_nbias[l] = v[l, 26:28, 0:6]
        o_qb[l:l + 1, :] = v[l, 28:29, 0:6]
        o_ob[l:l + 1, :] = v[l, 29:30, 0:6]
        o_db[l:l + 1, :] = v[l, 29:30, 0:6]
        o_ub[l:l + 1, :] = v[l, 30:31, 8:32]
        for h in range(2):
            o_up[l, :, h * HALF:(h + 1) * HALF] = u[l, 24 * h:24 * h + 24, :]
        for i in range(6):
            o_q[i, l:l + 1, :] = v[l, i:i + 1, :]
            o_o[i, l:l + 1, :] = v[l, 6 + i:7 + i, :]
            for g in range(4):
                at = 32 + 16 * g + 4 + i
                o_down[i, l:l + 1, g * D:(g + 1) * D] = v[l, at:at + 1, :]
    o_kv[...] = v[0, 18:24, 0:128]


def pack(y, gx, v, u):
    whole = pl.BlockSpec(memory_space=pltpu.VMEM)
    shapes = [(2, 2, 6), (2, 2, 6), (6, 2, D), (2, 6), (6, 128), (6, 2, D), (2, 6), (2, 24, D), (2, 24), (6, 2, FF), (2, 6)]
    return pl.pallas_call(
        pack_kernel,
        out_shape=tuple(
            [jax.ShapeDtypeStruct((TOK, D), BF16)] * 2 + [jax.ShapeDtypeStruct(shape, F32) for shape in shapes]),
        in_specs=[whole] * 4,
        out_specs=(whole,) * 13,
        name="results",
    )(y, gx, v, u)


def on_device(
    layer_input, segments, norm_gain, norm_bias, query_weight, query_bias, keyval_weight, output_weight,
    output_bias, upward_weight, upward_bias, downward_weight, downward_bias, cotangent,
):
    consts = [jnp.asarray(v, BF16) for v in CONSTS]
    y, gx, gain, nbias, q, qb, kv, o, ob, up, ub, down, db = pack(*make_call()(
        layer_input, segments, cotangent, norm_gain, norm_bias, query_weight.transpose(1, 0, 2), query_bias,
        keyval_weight, output_weight.transpose(2, 0, 1), output_bias, upward_weight.transpose(0, 2, 1), upward_bias,
        downward_weight.transpose(2, 0, 1), downward_bias, *consts))
    return (
        y, gx, gain, nbias, q.transpose(1, 0, 2), qb, kv, o.transpose(1, 2, 0), ob, up.transpose(0, 2, 1), ub,
        down.transpose(1, 2, 0), db,
    )


def solution(mesh):
    in_specs = (
        P(("dp", "fsdp"), None),
        P(("dp", "fsdp"), None),
        P(None, None, ("dp", "fsdp")),
        P(None, None, ("dp", "fsdp")),
        P(None, ("dp", "fsdp"), None),
        P(None, ("dp", "fsdp")),
        P(("dp", "fsdp"), None),
        P(None, None, ("dp", "fsdp")),
        P(None, ("dp", "fsdp")),
        P(None, None, ("dp", "fsdp")),
        P(None, ("dp", "fsdp")),
        P(None, None, ("dp", "fsdp")),
        P(None, ("dp", "fsdp")),
        P(("dp", "fsdp"), None),
    )
    out_specs = (
        P(("dp", "fsdp"), None),
        P(("dp", "fsdp"), None),
        P(None, None, ("dp", "fsdp")),
        P(None, None, ("dp", "fsdp")),
        P(None, ("dp", "fsdp"), None),
        P(None, ("dp", "fsdp")),
        P(("dp", "fsdp"), None),
        P(None, None, ("dp", "fsdp")),
        P(None, ("dp", "fsdp")),
        P(None, None, ("dp", "fsdp")),
        P(None, ("dp", "fsdp")),
        P(None, None, ("dp", "fsdp")),
        P(None, ("dp", "fsdp")),
    )
    return jax.shard_map(on_device, mesh=mesh, in_specs=in_specs, out_specs=out_specs, check_vma=False)
```

```python
import functools

import jax
import jax.numpy as jnp
import numpy as np
from jax import lax
from jax.experimental import pallas as pl
from jax.experimental.pallas import tpu as pltpu
from jax.sharding import PartitionSpec as P

MESH = pl.DeviceIdType.MESH
F32 = jnp.float32
BF16 = jnp.bfloat16

H = 12
HD = 64
D = 768
FF = 3072
TOK = 256
HALF = 384
ROWS = 512
KV0, VEC0, Q0, O0, D0, U0 = 0, 16, 32, 80, 128, 320
CHUNK = 64

norm_epsilon = 1e-05
masked_score = -1e30
rotary_base = 10000.0
root_half = 0.7071067811865476
inverse_root_tau = 0.3989422804014327
scale = HD**-0.5


def place_constants():
    qod = np.zeros((288, 512), np.float32)
    kv = np.zeros((48, 512), np.float32)
    for s in range(8):
        for i in range(6):
            r = s * 6 + i
            qod[r, s * CHUNK + 22 + i] = 1
            qod[48 + r, s * CHUNK + 28 + i] = 1
            for g in range(4):
                qod[96 + 48 * g + r, s * CHUNK + 34 + 4 * i + g] = 1
            kv[r, s * CHUNK + 16 + i] = 1
    sums = np.zeros((256, 160), np.float32)
    sums_kv = np.zeros((256, 48), np.float32)
    for s in range(8):
        for i in range(6):
            for kind in range(3):
                sums[s * 32 + 6 * kind + i, 48 * kind + s * 6 + i] = 1
            sums_kv[s * 32 + 18 + i, s * 6 + i] = 1
        for k in range(8):
            sums[s * 32 + 24 + k, 144 + k] = 1
    up = np.zeros((192, 192), np.float32)
    for h in range(2):
        for x in range(4):
            for j in range(24):
                up[h * 96 + x * 24 + j, x * 48 + h * 24 + j] = 1
    perm = np.zeros((768, 768), np.float32)
    for chip in range(16):
        for c in range(2):
            for j in range(24):
                perm[chip * 48 + c * 24 + j, c * 384 + chip * 24 + j] = 1
    spread48 = np.zeros((128, 768), np.float32)
    spread48[np.arange(768) % 48, np.arange(768)] = 1
    spread96 = np.zeros((128, 1536), np.float32)
    spread96[np.arange(1536) % 96, np.arange(1536)] = 1
    return qod, kv, up, perm, spread48, spread96, sums, sums_kv, up.T


CONSTS = place_constants()


def nn(a, b):
    return jnp.dot(a, b, preferred_element_type=F32)


def nt(a, b):
    return lax.dot_general(a, b, (((1,), (1,)), ((), ())), preferred_element_type=F32)


def tn(a, b):
    return lax.dot_general(a, b, (((0,), (0,)), ((), ())), preferred_element_type=F32)


def ranges(lengths):
    at, out = 0, []
    for n in lengths:
        out.append((at, n))
        at += n
    return out


class Place:
    def __init__(self):
        self.z = lax.axis_index("dp")
        f = lax.axis_index("fsdp")
        self.y = f // 8
        self.x = (f // 2) % 4
        self.c = f % 2

    def dev(self, dz=0, dy=0, dx=0, dc=0):
        z = (self.z + dz) % 4
        y = (self.y + dy) % 4
        x = (self.x + dx) % 4
        c = (self.c + dc) % 2
        return (z, y * 8 + x * 2 + c)

    def along(self, axis, d):
        return self.dev(**{"d" + axis: d})

    def pos(self, axis):
        return getattr(self, axis)


class Ring:
    def __init__(self, me, axis, view, sems, many):
        self.me, self.axis, self.view, self.sems, self.many = me, axis, view, sems, many
        self.p = me.pos(axis)

    def _copy(self, to, src, dst, sem):
        return pltpu.make_async_remote_copy(
            src_ref=src,
            dst_ref=dst,
            send_sem=self.sems.at[0],
            recv_sem=self.sems.at[sem],
            device_id=self.me.along(self.axis, to),
            device_id_type=MESH,
        )

    def _await(self, ref, sem):
        pltpu.make_async_copy(ref, ref, self.sems.at[sem]).wait()

    def sent(self):
        self._await(self.many(3), 0)


class Gather(Ring):
    def _pass(self, to, k, h, sem):
        block = self.view(k % 4, h)
        self._copy(to, block, block, sem).start()

    def start(self):
        p = self.p
        self._pass(1, p, 0, 1)
        self._pass(-1, p, 1, 2)
        self._pass(1, p, 1, 3)
        self._pass(-1, p, 0, 3)

    def forward(self):
        p = self.p
        self._await(self.view((p + 3) % 4, 0), 1)
        self._pass(1, p + 3, 0, 4)
        self._await(self.view((p + 1) % 4, 1), 2)
        self._pass(-1, p + 1, 1, 4)

    def near(self):
        self._await(self.many(1), 3)

    def far(self):
        self._await(self.many(1), 4)

    def finish(self):
        self.near()
        self.far()
        self.sent()


class Scatter(Ring):
    def __init__(self, me, axis, view, sems, many, buf, leads, rows):
        super().__init__(me, axis, view, sems, many)
        self.buf, self.leads, self.rows = buf, leads, rows

    def _slot(self, j, h):
        ref = self.buf.at[j]
        n = self.rows[h]
        if n != ref.shape[-2]:
            ref = ref.at[tuple(slice(None) for _ in self.leads) + (pl.ds(0, n),)]
        return ref

    def _pass(self, to, k, h, slot, sem):
        self._copy(to, self.view(k % 4, h), self._slot(slot, h), sem).start()

    def _add(self, k, h, slots):
        target = self.view(k, h)
        srcs = [self._slot(s, h) for s in slots]

        def one(idx):
            total = target[idx].astype(F32)
            for s in srcs:
                total = total + s[idx].astype(F32)
            target[idx] = total.astype(BF16)

        if not self.leads:
            one((slice(None), slice(None)))
        else:

            @pl.loop(0, self.leads[0])
            def _(i):
                one((i,))

    def start_far(self):
        p = self.p
        self._pass(1, p + 2, 0, 0, 1)
        self._pass(-1, p + 2, 1, 1, 2)

    def start_near(self):
        p = self.p
        self._pass(1, p + 1, 1, 3, 3)
        self._pass(-1, p + 3, 0, 4, 3)

    def start(self):
        self.start_far()
        self.start_near()

    def forward(self):
        p = self.p
        self._await(self._slot(0, 0), 1)
        self._add((p + 1) % 4, 0, [0])
        self._pass(1, p + 1, 0, 2, 3)
        self._await(self._slot(1, 1), 2)
        self._add((p + 3) % 4, 1, [1])
        self._pass(-1, p + 3, 1, 5, 3)

    def finish(self):
        self._await(self.many(2), 3)
        self._add(self.p, 0, [2, 4])
        self._add(self.p, 1, [3, 5])
        self.sent()


class Direct(Ring):
    def __init__(self, me, axis, view, sems, many, buf):
        super().__init__(me, axis, view, sems, many)
        self.buf = buf

    def start(self):
        for j, to in enumerate((2, 1, -1)):
            self._copy(to, self.view((self.p + to) % 4), self.buf.at[j], 1).start()

    def finish(self):
        self._await(self.many(3), 1)
        target = self.view(self.p)
        total = target[...].astype(F32)
        for j in range(3):
            total = total + self.buf[j].astype(F32)
        target[...] = total.astype(BF16)
        self.sent()


def kernel(
    xin, seg, cot, w_gain, w_nbias, w_q, w_qb, w_kv, w_o, w_ob, w_up, w_ub, w_down, w_db, h_qod, h_kv, h_up, h_perm, h_s48, h_s96, h_sums, h_sums_kv, h_upT,
    out_y, out_gx, out_v, out_u,
    W, chunk, rawu, got, gotu, vecs, ubv,
    X2, gl, seg2, cosT, sinT, mbias, n_, r_, h1, attn, mlp, kvT, k_, v_, qT, p_, mixT, mixed, act, slope,
    acc, glT, attnT, gm, gmT, dk, dv, gs, vg, ubg, g_, xs, xr,
    bA2, bB2, bO2, bU2, bD1, bD2, bA3, bB3, bO3, bU3, bD3, back, rgot, rgotu,
    c_qod, c_kv, c_up, c_perm, c_s48, c_s96, c_sums, c_sums_kv, c_upT,
    const_sem, pair_send, pair_recv, line_sem, ag_sem, rs_sem,
):
    me = Place()
    z, y, x, c = me.z, me.y, me.x, me.c
    s_me = x * 2 + c

    consts = [(h_perm, c_perm), (h_qod, c_qod), (h_kv, c_kv), (h_up, c_up), (h_s48, c_s48), (h_s96, c_s96),
              (h_sums, c_sums), (h_sums_kv, c_sums_kv), (h_upT, c_upT)]
    const_copies = [pltpu.make_async_copy(h, v, const_sem.at[i]) for i, (h, v) in enumerate(consts)]
    for cp in const_copies:
        cp.start()

    bar = pltpu.get_barrier_semaphore()
    line = [(dx, dc) for dx in range(4) for dc in range(2) if (dx, dc) != (0, 0)]
    partners = [me.dev(dx=dx, dc=dc) for dx, dc in line]
    partners += [me.dev(dy=d) for d in (1, 2, 3)] + [me.dev(dz=d) for d in (1, 2, 3)]
    for d in partners:
        pl.semaphore_signal(bar, inc=1, device_id=d, device_id_type=MESH)
    sibling = me.dev(dc=1)

    def to_sibling(i, src, dst):
        return pltpu.make_async_remote_copy(
            src_ref=src, dst_ref=dst, send_sem=pair_send.at[i], recv_sem=pair_recv.at[i],
            device_id=sibling, device_id_type=MESH)

    def lane_place():
        r = lax.broadcasted_iota(jnp.int32, (128, HALF), 0)
        m = lax.broadcasted_iota(jnp.int32, (128, HALF), 1)
        small = (r < 6) & (m == r + 6 * s_me)
        wide = (r >= 8) & (r < 32) & (m == r - 8 + 128 + 24 * x)
        return jnp.where(small | wide, 1.0, 0.0).astype(BF16)

    def line_copies(l, bufs, into, bufu, intou, sems, rows=slice(None)):
        out = []
        for dx, dc in line:
            t = (c + dc) % 2
            s_to = ((x + dx) % 4) * 2 + t
            out.append(pltpu.make_async_remote_copy(
                src_ref=bufs(s_to, t), dst_ref=into.at[l, s_me, rows], send_sem=sems.at[0], recv_sem=sems.at[1],
                device_id=me.dev(dx=dx, dc=dc), device_id_type=MESH))
        for dx in range(1, 4):
            out.append(pltpu.make_async_remote_copy(
                src_ref=bufu((x + dx) % 4), dst_ref=intou.at[l, x], send_sem=sems.at[2],
                recv_sem=sems.at[3], device_id=me.dev(dx=dx), device_id_type=MESH))
        for cp in out:
            cp.start()

    def line_wait(sems, rows=CHUNK):
        seven, three = W.at[0, 0, 0, pl.ds(0, 7 * rows)], W.at[0, 0, 0, pl.ds(0, 144)]
        for i, ref in enumerate((seven, seven, three, three)):
            pltpu.make_async_copy(ref, ref, sems.at[i]).wait()

    h1[0:2 * CHUNK, :] = jnp.zeros((2 * CHUNK, D), F32)
    for l in range(2):
        h1[7 * l:7 * l + 2, 0:6] = w_gain[l].astype(F32)
        h1[7 * l + 2:7 * l + 4, 0:6] = w_nbias[l].astype(F32)
        for k, ref in ((4, w_qb), (5, w_ob), (6, w_db)):
            h1[7 * l + k:7 * l + k + 1, 0:6] = ref[...].astype(F32)[l:l + 1]
    h1[0:2, 8:32] = w_ub[...].astype(F32)
    h1[16:22, 0:128] = w_kv[...].astype(F32)
    for i in range(6):
        q2, o2, d2 = w_q[i].astype(F32), w_o[i].astype(F32), w_down[i].astype(F32)
        for l in range(2):
            at = CHUNK * l
            h1[at + 22 + i:at + 23 + i, :] = q2[l:l + 1]
            h1[at + 28 + i:at + 29 + i, :] = o2[l:l + 1]
            for g in range(4):
                h1[at + 34 + 4 * i + g:at + 35 + 4 * i + g, :] = d2[l:l + 1, g * D:(g + 1) * D]
    for l in range(2):
        u = w_up[l].astype(F32)
        rawu[l] = jnp.concatenate([u[:, 0:HALF], u[:, HALF:]], axis=0).astype(BF16)

    const_copies[0].wait()
    place = lane_place()

    def prepare(l):
        vf = h1[CHUNK * l:CHUNK * l + CHUNK, :]
        v = vf.astype(BF16)
        vp = nn(v, c_perm[...]).astype(BF16).astype(F32)
        row = lax.broadcasted_iota(jnp.int32, (CHUNK, HALF), 0)
        lane = lax.broadcasted_iota(jnp.int32, (CHUNK, HALF), 1)
        if l == 0:
            head = jnp.where(row < 16, nn(v[:, 0:128], place), jnp.where(lane < 128, vf[:, 0:HALF], 0.0))
        for t in range(2):
            part = jnp.where(row < 34, vf[:, t * HALF:(t + 1) * HALF], vp[:, t * HALF:(t + 1) * HALF])
            if l == 0:
                ours = jnp.where((lane < 128) | (c == t), head, 0.0)
                part = jnp.where(row < 22, ours, part)
            chunk[l, t] = part.astype(BF16)

    def send_chunks(l):
        first = 0 if l == 0 else 16
        rows = pl.ds(first, CHUNK - first)
        line_copies(l, lambda s, t: chunk.at[l, t, rows], got, lambda xx: rawu.at[l], gotu, line_sem.at[l], rows)
        if l == 1:
            got[l, :, 0:16, :] = jnp.zeros((8, 16, HALF), BF16)
        got[l, s_me, rows] = chunk[l, c, rows]
        gotu[l, x] = rawu[l]

    prepare(0)
    seg2[c] = jnp.broadcast_to(seg[...], (8, TOK))
    own = pl.ds(pl.multiple_of(c * TOK, TOK), TOK)

    pl.semaphore_wait(bar, len(partners))

    def to_sibling(i, src, dst):
        return pltpu.make_async_remote_copy(
            src_ref=src, dst_ref=dst, send_sem=pair_send.at[i], recv_sem=pair_recv.at[i],
            device_id=sibling, device_id_type=MESH)

    send_chunks(0)
    seg_copy = to_sibling(0, seg2.at[c], seg2.at[c])
    seg_copy.start()
    x_copy = to_sibling(1, xin, X2.at[c])
    x_copy.start()
    c_copy = to_sibling(2, cot, gl.at[own])
    c_copy.start()
    X2[c] = xin[...]
    gl[own, :] = cot[...]
    prepare(1)
    send_chunks(1)

    half_width = HD // 8
    frequency = np.float32(rotary_base) ** (-(np.arange(half_width, dtype=np.float32) * 2.0) / (2 * half_width))
    row = lax.broadcasted_iota(jnp.int32, (half_width, TOK), 0)
    freq = jnp.zeros((half_width, TOK), F32)
    for f in range(half_width):
        freq = jnp.where(row == f, float(frequency[f]), freq)
    seg_copy.wait()
    for b in range(2):
        docs = seg2[b].astype(F32)
        over_lanes = jnp.broadcast_to(docs[0:1], (TOK, TOK))
        over_rows = over_lanes.T
        earlier = jnp.sum(jnp.where(over_rows < over_lanes, 1.0, 0.0), axis=0, keepdims=True)
        place = lax.broadcasted_iota(jnp.int32, (1, TOK), 1).astype(F32) - earlier
        angle = jnp.broadcast_to(place, (8, TOK)) * freq
        cosT[:, b * TOK:(b + 1) * TOK] = jnp.cos(angle)
        sinT[:, b * TOK:(b + 1) * TOK] = jnp.sin(angle)
        kk = lax.broadcasted_iota(jnp.int32, (TOK, TOK), 0)
        qq = lax.broadcasted_iota(jnp.int32, (TOK, TOK), 1)
        mbias[b] = jnp.where((over_rows == over_lanes) & (kk <= qq), 0.0, masked_score)
    x_copy.wait()
    c_copy.wait()

    CH = 64

    def norm_of(h):
        centred = h - jnp.mean(h, axis=-1, keepdims=True)
        inverse = lax.rsqrt(jnp.mean(centred * centred, axis=-1, keepdims=True) + norm_epsilon)
        return centred * inverse, inverse

    def normalise(i, h):
        rows = pl.ds(pl.multiple_of(i * CH, CH), CH)
        n, inverse = norm_of(h)
        n_[rows, :] = n
        r_[rows, :] = jnp.broadcast_to(inverse, (CH, 128))

    def input_rows(i):
        return X2[i // 4, pl.ds(pl.multiple_of((i % 4) * CH, CH), CH), :].astype(F32)

    @pl.loop(0, 8)
    def _(i):
        normalise(i, input_rows(i))

    glT[...] = gl[...].T
    for cp in const_copies[1:]:
        cp.wait()

    def quarter(k):
        return pl.multiple_of(D0 + 48 * k, 16)

    def assemble(l):
        line_wait(line_sem.at[l], CHUNK if l == 0 else CHUNK - 16)
        stack = got[l].reshape(512, HALF)
        W[l, z, y, Q0:D0, :] = nn(c_qod[0:96, :], stack).astype(BF16)
        down = nn(c_qod[pl.ds(pl.multiple_of(96 + 48 * x, 16), 48), :], stack).astype(BF16)
        W[l, z, y, pl.ds(quarter(x), 48), :] = down
        if l == 0:
            kv = nn(c_kv[...], stack[:, 0:128]).astype(BF16)
            W[0, z, y, KV0:KV0 + 16, :] = jnp.concatenate([kv[0:16], kv[16:32], kv[32:48]], axis=1)
            vec = got[0, 0, 0:16, :].astype(F32)
            for s in range(1, 8):
                vec = vec + got[0, s, 0:16, :].astype(F32)
            W[0, z, y, VEC0:VEC0 + 16, :] = vec.astype(BF16)
        W[l, z, y, U0:ROWS, :] = nn(c_up[...], gotu[l].reshape(192, HALF)).astype(BF16)

    def many(n, wide):
        if wide:
            return lambda count: W.at[0, pl.ds(0, count), :, pl.ds(0, n), :]
        return lambda count: W.at[0, 0, pl.ds(0, count), pl.ds(0, n), :]

    def cut(row0, n, h):
        first = halves(n)[0]
        return pl.ds(row0 if h == 0 else pl.multiple_of(row0 + first, 16), first if h == 0 else n - first)

    def halves(n):
        first = (n + 31) // 32 * 16
        return (first, n - first)

    def gathers(l):
        g = {}

        def y_then_z(i, name, row0, n):
            g[name + "2"] = Gather(me, "y", lambda k, h: W.at[l, z, k, cut(row0, n, h), :], ag_sem.at[l, i], many(n, False))
            g[name + "3"] = Gather(me, "z", lambda k, h: W.at[l, k, pl.ds(2 * h, 2), pl.ds(row0, n), :], ag_sem.at[l, i + 1],
                                   many(n, True))

        def z_then_y(i, name, row0, n):
            g[name + "2"] = Gather(me, "z", lambda k, h: W.at[l, k, y, cut(row0, n, h), :], ag_sem.at[l, i], many(n, False))
            g[name + "3"] = Gather(me, "y", lambda k, h: W.at[l, pl.ds(2 * h, 2), k, pl.ds(row0, n), :], ag_sem.at[l, i + 1],
                                   many(n, True))

        e0 = 0 if l == 0 else Q0
        en = (D0 - e0) // 2
        y_then_z(0, "E", e0, en)
        z_then_y(2, "F", e0 + en, en)
        z_then_y(4, "D", quarter(x), 48)
        y_then_z(6, "U", U0, 112)
        z_then_y(8, "V", U0 + 112, 80)
        for i, dy in enumerate((0, 1, 3, 2)):
            g["D4", i] = Gather(me, "x", lambda k, h, dy=dy: W.at[l, pl.ds(2 * h, 2), (y + dy) % 4, pl.ds(quarter(k), 48), :],
                                ag_sem.at[l, 10 + i], many(48, True))
        return g

    g0, g1 = gathers(0), gathers(1)

    def second_stage(l, g):
        assemble(l)
        for n in "EFDUV":
            g[n + "2"].start()

    def forward_on(r, *names):
        for n in names:
            r[n].forward()

    def third_stage(g, first="EFD", rest="UV"):
        for n in first:
            g[n + "2"].finish()
            g[n + "3"].start()
        g["D4", 0].start()
        for n in rest:
            g[n + "2"].finish()
            g[n + "3"].start()

    def first_quarters(g):
        g["D3"].forward()
        g["D4", 0].forward()
        g["D3"].near()
        g["D4", 1].start()
        g["D4", 2].start()

    def heads_ready(g):
        g["E3"].finish()
        g["F3"].finish()

    def last_quarter(g):
        g["D3"].far()
        g["D4", 3].start()
        g["D4", 1].forward()
        g["D4", 2].forward()

    def hidden_ready(g):
        g["U3"].finish()
        g["V3"].finish()

    def down_ready(g):
        g["D3"].sent()
        for i in range(4):
            g["D4", i].finish()

    second_stage(0, g0)
    forward_on(g0, "E2", "F2", "D2", "U2", "V2")
    third_stage(g0, rest="")
    g0["U2"].finish()
    g0["V2"].finish()
    forward_on(g0, "E3", "F3")
    g0["U3"].start()
    g0["V3"].start()
    second_stage(1, g1)
    heads_ready(g0)

    tile = W[0, :, :, VEC0:VEC0 + 16, :].reshape(256, HALF)
    wide = nn(tile[:, 0:128], c_s48[...])
    at = lax.broadcasted_iota(jnp.int32, (16, D), 1)
    total = jnp.zeros((16, D), F32)
    for m in range(16):
        total = total + jnp.where((at >= 48 * m) & (at < 48 * m + 48), wide[16 * m:16 * m + 16], 0.0)
    vecs[...] = total
    wide = nn(tile[:, 128:256], c_s96[...])
    at = lax.broadcasted_iota(jnp.int32, (16, 1536), 1)
    total = jnp.zeros((16, 1536), F32)
    for m in range(16):
        total = total + jnp.where((at >= 96 * m) & (at < 96 * m + 96), wide[16 * m:16 * m + 16], 0.0)
    for l in range(2):
        for k in range(4):
            ubv[l, k] = jnp.broadcast_to(total[l:l + 1, k * HALF:(k + 1) * HALF], (8, HALF))

    def vec(l, k):
        return vecs[7 * l + k:7 * l + k + 1, :]

    def norm_inputs(l, again=False):
        @pl.loop(0, 8)
        def _(i):
            rows = pl.ds(pl.multiple_of(i * CH, CH), CH)
            n = norm_of(input_rows(i))[0] if again else n_[rows, :]
            attn[rows, :] = (n * vec(l, 0) + vec(l, 2)).astype(BF16)
            mlp[rows, :] = (n * vec(l, 1) + vec(l, 3)).astype(BF16)

    def key_weight():
        kvw = W[0, :, :, KV0:KV0 + 16, :]
        return jnp.concatenate([kvw[..., 0:128], kvw[..., 128:256], kvw[..., 256:384]], axis=2).reshape(D, 128)

    def weight(l, row0, n=48):
        return W[l, :, :, pl.ds(row0, n), :].reshape(16 * n, HALF)

    def up_weight(l, k, h):
        return W[l, k, :, U0 + 96 * h:U0 + 96 * h + 96, :].reshape(HALF, HALF)

    def down_weight(l, k):
        return weight(l, pl.multiple_of(D0 + 48 * k, 16))

    def rotate_heads(v, heads):
        v = v.reshape(heads, HD, 512)
        cs, sn = cosT[...][None], sinT[...][None]
        u1, u2 = v[:, 0:8, :], v[:, 8:16, :]
        return jnp.concatenate([u1 * cs - u2 * sn, u2 * cs + u1 * sn, v[:, 16:, :]], axis=1).reshape(heads * HD, 512)

    def rotate_heads_back(v, heads):
        v = v.reshape(heads, HD, 512)
        cs, sn = cosT[...][None], sinT[...][None]
        u1, u2 = v[:, 0:8, :], v[:, 8:16, :]
        return jnp.concatenate([u1 * cs + u2 * sn, u2 * cs - u1 * sn, v[:, 16:, :]], axis=1).reshape(heads * HD, 512)

    def far_first(p, i):
        return (p + jnp.where(i == 0, 2, jnp.where(i == 1, 1, jnp.where(i == 2, 3, 0)))) % 4

    def serve(i, points):
        for at, step in points.items():
            pl.when(i == at)(step)

    def steps(*todo):
        def run():
            for step, *args in todo:
                step(*args)

        return run

    def down_block(l, rows):
        acc[rows, :] = nt(mixed[l, rows, :], weight(l, O0))
        for k in range(4):
            acc[rows, :] += nt(act[l, k, rows, :], down_weight(l, k))

    def forward(l, in_heads, before_ffn, in_ffn, after_hidden):
        norm_inputs(l)
        if l == 0:
            kv = nn(attn[...], key_weight()).T
            keys = rotate_heads(kv[0:HD], 1)
            kvT[0:HD, :] = keys.astype(BF16)
            kvT[HD:, :] = kv[HD:].astype(BF16)
            k_[...] = keys.T.astype(BF16)
            v_[...] = kv[HD:].T.astype(BF16)
        qb = vec(l, 4)
        qb = jnp.where(c == 0, qb[:, 0:HALF], qb[:, HALF:])
        q = nn(attn[...], weight(l, Q0)) + qb
        qT[l] = rotate_heads(q.T, 6).astype(BF16)

        @pl.loop(0, 3)
        def _(pair):
          serve(2 * pair, in_heads)
          serve(2 * pair + 1, in_heads)
          for h in (2 * pair, 2 * pair + 1):
            hs = pl.ds(pl.multiple_of(h * HD, HD), HD)
            for b in range(2):
                bs = slice(b * TOK, (b + 1) * TOK)
                s = nn(k_[bs, :], qT[l, hs, bs]) * scale + mbias[b]
                e = jnp.exp(s - jnp.max(s, axis=0, keepdims=True))
                low = (e * (1.0 / jnp.sum(e, axis=0, keepdims=True))).astype(BF16)
                p_[l, h, b] = low
                mixT[hs, bs] = nn(kvT[HD:, bs], low).astype(BF16)

        mixed[l] = mixT[...].T
        before_ffn()

        @pl.loop(0, 4)
        def _(i):
            k = far_first(x, i) if l == 1 else i
            serve(i, in_ffn)
            for b in range(2):
                rows = slice(b * TOK, (b + 1) * TOK)
                hid = nt(mlp[rows, 0:HALF], up_weight(l, k, 0)) + nt(mlp[rows, HALF:], up_weight(l, k, 1))
                hid = hid + ubv[l, k, 0:1, :]
                phi = 0.5 * (1.0 + lax.erf(hid * root_half))
                low = (hid * phi).astype(BF16)
                act[l, k, rows, :] = low
                slope[l, k, rows, :] = (phi + hid * jnp.exp(-0.5 * hid * hid) * inverse_root_tau).astype(BF16)
            after_hidden(i, k)

    forward(
        0,
        {
            0: steps((first_quarters, g0)),
            2: steps((forward_on, g0, "U3", "V3"), (forward_on, g1, "E2", "F2", "D2", "U2", "V2")),
            3: steps((last_quarter, g0)),
            4: steps((third_stage, g1)),
        },
        steps((forward_on, g0, ("D4", 3)), (hidden_ready, g0)),
        {
            1: steps((forward_on, g1, "E3", "F3")),
            2: steps((first_quarters, g1)),
            3: steps((forward_on, g1, "U3", "V3")),
        },
        lambda i, k: None,
    )
    down_ready(g0)
    swap = [to_sibling(3 + b, xs.at[b], xr.at[b]) for b in range(2)]
    for b in range(2):
        down_block(0, slice(b * TOK, (b + 1) * TOK))
        xs[b] = acc[b * TOK:(b + 1) * TOK, :].astype(BF16)
        swap[b].start()
        if b == 0:
            last_quarter(g1)
    heads_ready(g1)
    for cp in swap:
        cp.wait()

    @pl.loop(0, 8)
    def _(i):
        b = i // 4
        rows = pl.ds(pl.multiple_of((i % 4) * CH, CH), CH)
        h = X2[b, rows, :].astype(F32) + (vec(0, 5) + vec(0, 6))
        h = h + (xs[b, rows, :].astype(F32) + xr[b, rows, :].astype(F32))
        normalise(i, h)

        @pl.when(b == c)
        def _():
            h1[rows, :] = h

    def scatters(l):
        gslot = 2 if l == 1 else 1
        g = {}

        def y_then_z(i, name, row0, n, b2, b3):
            g[name + "2"] = Scatter(me, "y", lambda k, h: W.at[gslot, pl.ds(2 * h, 2), k, pl.ds(row0, n), :],
                                    rs_sem.at[l, i], many(n, True), b2.at[l], (2,), (n, n))
            g[name + "3"] = Direct(me, "z", lambda k: W.at[gslot, k, y, pl.ds(row0, n), :], rs_sem.at[l, i + 1],
                                   many(n, False), b3.at[l, :, pl.ds(0, n)])

        for i, dy in enumerate((2, 1, 3, 0)):
            g["D1", i] = Scatter(me, "x", lambda k, h, dy=dy: W.at[gslot, pl.ds(2 * h, 2), (y + dy) % 4, pl.ds(quarter(k), 48), :],
                                 rs_sem.at[l, i], many(48, True), bD1.at[l, i], (2,), (48, 48))
        y_then_z(4, "D", quarter(x), 48, bD2, bD3)
        y_then_z(6, "O", O0, 48, bO2, bO3)
        a0 = 0 if l == 0 else VEC0
        y_then_z(8, "A", a0, 48 - a0, bA2, bA3)
        y_then_z(10, "B", 48, 32, bB2, bB3)
        g["U2"] = Scatter(me, "z", lambda k, h: W.at[gslot, k, pl.ds(2 * h, 2), pl.ds(U0, 192), :], rs_sem.at[l, 12],
                          many(192, True), bU2.at[l], (2,), (192, 192))
        g["U3"] = Scatter(me, "y", lambda k, h: W.at[gslot, z, k, cut(U0, 192, h), :], rs_sem.at[l, 13],
                          many(192, False), bU3.at[l], (), (96, 96))
        return g

    def finish_line(l):
        B = W.at[2 if l == 1 else 1, z, y]
        rows = jnp.concatenate([B[Q0:D0, :], B[pl.ds(quarter(x), 48), :], B[VEC0:VEC0 + 16, :]], axis=0)
        stack = nn(c_sums[...], rows)
        if l == 0:
            kv = B[KV0:KV0 + 16, :]
            kv = jnp.concatenate([kv[:, 0:128], kv[:, 128:256], kv[:, 256:384]], axis=0)
            stack = stack + jnp.concatenate([nn(c_sums_kv[...], kv), jnp.zeros((256, 256), F32)], axis=1)
        back[l] = stack.astype(BF16).reshape(8, 32, HALF)
        gotu[l] = nn(c_upT[...], B[U0:ROWS, :]).astype(BF16).reshape(4, 48, HALF)
        line_copies(l, lambda s, t: back.at[l, s], rgot, lambda xx: gotu.at[l, xx], rgotu, line_sem.at[2 + l])
        rgot[l, s_me] = back[l, s_me]
        rgotu[l, x] = gotu[l, x]

    def last_sums(l):
        line_wait(line_sem.at[2 + l], 32)
        halves, tiles = [], []
        for t in range(2):
            parts = [rgot[l, 2 * xx + t].astype(F32) for xx in range(4)]
            halves.append(parts[0] + parts[1] + parts[2] + parts[3])
        for xx in range(4):
            tiles.append(jnp.concatenate([rgot[l, 2 * xx, 0:32, :], rgot[l, 2 * xx + 1, 0:32, :]], axis=1))
        unperm = nt(jnp.concatenate(tiles, axis=0), c_perm[...])
        row = lax.broadcasted_iota(jnp.int32, (32, HALF), 0)
        lane = lax.broadcasted_iota(jnp.int32, (32, HALF), 1)
        both = halves[0] + halves[1]
        mine = jnp.where(lane < 128, both, jnp.where(c == 0, halves[0], halves[1]))
        hi = mine.astype(BF16)
        lo = (mine - hi.astype(F32)).astype(BF16)
        spot = lane_place()
        small = nt(hi, spot) + nt(lo, spot)
        out_v[l, 0:32, 0:HALF] = jnp.where(row < 18, halves[0], both)
        out_v[l, 0:32, HALF:] = halves[1]
        out_v[l, 24:32, 0:128] = small[24:32]
        for xx in range(4):
            out_v[l, 32 + 16 * xx:48 + 16 * xx, :] = unperm[32 * xx + 8:32 * xx + 24]
        u = rgotu[l, 0].astype(F32)
        for xx in range(1, 4):
            u = u + rgotu[l, xx].astype(F32)
        out_u[l] = u

    r1, r0 = scatters(1), scatters(0)

    def first_sums(r):
        for i in range(4):
            r["D1", i].start()
        r["O2"].start()

    def next_ring(r, *names):
        for n in names:
            r[n + "2"].finish()
            r[n + "3"].start()

    def down_second(r):
        r["D1", 0].finish()
        r["D2"].start_far()
        r["D1", 1].finish()
        r["D1", 2].finish()
        r["D2"].start_near()
        r["D1", 3].finish()

    def finish_third(r, names):
        for n in names:
            r[n].finish()

    def out_grad(l):
        for b in range(2):
            rows = slice(b * HALF, (b + 1) * HALF)
            part = nn(glT[rows, :], mixed[l]).astype(BF16).reshape(2, 4, 48, HALF)
            W[2 if l == 1 else 1, 2 * b:2 * b + 2, :, O0:O0 + 48, :] = part

    def down_grad(l, r, i, k):
        rows_d = pl.ds(pl.multiple_of(D0 + 48 * k, 16), 48)
        for b in range(2):
            rows = slice(b * HALF, (b + 1) * HALF)
            part = nn(glT[rows, :], act[l, k]).astype(BF16).reshape(2, 4, 48, HALF)
            W[2 if l == 1 else 1, 2 * b:2 * b + 2, :, rows_d, :] = part
        rings = [r["D1", j] for j in range(4)]
        serve(i, {0: steps(*((ring.start_far,) for ring in rings)), 2: steps(*((ring.start_near,) for ring in rings))})

    def backward(l, r, in_ffn, before_heads, in_heads, before_query):
        G = W.at[2 if l == 1 else 1]
        vg[5:6, :] = jnp.sum(gl[own, :].astype(F32), axis=0, keepdims=True)
        acc[...] = jnp.zeros_like(acc)

        @pl.loop(0, 4)
        def _(i):
            k = far_first(z, i)
            serve(i, in_ffn)
            sums = jnp.zeros((1, HALF), F32)
            for b in range(2):
                rows = slice(b * TOK, (b + 1) * TOK)
                gh = nn(gl[rows, :], down_weight(l, k)) * slope[l, k, rows, :].astype(F32)
                gh = gh.astype(BF16)
                slope[l, k, rows, :] = gh
                sums = sums + jnp.sum(gh.astype(F32), axis=0, keepdims=True)
                for h in range(2):
                    acc[rows, h * HALF:(h + 1) * HALF] += nn(gh, up_weight(l, k, h))
            ubg[k] = jnp.broadcast_to(sums, (8, HALF))
            ghT = slope[l, k].T
            for h in range(2):
                part = nn(ghT, mlp[:, h * HALF:(h + 1) * HALF]).astype(BF16).reshape(4, 96, HALF)
                G[k, :, U0 + 96 * h:U0 + 96 * h + 96, :] = part
            serve(i, {0: r["U2"].start_far, 2: r["U2"].start_near})

        before_heads()

        for b in range(2):
            rows = slice(b * TOK, (b + 1) * TOK)
            gm[rows, :] = nn(gl[rows, :], weight(l, O0)).astype(BF16)
        gmT[...] = gm[...].T

        if l == 1:
            dk[...] = jnp.zeros_like(dk)
            dv[...] = jnp.zeros_like(dv)

        @pl.loop(0, 3)
        def _(pair):
          serve(2 * pair, in_heads)
          serve(2 * pair + 1, in_heads)
          for h in (2 * pair, 2 * pair + 1):
            hs = pl.ds(pl.multiple_of(h * HD, HD), HD)
            for b in range(2):
                bs = slice(b * TOK, (b + 1) * TOK)
                low = p_[l, h, b]
                probs = low.astype(F32)
                t = probs * nn(v_[bs, :], gmT[hs, bs])
                grad = (t - probs * jnp.sum(t, axis=0, keepdims=True)).astype(BF16)
                dq = nn(kvT[0:HD, bs], grad) * scale
                cs, sn = cosT[:, bs], sinT[:, bs]
                u1, u2 = dq[0:8], dq[8:16]
                dq = jnp.concatenate([u1 * cs + u2 * sn, u2 * cs - u1 * sn, dq[16:]], axis=0)
                mixT[hs, bs] = dq.astype(BF16)
                dk[bs, :] += nt(grad, qT[l, hs, bs])
                dv[bs, :] += nt(low, gmT[hs, bs])

        before_query()
        low = mixT[...].T
        gm[...] = low
        qsum = jnp.sum(low.astype(F32), axis=0, keepdims=True)
        zero = jnp.zeros_like(qsum)
        vg[4:5, :] = jnp.concatenate([jnp.where(c == 0, qsum, zero), jnp.where(c == 0, zero, qsum)], axis=1)
        if l == 0:
            keys = rotate_heads_back((dk[...] * scale).T, 1).T
            gs[...] = jnp.concatenate([keys, dv[...]], axis=1).astype(BF16)

    def query_grad(l, r):
        G = W.at[2 if l == 1 else 1]
        for b in range(2):
            rows = slice(b * HALF, (b + 1) * HALF)
            part = nn(attnT[rows, :], gm[...]).astype(BF16).reshape(2, 4, 48, HALF)
            G[2 * b:2 * b + 2, :, Q0:Q0 + 48, :] = part
        r["B2"].start()
        if l == 0:
            dkv = nn(attnT[...], gs[...]).astype(BF16).reshape(4, 4, 48, 128)
            G[:, :, KV0:KV0 + 16, :] = jnp.concatenate([dkv[:, :, 0:16], dkv[:, :, 16:32], dkv[:, :, 32:48]], axis=3)

    def fold_block(l, b, sums):
        hold = g_ if l == 1 else h1
        rows = slice(b * TOK, (b + 1) * TOK)
        ea = nt(gm[rows, :], weight(l, Q0))
        if l == 0:
            ea = ea + nt(gs[rows, :], key_weight())
        hold[...] = ea

        def fold(i, sums):
            rows = pl.ds(pl.multiple_of(i * CH, CH), CH)
            all_rows = pl.ds(pl.multiple_of(b * TOK + i * CH, CH), CH)
            n = n_[all_rows, :] if l == 1 else norm_of(X2[b, rows, :].astype(F32))[0]
            ea, em = hold[rows, :], acc[all_rows, :]
            xs[b, rows, :] = (ea * vec(l, 0) + em * vec(l, 1)).astype(BF16)
            add = [ea * n, em * n, ea, em]
            return tuple(s + jnp.sum(a, axis=0, keepdims=True) for s, a in zip(sums, add))

        return lax.fori_loop(0, 4, fold, sums)

    def vector_grad(l, r, sums):
        G = W.at[2 if l == 1 else 1]
        for k in range(4):
            vg[k:k + 1, :] = sums[k]
        at = lax.broadcasted_iota(jnp.int32, (16, D), 1)
        rowk = lax.broadcasted_iota(jnp.int32, (16, D), 0)
        vv = jnp.where(rowk < 6, vg[...], 0.0)
        parts = [jnp.where((at >= 48 * m) & (at < 48 * m + 48), vv, 0.0).astype(BF16) for m in range(16)]
        small = nt(jnp.concatenate(parts, axis=0), c_s48[...]).astype(BF16)
        ub = jnp.concatenate([ubg[k][0:1, :] for k in range(4)], axis=1)
        at = lax.broadcasted_iota(jnp.int32, (16, 1536), 1)
        rowk = lax.broadcasted_iota(jnp.int32, (16, 1536), 0)
        ub = jnp.where(rowk == 6, jnp.broadcast_to(ub, (16, 1536)), 0.0)
        parts = [jnp.where((at >= 96 * m) & (at < 96 * m + 96), ub, 0.0).astype(BF16) for m in range(16)]
        wide = nt(jnp.concatenate(parts, axis=0), c_s96[...]).astype(BF16)
        both = jnp.concatenate([small, wide, jnp.zeros((256, 128), BF16)], axis=1)
        G[:, :, VEC0:VEC0 + 16, :] = both.reshape(4, 4, 16, HALF)
        r["A2"].start()

    def through_norm(n, inverse, g, s):
        m1 = jnp.mean(s, axis=-1, keepdims=True)
        m2 = jnp.mean(s * n, axis=-1, keepdims=True)
        return g + inverse * (s - m1 - n * m2)

    no_sums = (jnp.zeros((1, D), F32),) * 4

    forward(
        1,
        {1: steps((g1["D4", 3].forward,))},
        steps((out_grad, 1), (r1["O2"].start,), (hidden_ready, g1)),
        {},
        lambda i, k: down_grad(1, r1, i, k),
    )
    attnT[...] = attn[...].T
    down_ready(g1)
    backward(
        1, r1,
        {1: steps((forward_on, r1, "O2")), 3: steps((forward_on, r1, ("D1", 0)))},
        steps((forward_on, r1, ("D1", 1)), (next_ring, r1, "O")),
        {2: steps((forward_on, r1, ("D1", 2))), 4: steps((forward_on, r1, ("D1", 3)))},
        steps((forward_on, r1, "U2")),
    )
    swap = [to_sibling(6 + b, xs.at[b], xr.at[2 + b]) for b in range(2)]
    sums = no_sums
    for b in range(2):
        sums = fold_block(1, b, sums)
        swap[b].start()
    query_grad(1, r1)
    vector_grad(1, r1, sums)
    other = pl.ds(pl.multiple_of((1 - c) * TOK, TOK), TOK)
    down_block(1, other)
    xs[2] = acc[other, :].astype(BF16)
    y_copy = to_sibling(5, xs.at[2], xr.at[0])
    down_block(1, own)
    for cp in swap:
        cp.wait()
    y_copy.start()

    @pl.loop(0, 8)
    def _(i):
        b = i // 4
        rows = pl.ds(pl.multiple_of((i % 4) * CH, CH), CH)
        s = xs[b, rows, :].astype(F32) + xr[2 + b, rows, :].astype(F32)
        all_rows = pl.ds(pl.multiple_of(i * CH, CH), CH)
        g = through_norm(n_[all_rows, :], r_[all_rows, 0:1], gl[all_rows, :].astype(F32), s)
        gl[all_rows, :] = g.astype(BF16)

        @pl.when(b == c)
        def _():
            g_[rows, :] = g

    down_second(r1)
    forward_on(r1, "A2", "B2")
    glT[...] = gl[...].T

    @pl.loop(0, 4)
    def _(i):
        down_grad(0, r0, i, far_first(x, i))

    out_grad(0)
    r0["O2"].start()
    norm_inputs(0, again=True)
    attnT[...] = attn[...].T
    y_copy.wait()
    out_y[...] = (h1[...] + (vec(1, 5) + vec(1, 6)) + acc[own, :] + xr[0].astype(F32)).astype(BF16)
    backward(
        0, r0,
        {
            1: steps((forward_on, r0, "O2")),
            2: steps((next_ring, r1, "U"), (forward_on, r1, "D2")),
            3: steps((next_ring, r1, "A", "B"), (forward_on, r0, ("D1", 0))),
        },
        steps((forward_on, r0, ("D1", 1))),
        {
            0: steps((next_ring, r0, "O")),
            1: steps((forward_on, r0, ("D1", 2))),
            2: steps((next_ring, r1, "D"), (forward_on, r1, "U3")),
            3: steps((forward_on, r0, "U2", ("D1", 3))),
        },
        steps(),
    )
    query_grad(0, r0)
    sums = no_sums
    for b in range(2):
        sums = fold_block(0, b, sums)
    swap = to_sibling(8, xs.at[1 - c], xr.at[1])
    swap.start()
    r0["D1", 0].finish()
    r0["D2"].start_far()
    vector_grad(0, r0, sums)
    r0["D1", 1].finish()
    r0["D1", 2].finish()
    r0["D2"].start_near()
    r0["D1", 3].finish()
    forward_on(r0, "B2")
    next_ring(r0, "U")
    finish_third(r1, ("O3", "A3", "B3", "D3", "U3"))
    finish_line(1)
    forward_on(r0, "A2", "D2")
    next_ring(r0, "B", "A", "D")
    forward_on(r0, "U3")
    swap.wait()

    @pl.loop(0, 4)
    def _(i):
        rows = pl.ds(pl.multiple_of(i * CH, CH), CH)
        s = xs[c, rows, :].astype(F32) + xr[1, rows, :].astype(F32)
        n, inverse = norm_of(X2[c, rows, :].astype(F32))
        out_gx[rows, :] = through_norm(n, inverse, g_[rows, :], s).astype(BF16)

    last_sums(1)
    finish_third(r0, ("O3", "U3", "B3", "A3", "D3"))
    finish_line(0)
    last_sums(0)


def vmem(*shape, dtype=BF16):
    return pltpu.VMEM(shape, dtype)


def make_call():
    T2 = 2 * TOK
    scratch = [
        vmem(3, 4, 4, ROWS, HALF), vmem(2, 2, CHUNK, HALF), vmem(2, 48, HALF), vmem(2, 8, CHUNK, HALF), vmem(2, 4, 48, HALF),
        vmem(16, D, dtype=F32), vmem(2, 4, 8, HALF, dtype=F32),
        vmem(2, TOK, D), vmem(T2, D), vmem(2, 8, TOK, dtype=jnp.int32), vmem(8, T2, dtype=F32), vmem(8, T2, dtype=F32),
        vmem(2, TOK, TOK, dtype=F32), vmem(T2, D, dtype=F32), vmem(T2, 128, dtype=F32), vmem(TOK, D, dtype=F32),
        vmem(T2, D), vmem(T2, D), vmem(128, T2), vmem(T2, HD), vmem(T2, HD), vmem(2, HALF, T2), vmem(2, 6, 2, TOK, TOK),
        vmem(HALF, T2), vmem(2, T2, HALF), vmem(2, 4, T2, HALF), vmem(2, 4, T2, HALF),
        vmem(T2, D, dtype=F32), vmem(D, T2), vmem(D, T2), vmem(T2, HALF), vmem(HALF, T2),
        vmem(T2, HD, dtype=F32), vmem(T2, HD, dtype=F32), vmem(T2, 128), vmem(16, D, dtype=F32),
        vmem(4, 8, HALF, dtype=F32), vmem(TOK, D, dtype=F32), vmem(3, TOK, D), vmem(4, TOK, D),
        vmem(2, 6, 2, 48, HALF), vmem(2, 6, 2, 32, HALF), vmem(2, 6, 2, 48, HALF), vmem(2, 6, 2, 192, HALF),
        vmem(2, 4, 6, 2, 48, HALF), vmem(2, 6, 2, 48, HALF),
        vmem(2, 3, 48, HALF), vmem(2, 3, 32, HALF), vmem(2, 3, 48, HALF), vmem(2, 6, 96, HALF), vmem(2, 3, 48, HALF),
        vmem(2, 8, 32, HALF), vmem(2, 8, 32, HALF), vmem(2, 4, 48, HALF),
        *[vmem(*v.shape) for v in (CONSTS[i] for i in range(9))],
        pltpu.SemaphoreType.DMA((9,)), pltpu.SemaphoreType.DMA((9,)), pltpu.SemaphoreType.DMA((9,)),
        pltpu.SemaphoreType.DMA((4, 4)), pltpu.SemaphoreType.DMA((2, 14, 5)), pltpu.SemaphoreType.DMA((2, 14, 4)),
    ]
    whole = pl.BlockSpec(memory_space=pltpu.VMEM)
    return pl.pallas_call(
        kernel,
        out_shape=(
            jax.ShapeDtypeStruct((TOK, D), BF16),
            jax.ShapeDtypeStruct((TOK, D), BF16),
            jax.ShapeDtypeStruct((2, 96, D), F32),
            jax.ShapeDtypeStruct((2, 48, HALF), F32),
        ),
        in_specs=[whole] * 14 + [pl.BlockSpec(memory_space=pl.ANY)] * 9,
        out_specs=(whole,) * 4,
        scratch_shapes=scratch,
        compiler_params=pltpu.CompilerParams(
            collective_id=0, has_side_effects=True, vmem_limit_bytes=64 * 2**20 - 65536
        ),
        name="two_layers",
    )


def pack_kernel(
    y, gx, v, u,
    o_y, o_gx, o_gain, o_nbias, o_q, o_qb, o_kv, o_o, o_ob, o_up, o_ub, o_down, o_db,
):
    o_y[...] = y[...]
    o_gx[...] = gx[...]
    for l in range(2):
        o_gain[l] = v[l, 24:26, 0:6]
        o_nbias[l] = v[l, 26:28, 0:6]
        o_qb[l:l + 1, :] = v[l, 28:29, 0:6]
        o_ob[l:l + 1, :] = v[l, 29:30, 0:6]
        o_db[l:l + 1, :] = v[l, 29:30, 0:6]
        o_ub[l:l + 1, :] = v[l, 30:31, 8:32]
        for h in range(2):
            o_up[l, :, h * HALF:(h + 1) * HALF] = u[l, 24 * h:24 * h + 24, :]
        for i in range(6):
            o_q[i, l:l + 1, :] = v[l, i:i + 1, :]
            o_o[i, l:l + 1, :] = v[l, 6 + i:7 + i, :]
            for g in range(4):
                at = 32 + 16 * g + 4 + i
                o_down[i, l:l + 1, g * D:(g + 1) * D] = v[l, at:at + 1, :]
    o_kv[...] = v[0, 18:24, 0:128]


def pack(y, gx, v, u):
    whole = pl.BlockSpec(memory_space=pltpu.VMEM)
    shapes = [(2, 2, 6), (2, 2, 6), (6, 2, D), (2, 6), (6, 128), (6, 2, D), (2, 6), (2, 24, D), (2, 24), (6, 2, FF), (2, 6)]
    return pl.pallas_call(
        pack_kernel,
        out_shape=tuple(
            [jax.ShapeDtypeStruct((TOK, D), BF16)] * 2 + [jax.ShapeDtypeStruct(shape, F32) for shape in shapes]),
        in_specs=[whole] * 4,
        out_specs=(whole,) * 13,
        name="results",
    )(y, gx, v, u)


def on_device(
    layer_input, segments, norm_gain, norm_bias, query_weight, query_bias, keyval_weight, output_weight,
    output_bias, upward_weight, upward_bias, downward_weight, downward_bias, cotangent,
):
    consts = [jnp.asarray(v, BF16) for v in CONSTS]
    y, gx, gain, nbias, q, qb, kv, o, ob, up, ub, down, db = pack(*make_call()(
        layer_input, segments, cotangent, norm_gain, norm_bias, query_weight.transpose(1, 0, 2), query_bias,
        keyval_weight, output_weight.transpose(2, 0, 1), output_bias, upward_weight.transpose(0, 2, 1), upward_bias,
        downward_weight.transpose(2, 0, 1), downward_bias, *consts))
    return (
        y, gx, gain, nbias, q.transpose(1, 0, 2), qb, kv, o.transpose(1, 2, 0), ob, up.transpose(0, 2, 1), ub,
        down.transpose(1, 2, 0), db,
    )


def solution(mesh):
    in_specs = (
        P(("dp", "fsdp"), None),
        P(("dp", "fsdp"), None),
        P(None, None, ("dp", "fsdp")),
        P(None, None, ("dp", "fsdp")),
        P(None, ("dp", "fsdp"), None),
        P(None, ("dp", "fsdp")),
        P(("dp", "fsdp"), None),
        P(None, None, ("dp", "fsdp")),
        P(None, ("dp", "fsdp")),
        P(None, None, ("dp", "fsdp")),
        P(None, ("dp", "fsdp")),
        P(None, None, ("dp", "fsdp")),
        P(None, ("dp", "fsdp")),
        P(("dp", "fsdp"), None),
    )
    out_specs = (
        P(("dp", "fsdp"), None),
        P(("dp", "fsdp"), None),
        P(None, None, ("dp", "fsdp")),
        P(None, None, ("dp", "fsdp")),
        P(None, ("dp", "fsdp"), None),
        P(None, ("dp", "fsdp")),
        P(("dp", "fsdp"), None),
        P(None, None, ("dp", "fsdp")),
        P(None, ("dp", "fsdp")),
        P(None, None, ("dp", "fsdp")),
        P(None, ("dp", "fsdp")),
        P(None, None, ("dp", "fsdp")),
        P(None, ("dp", "fsdp")),
    )
    return jax.shard_map(on_device, mesh=mesh, in_specs=in_specs, out_specs=out_specs, check_vma=False)
```
